32 devices in a mesh: dp: 16 (over z, y, core), mlp: 2 (over x).
Axes of the slice: x: 2, y: 2, z: 4, core: 2. Of those that a mesh axis runs over, the one named last changes fastest.
Arguments:
- block_input: bfloat16 [32768, 512], P(('dp', 'mlp')), may hold values from -6 to 6
- doc_lengths: int32 [32, 4], P(('dp', 'mlp')), may hold values from 0 to 1024, as said below
- norm_gain: bfloat16 [2, 512], replicated, may hold values from 0.25 to 1.75
- norm_bias: bfloat16 [2, 512], replicated, may hold values from -1.75 to 1.75
- qkv_weight: bfloat16 [2, 512, 1536], replicated, may hold values from -0.25 to 0.25
- qkv_bias: bfloat16 [2, 1536], replicated, may hold values from -3 to 3
- out_weight: bfloat16 [2, 512, 512], replicated, may hold values from -1 to 1
- out_bias: bfloat16 [2, 512], replicated, may hold values from -1.75 to 1.75
- up_weight: bfloat16 [2, 512, 2048], P(None, None, 'mlp'), may hold values from -0.25 to 0.25
- up_bias: bfloat16 [2, 2048], P(None, 'mlp'), may hold values from -3 to 3
- down_weight: bfloat16 [2, 2048, 512], P(None, 'mlp'), may hold values from -0.125 to 0.125
- down_bias: bfloat16 [2, 512], replicated, may hold values from -1.75 to 1.75
- out_grad: bfloat16 [32768, 512], P(('dp', 'mlp')), may hold values from -6 to 6
Outputs:
- block_output: bfloat16 [32768, 512], P(('dp', 'mlp'))
- input_grad: float32 [32768, 512], P(('dp', 'mlp'))
- norm_gain_grad: float32 [2, 512], replicated
- norm_bias_grad: float32 [2, 512], replicated
- qkv_weight_grad: float32 [2, 512, 1536], replicated
- qkv_bias_grad: float32 [2, 1536], replicated
- out_weight_grad: float32 [2, 512, 512], replicated
- out_bias_grad: float32 [2, 512], replicated
- up_weight_grad: float32 [2, 512, 2048], P(None, None, 'mlp')
- up_bias_grad: float32 [2, 2048], P(None, 'mlp')
- down_weight_grad: float32 [2, 2048, 512], P(None, 'mlp')
- down_bias_grad: float32 [2, 512], replicated
The draws below stay inside these ranges and needn't reach their ends.
Inputs may be any that keep to these rules, and one draw needn't show every extreme that they name: `doc_lengths`: each device's 4 lengths add up to 1024; a length of 0 is an empty slot; on one device a single document fills all 1024 rows.
All inputs are finite; a program needn't handle non-finite values.
Results may differ from the reference program's by a relative error of at most 0.012.
Values may be sent and summed in bfloat16 or wider, within the bound.
A program may use at most 256 MiB of HBM per device.

```python
import jax
import jax.numpy as jnp
from jax import lax

D = 512
HEADS = 8
FF = 2048
ROT = 16
LAYERS = 2
DOCS = 4
TOK_DEV = 1024
SHARDS = 32
TOKENS = 32768


def draw_doc_lengths(key, part):
    key = jax.random.fold_in(key, 11)
    key_cuts, key_device, key_slot = jax.random.split(key, 3)
    cuts = jax.random.randint(key_cuts, (SHARDS, DOCS - 1), 0, TOK_DEV + 1)
    cuts = jnp.sort(cuts, axis=1)
    edges = jnp.concatenate([jnp.zeros((SHARDS, 1), jnp.int32), cuts.astype(jnp.int32), jnp.full((SHARDS, 1), TOK_DEV, jnp.int32)], axis=1)
    lengths = edges[:, 1:] - edges[:, :-1]
    whole_device = jax.random.randint(key_device, (), 0, SHARDS)
    whole_slot = jax.random.randint(key_slot, (), 0, DOCS)
    single = jnp.where(jnp.arange(DOCS) == whole_slot, TOK_DEV, 0).astype(jnp.int32)
    lengths = jnp.where(jnp.arange(SHARDS)[:, None] == whole_device, single[None, :], lengths)
    return lengths.astype(jnp.int32)


def block_levels(stream_key, extent, shards, smallest, top_value):
    def one(axis_at, blocks):
        heights = jax.random.uniform(jax.random.fold_in(jax.random.fold_in(stream_key, 6), axis_at), (blocks,), jnp.float32, smallest / len(shards), top_value / len(shards))
        return jnp.repeat(jnp.exp(heights), extent[axis_at] // blocks).reshape((-1,) + (1,) * (len(extent) - axis_at - 1))

    level = one(*shards[0])
    for cut in shards[1:]:
        level = level * one(*cut)
    return level


def noise(own_key, shape, scale, bound, pieces=(), kind=jnp.bfloat16):
    level = block_levels(own_key, shape, pieces, -0.22, 0.18) if pieces else 1.0
    entries = jax.random.normal(own_key, shape, jnp.float32) * scale * level
    return jnp.minimum(jnp.maximum(entries, -bound), bound).astype(kind)


def setup_inputs(seed: int = 0) -> dict:
    keys = jax.random.split(jax.random.key(seed), 14)
    block_input = noise(keys[0], (TOKENS, D), 1.0, 6.0, ((0, 32),))
    doc_lengths = draw_doc_lengths(jax.random.fold_in(keys[13], 71), 0)
    norm_gain = jnp.clip(1.0 + 0.15 * jax.random.normal(keys[2], (LAYERS, D), jnp.float32), 0.25, 1.75).astype(jnp.bfloat16)
    norm_bias = noise(keys[3], (LAYERS, D), 0.3, 1.75)
    qkv_weight = noise(keys[4], (LAYERS, D, 3 * D), D ** -0.5, 0.25)
    qkv_bias = noise(keys[5], (LAYERS, 3 * D), 0.5, 3.0)
    out_weight = noise(keys[6], (LAYERS, D, D), (D // 16) ** -0.5, 1.0)
    out_bias = noise(keys[7], (LAYERS, D), 0.3, 1.75)
    up_weight = noise(keys[8], (LAYERS, D, FF), D ** -0.5, 0.25, ((2, 2),))
    up_bias = noise(keys[9], (LAYERS, FF), 0.5, 3.0, ((1, 2),))
    down_weight = noise(keys[10], (LAYERS, FF, D), FF ** -0.5, 0.125, ((1, 2),))
    down_bias = noise(keys[11], (LAYERS, D), 0.3, 1.75)
    out_grad = noise(keys[12], (TOKENS, D), 1.0, 6.0, ((0, 32),))
    return {"block_input": block_input, "doc_lengths": doc_lengths, "norm_gain": norm_gain, "norm_bias": norm_bias, "qkv_weight": qkv_weight, "qkv_bias": qkv_bias, "out_weight": out_weight, "out_bias": out_bias, "up_weight": up_weight, "up_bias": up_bias, "down_weight": down_weight, "down_bias": down_bias, "out_grad": out_grad}


norm_eps = 1e-05
rotary_base = 10000.0

@jax.custom_vjp
def low(v):
    return lax.optimization_barrier(v.astype(jnp.bfloat16)).astype(jnp.float32)

@jax.custom_vjp
def low_back(v):
    return v

def low_keep(v):
    return (low(v), None)

def low_pass(kept, grad):
    return (grad,)

def back_keep(v):
    return (v, None)

def back_low(kept, grad):
    return (low(grad),)
low.defvjp(low_keep, low_pass)
low_back.defvjp(back_keep, back_low)

def matmul(left, right):
    return jnp.dot(left, right, precision=lax.Precision.HIGHEST)

def layer_norm(values, gain_row, bias_row):
    centre = lax.optimization_barrier(jnp.mean(values, axis=-1, keepdims=True))
    centred = values - centre
    spread = lax.optimization_barrier(jnp.mean(centred * centred, axis=-1, keepdims=True))
    return centred * lax.rsqrt(spread + norm_eps) * gain_row + bias_row

def doc_layout(lengths, row_count):
    lengths = lengths.astype(jnp.int32)
    ends = jnp.cumsum(lengths).astype(jnp.int32)
    starts = (ends - lengths).astype(jnp.int32)
    row_index = jnp.arange(row_count, dtype=jnp.int32)
    doc_owner = lax.optimization_barrier(jnp.sum((row_index[:, None] >= ends[None, :]).astype(jnp.int32), axis=1)).astype(jnp.int32)
    matched = doc_owner[:, None] == jnp.arange(lengths.shape[0], dtype=jnp.int32)[None, :]
    doc_start = lax.optimization_barrier(jnp.sum(jnp.where(matched, starts[None, :], 0), axis=1)).astype(jnp.int32)
    allowed = (doc_owner[:, None] == doc_owner[None, :]) & (row_index[None, :] <= row_index[:, None])
    return (allowed, (row_index - doc_start).astype(jnp.int32))

def rotary_tables(position, rot_dims):
    half_dims = rot_dims // 2
    freqs = rotary_base ** (-(2.0 * jnp.arange(half_dims, dtype=jnp.float32) / rot_dims))
    angles = position.astype(jnp.float32)[:, None] * freqs[None, :]
    return (jnp.cos(angles), jnp.sin(angles))

def rotate(heads_in, cosines, sine_table, rot_dims):
    half_dims = rot_dims // 2
    first_half = heads_in[..., :half_dims]
    second_half = heads_in[..., half_dims:rot_dims]
    remainder = heads_in[..., rot_dims:]
    cos_rows = cosines[:, None, :]
    sin_rows = sine_table[:, None, :]
    return jnp.concatenate([first_half * cos_rows - second_half * sin_rows, second_half * cos_rows + first_half * sin_rows, remainder], axis=-1)

def attend(packed, lengths):
    row_count = packed.shape[0]
    head_size = D // HEADS
    head_shape = (row_count, HEADS, head_size)
    allowed, position = doc_layout(lengths, row_count)
    cosines, sine_table = rotary_tables(position, ROT)
    queries = low(rotate(packed[:, :D].reshape(head_shape), cosines, sine_table, ROT))
    key_rows = low(rotate(packed[:, D:2 * D].reshape(head_shape), cosines, sine_table, ROT))
    value_rows = low(packed[:, 2 * D:].reshape(head_shape))
    scores = low_back(jnp.einsum('qhd,khd->hqk', queries, key_rows, precision=lax.Precision.HIGHEST) * head_size ** (-0.5))
    scores = jnp.where(allowed[None, :, :], scores, -1e+30)
    row_top = lax.optimization_barrier(jnp.max(scores, axis=-1, keepdims=True))
    expo = jnp.exp(scores - row_top)
    attend_weights = low(expo / lax.optimization_barrier(jnp.sum(expo, axis=-1, keepdims=True)))
    mixed = jnp.einsum('hqk,khd->qhd', attend_weights, value_rows, precision=lax.Precision.HIGHEST).reshape(row_count, D)
    return low(low_back(mixed))

def attend_pair(pair):
    return attend(pair[0], pair[1])

def forward(inputs, lengths, gains, biases, qkv_weight, qkv_bias, out_weight, out_bias, up_weight, up_bias, down_weight, down_bias):
    stream = inputs
    for layer_index in range(LAYERS):
        hidden = low(layer_norm(stream, gains[layer_index], biases[layer_index]))
        packed = low_back(matmul(hidden, qkv_weight[layer_index]) + qkv_bias[layer_index])
        blocks = packed.reshape(SHARDS, TOK_DEV, 3 * D)
        mixed = lax.map(jax.checkpoint(attend_pair), (blocks, lengths)).reshape(TOKENS, D)
        attn_out = matmul(mixed, out_weight[layer_index]) + out_bias[layer_index]
        pre_act = low_back(matmul(hidden, up_weight[layer_index]) + up_bias[layer_index])
        activ = low(jax.nn.gelu(pre_act, approximate=False))
        mlp_out = matmul(activ, down_weight[layer_index]) + down_bias[layer_index]
        stream = stream + low_back(attn_out + mlp_out)
    return stream

def reference(block_input, doc_lengths, norm_gain, norm_bias, qkv_weight, qkv_bias, out_weight, out_bias, up_weight, up_bias, down_weight, down_bias, out_grad):
    params = tuple((item.astype(jnp.float32) for item in (norm_gain, norm_bias, qkv_weight, qkv_bias, out_weight, out_bias, up_weight, up_bias, down_weight, down_bias)))

    def apply_all(inputs, *weights):
        return forward(inputs, doc_lengths, *weights)
    result, pullback = jax.vjp(apply_all, block_input.astype(jnp.float32), *params)
    grads = pullback(out_grad.astype(jnp.float32))
    return (result.astype(jnp.bfloat16), grads[0], grads[1], grads[2], grads[3], grads[4], grads[5], grads[6], grads[7], grads[8], grads[9], grads[10])
```

```python
import functools
import math

import jax
import jax.numpy as jnp
from jax import lax
from jax.experimental import pallas as pl
from jax.experimental.pallas import tpu as pltpu
from jax.sharding import PartitionSpec as P

HEADS = 8
ROT = 16
HALF = ROT // 2
BLK = 256
norm_eps = 1e-05
rotary_base = 10000.0
bf16 = jnp.bfloat16
f32 = jnp.float32
NEG = -1e30
LOG2E = math.log2(math.e)
LN2 = math.log(2.0)


def dot_nn(a, b):
    return lax.dot_general(a, b, (((1,), (0,)), ((), ())), preferred_element_type=f32)


def dot_nt(a, b):
    return lax.dot_general(a, b, (((1,), (1,)), ((), ())), preferred_element_type=f32)


def dot_tn(a, b):
    return lax.dot_general(a, b, (((0,), (0,)), ((), ())), preferred_element_type=f32)


def row_of(ref, layer):
    return ref[...].astype(f32)[layer : layer + 1, :]


def doc_tables(lens, rows):
    lane = lax.broadcasted_iota(jnp.int32, (HALF, rows), 1)
    sub = lax.broadcasted_iota(jnp.int32, (HALF, rows), 0)
    start = jnp.int32(0)
    hot = jnp.zeros((HALF, rows), f32)
    first = jnp.zeros((HALF, rows), jnp.int32)
    for slot in range(lens.shape[1]):
        end = start + lens[0, slot]
        inside = (lane >= start) & (lane < end)
        hot = jnp.where(inside & (sub == slot), 1.0, hot)
        first = jnp.where(inside, start, first)
        start = end
    return hot, lane - first


def rotary_tables(position):
    index = lax.broadcasted_iota(jnp.int32, position.shape, 0).astype(f32)
    freqs = jnp.exp(index * (-2.0 / ROT * math.log(rotary_base)))
    angles = position.astype(f32) * freqs
    return jnp.cos(angles), jnp.sin(angles)


def rotate(values, cosines, sines):
    size = 64
    heads = values.shape[0] // size
    split = values.reshape(heads, size, values.shape[1])
    first, second, rest = split[:, :HALF], split[:, HALF:ROT], split[:, ROT:]
    turned = jnp.concatenate(
        [first * cosines - second * sines, second * cosines + first * sines, rest], axis=1
    )
    return turned.reshape(values.shape)


def mask_rows(hot):
    sub = lax.broadcasted_iota(jnp.int32, hot.shape, 0)
    rows = jnp.where(sub < 4, jnp.where(hot > 0.0, 0.0, NEG), jnp.where(sub < 7, 1.0, 0.0))
    return rows


def causal_bias():
    row = lax.broadcasted_iota(jnp.int32, (BLK, BLK), 0)
    col = lax.broadcasted_iota(jnp.int32, (BLK, BLK), 1)
    return jnp.where(row <= col, 0.0, NEG)


def norm_stats(values):
    centre = jnp.mean(values, axis=-1, keepdims=True)
    centred = values - centre
    spread = jnp.mean(centred * centred, axis=-1, keepdims=True)
    return centred, lax.rsqrt(spread + norm_eps)


def split3(value):
    a = value.astype(bf16).astype(f32)
    rest = value - a
    b = rest.astype(bf16).astype(f32)
    return jnp.concatenate([a, b, rest - b], axis=0)


def attention_forward(qkv, mix, lse, hot_s, mask_s, tri, krow, scores, probs, group):
    tokens = qkv.shape[1]
    width = qkv.shape[0] // 3
    blocks = tokens // BLK

    def heads(step, carry):
        tops = [{} for _ in range(group)]
        sums = [{} for _ in range(group)]
        rows = [pl.multiple_of((step * group + j) * 64, 64) for j in range(group)]
        for j in range(group):
            keyed = jnp.concatenate(
                [
                    qkv[pl.ds(width + rows[j], 64), :],
                    mask_s[...],
                    jnp.zeros((48, tokens), bf16),
                ],
                axis=0,
            )
            krow[j] = keyed.T
        for stage in range(group + 2):
            for i in range(blocks):
                n = (i + 1) * BLK
                at = slice(i * BLK, n)
                if stage < group:
                    j = stage
                    query = jnp.concatenate(
                        [qkv[pl.ds(rows[j], 64), at], hot_s[:, at], jnp.zeros((48, BLK), bf16)],
                        axis=0,
                    )
                    raw = dot_nn(krow[j, 0:n, :], query)
                    diagonal = raw[i * BLK :] + tri[...]
                    top = jnp.max(diagonal, axis=0, keepdims=True)
                    if i:
                        top = jnp.maximum(top, jnp.max(raw[: i * BLK], axis=0, keepdims=True))
                        scores[j % 2, i, 0 : i * BLK, :] = raw[: i * BLK]
                    scores[j % 2, i, i * BLK : n, :] = diagonal
                    tops[j][i] = top
                if 0 <= stage - 1 < group:
                    j = stage - 1
                    weights = jnp.exp2(scores[j % 2, i, 0:n, :] - tops[j][i])
                    sums[j][i] = jnp.sum(weights, axis=0, keepdims=True)
                    probs[j % 2, i, 0:n, :] = weights.astype(bf16)
                if 0 <= stage - 2 < group:
                    j = stage - 2
                    out = dot_nn(qkv[pl.ds(2 * width + rows[j], 64), 0:n], probs[j % 2, i, 0:n, :])
                    mix[pl.ds(rows[j], 64), at] = (out / sums[j][i]).astype(bf16)
                    lse[pl.ds(step * group + j, 1), at] = tops[j][i] + jnp.log2(sums[j][i])
        return carry

    lax.fori_loop(0, HEADS // group, heads, 0)


def forward_kernel(
    lens,
    block_input,
    gain,
    bias,
    qkv_bias,
    out_bias,
    up_bias,
    down_bias,
    qkv_w_h,
    out_w_h,
    up_w_h,
    down_w_h,
    block_output,
    stream_h,
    hid_h,
    qkv_h,
    mix_h,
    lse_h,
    act_h,
    slope_h,
    stream,
    hidden,
    hid,
    qkv,
    mix,
    lse,
    act,
    slope,
    qkv_w,
    out_w,
    up_w,
    down_w,
    qkv_b,
    pre,
    hot_s,
    mask_s,
    cos_s,
    sin_s,
    tri,
    krow,
    scores,
    probs,
    in_sem,
    out_sem,
):
    tokens, width = block_input.shape
    layers = gain.shape[0]
    hidden_units = up_w.shape[2]
    blocks = tokens // BLK
    loads = [
        [
            pltpu.make_async_copy(src.at[layer], dst.at[layer], in_sem.at[layer, k])
            for k, (src, dst) in enumerate(
                ((qkv_w_h, qkv_w), (out_w_h, out_w), (up_w_h, up_w), (down_w_h, down_w))
            )
        ]
        for layer in range(layers)
    ]
    for layer in range(layers):
        for copy in loads[layer]:
            copy.start()
    hot, position = doc_tables(lens, tokens)
    zeros8 = jnp.zeros_like(hot)
    hot_s[...] = jnp.concatenate([hot, zeros8], axis=0).astype(bf16)
    mask_s[...] = jnp.concatenate([mask_rows(hot), zeros8], axis=0).astype(bf16)
    cos_s[...], sin_s[...] = rotary_tables(position)
    tri[...] = causal_bias()
    stream[...] = block_input[...].astype(f32)
    stores = []
    for layer in range(layers):
        gain_row, bias_row = row_of(gain, layer), row_of(bias, layer)
        qkv_b[...] = jnp.broadcast_to(row_of(qkv_bias, layer), (128, 3 * width)).T

        for copy in stores:
            copy.wait()
        stores = []

        def norm_block(i, carry):
            rows = pl.ds(pl.multiple_of(i * BLK, BLK), BLK)
            centred, scale = norm_stats(stream[rows, :])
            low = (centred * scale * gain_row + bias_row).astype(bf16)
            hidden[rows, :] = low
            hid[:, rows] = low.T
            return carry

        lax.fori_loop(0, blocks, norm_block, 0)
        loads[layer][0].wait()
        for part in range(3):
            cols = slice(part * width, (part + 1) * width)
            for i in range(blocks):
                at = slice(i * BLK, (i + 1) * BLK)
                value = dot_tn(qkv_w[layer, :, cols], hid[:, at])
                column = qkv_b[cols, :]
                value = value + jnp.concatenate([column] * (BLK // 128), axis=1)
                if part < 2:
                    value = rotate(value, cos_s[:, at], sin_s[:, at])
                if part == 0:
                    value = value * (64**-0.5 * LOG2E)
                qkv[cols, at] = value.astype(bf16)
        attention_forward(qkv, mix, lse, hot_s, mask_s, tri, krow, scores, probs, 4)

        def save(src, dst, k):
            copy = pltpu.make_async_copy(src, dst.at[layer], out_sem.at[k])
            copy.start()
            stores.append(copy)

        save(hid, hid_h, 0)
        save(qkv, qkv_h, 1)
        save(mix, mix_h, 2)
        save(lse, lse_h, 3)
        for k in range(1, 4):
            loads[layer][k].wait()
        shift = row_of(out_bias, layer) + row_of(down_bias, layer)
        up_row = row_of(up_bias, layer)
        chunk = 512

        def mlp_block(i, carry):
            rows = pl.ds(pl.multiple_of(i * BLK, BLK), BLK)
            for c in range(hidden_units // chunk):
                cs = slice(c * chunk, (c + 1) * chunk)
                pre[:, cs] = dot_nn(hidden[rows, :], up_w[layer, :, cs]) + up_row[:, cs]
            for c in range(hidden_units // chunk):
                cs = slice(c * chunk, (c + 1) * chunk)
                u = pre[:, cs]
                cdf = 0.5 + 0.5 * lax.erf(u * (2.0**-0.5))
                pdf = jnp.exp2(u * u * (-0.5 * LOG2E)) * ((2.0 * math.pi) ** -0.5)
                act[rows, cs] = (u * cdf).astype(bf16)
                slope[rows, cs] = (cdf + u * pdf).astype(bf16)
            total = dot_tn(mix[:, rows], out_w[layer]) + dot_nn(act[rows, :], down_w[layer])
            stream[rows, :] = stream[rows, :] + (total + shift)
            return carry

        lax.fori_loop(0, blocks, mlp_block, 0)
        save(act, act_h, 4)
        save(slope, slope_h, 5)
        if layer + 1 < layers:
            copy = pltpu.make_async_copy(stream, stream_h, out_sem.at[6])
            copy.start()
            stores.append(copy)
    block_output[...] = stream[...].astype(bf16)
    for copy in stores:
        copy.wait()


def attention_backward(qkv, mix, grad_mix, lse, hot_s, mask_s, tri, cos_s, sin_s, work, group):
    krow, vrow, qext, gext, probs, dscore = work
    tokens = qkv.shape[1]
    width = qkv.shape[0] // 3
    blocks = tokens // BLK
    ones = jnp.where(lax.broadcasted_iota(jnp.int32, (64, tokens), 0) < 3, 1.0, 0.0).astype(bf16)

    def heads(step, carry):
        rows = [pl.multiple_of((step * group + j) * 64, 64) for j in range(group)]
        for j in range(group):
            r = rows[j]
            keyed = jnp.concatenate(
                [qkv[pl.ds(width + r, 64), :], mask_s[...], jnp.zeros((48, tokens), bf16)], axis=0
            )
            krow[j] = keyed.T
            vrow[j] = jnp.concatenate([qkv[pl.ds(2 * width + r, 64), :], ones], axis=0).T
            grad = grad_mix[pl.ds(r, 64), :].astype(f32)
            total = jnp.sum(grad * mix[pl.ds(r, 64), :].astype(f32), axis=0, keepdims=True)
            qext[j] = jnp.concatenate(
                [
                    qkv[pl.ds(r, 64), :].astype(f32),
                    hot_s[0:4, :].astype(f32),
                    split3(-lse[pl.ds(step * group + j, 1), :]),
                    jnp.zeros((57, tokens), f32),
                ],
                axis=0,
            ).astype(bf16)
            gext[j] = jnp.concatenate(
                [grad, split3(-total), jnp.zeros((61, tokens), f32)], axis=0
            ).astype(bf16)
        for j in range(group):
            r = rows[j]
            for i in range(blocks):
                n = (i + 1) * BLK
                at = slice(i * BLK, n)
                raw = dot_nn(krow[j, 0:n, :], qext[j, :, at])
                if i:
                    raw = jnp.concatenate([raw[: i * BLK], raw[i * BLK :] + tri[...]], axis=0)
                else:
                    raw = raw + tri[...]
                weights = jnp.exp2(raw)
                slopes = dot_nn(vrow[j, 0:n, :], gext[j, :, at])
                dscore[j, 0:n, at] = (weights * slopes).astype(bf16)
                probs[j, 0:n, at] = weights.astype(bf16)
            dq, dk, dv = [], [], []
            for i in range(blocks):
                n = (i + 1) * BLK
                at = slice(i * BLK, n)
                dq.append(dot_nn(qkv[pl.ds(width + r, 64), 0:n], dscore[j, 0:n, at]))
                dk.append(dot_nt(qkv[pl.ds(r, 64), i * BLK :], dscore[j, at, i * BLK :]))
                dv.append(dot_nt(grad_mix[pl.ds(r, 64), i * BLK :], probs[j, at, i * BLK :]))
            dq = jnp.concatenate(dq, axis=1) * 64**-0.5
            dk = jnp.concatenate(dk, axis=1) * LN2
            qkv[pl.ds(r, 64), :] = rotate(dq, cos_s[...], -sin_s[...]).astype(bf16)
            qkv[pl.ds(width + r, 64), :] = rotate(dk, cos_s[...], -sin_s[...]).astype(bf16)
            qkv[pl.ds(2 * width + r, 64), :] = jnp.concatenate(dv, axis=1).astype(bf16)
        return carry

    lax.fori_loop(0, HEADS // group, heads, 0)


def backward_kernel(
    lens,
    block_input,
    out_grad,
    gain,
    bias,
    qkv_w_h,
    out_w_h,
    up_w_h,
    down_w_h,
    stream_h,
    hid_h,
    qkv_h,
    mix_h,
    lse_h,
    act_h,
    slope_h,
    input_grad,
    mlp_grad,
    att_grad,
    vec_grad,
    stream,
    grad_low,
    grad_mix,
    grad_hid,
    hid,
    qkv,
    mix,
    lse,
    act,
    slope,
    qkv_w,
    out_w,
    up_w,
    down_w,
    hot_s,
    mask_s,
    cos_s,
    sin_s,
    tri,
    krow,
    vrow,
    qext,
    gext,
    probs,
    dscore,
    in_sem,
):
    tokens, width = block_input.shape
    layers = gain.shape[0]
    hidden_units = up_w.shape[1]
    blocks = tokens // BLK
    grad = input_grad

    def load(src, dst, layer, k):
        copy = pltpu.make_async_copy(src, dst, in_sem.at[layer, k])
        copy.start()
        return copy

    def load_mlp(layer):
        return [
            load(slope_h.at[layer], slope, layer, 0),
            load(down_w_h.at[layer], down_w, layer, 1),
            load(act_h.at[layer], act, layer, 2),
            load(up_w_h.at[layer], up_w, layer, 3),
            load(hid_h.at[layer], hid.at[layer, 0:width, :], layer, 4),
        ]

    def load_att(layer):
        copies = [
            load(qkv_h.at[layer], qkv, layer, 5),
            load(mix_h.at[layer], mix, layer, 6),
            load(lse_h.at[layer], lse, layer, 7),
        ]
        return copies

    last = layers - 1
    mlp_loads, att_loads = load_mlp(last), load_att(last)
    weight_loads = [
        load(out_w_h, out_w, 0, 8),
        load(qkv_w_h, qkv_w, 0, 9),
        load(stream_h, stream, 0, 10),
    ]
    hot, position = doc_tables(lens, tokens)
    zeros8 = jnp.zeros_like(hot)
    hot_s[...] = jnp.concatenate([hot, zeros8], axis=0).astype(bf16)
    mask_s[...] = jnp.concatenate([mask_rows(hot), zeros8], axis=0).astype(bf16)
    cos_s[...], sin_s[...] = rotary_tables(position)
    tri[...] = causal_bias()
    for layer in range(layers):
        hid[layer, width : width + 16, :] = jnp.ones((16, tokens), bf16)
    grad[...] = out_grad[...].astype(f32)
    grad_low[...] = out_grad[...]
    for layer in reversed(range(layers)):
        mlp_loads[0].wait()
        mlp_loads[1].wait()
        mlp_loads[3].wait()

        def mlp_block(i, carry):
            rows = pl.ds(pl.multiple_of(i * BLK, BLK), BLK)
            for c in range(hidden_units // 512):
                cs = slice(c * 512, (c + 1) * 512)
                da = dot_nt(grad_low[rows, :], down_w[cs, :])
                slope[rows, cs] = (slope[rows, cs].astype(f32) * da).astype(bf16)
            grad_hid[rows, :] = dot_nt(slope[rows, :], up_w[...])
            return carry

        lax.fori_loop(0, blocks, mlp_block, 0)
        mlp_loads[2].wait()
        mlp_loads[4].wait()
        half = hidden_units // 2
        for c in range(hidden_units // 512):
            x, at = divmod(c * 512, half)
            cs = slice(c * 512, (c + 1) * 512)
            mlp_grad[layer, x, half + at : half + at + 512, :] = dot_tn(
                act[:, cs], grad_low[...]
            ).astype(bf16)
            up = dot_nn(hid[layer], slope[:, cs])
            mlp_grad[layer, x, at : at + 512, :] = up[:width].astype(bf16)
            vec_grad[layer, 6 + c : 7 + c, :] = up[width : width + 1]
        if layer:
            mlp_loads = load_mlp(layer - 1)
        if layer == last:
            weight_loads[0].wait()
            weight_loads[1].wait()
            weight_loads[2].wait()
        for copy in att_loads:
            copy.wait()
        att_grad[layer, 3 * width : 4 * width, :] = dot_nn(mix[...], grad_low[...]).astype(bf16)
        vec_grad[layer, 5:6, :] = jnp.sum(grad_low[...].astype(f32), axis=0, keepdims=True)
        grad_mix[...] = dot_nt(out_w[layer], grad_low[...]).astype(bf16)
        attention_backward(
            qkv,
            mix,
            grad_mix,
            lse,
            hot_s,
            mask_s,
            tri,
            cos_s,
            sin_s,
            (krow, vrow, qext, gext, probs, dscore),
            2,
        )
        for part in range(3):
            cols = slice(part * width, (part + 1) * width)
            got = dot_nt(hid[layer], qkv[cols, :])
            att_grad[layer, cols, :] = got[:width].astype(bf16)
            vec_grad[layer, 2 + part : 3 + part, :] = got[width : width + 1]
        gain_row = row_of(gain, layer)
        vec_grad[layer, 0:2, :] = jnp.zeros((2, width), f32)

        def norm_block(i, carry):
            rows = pl.ds(pl.multiple_of(i * BLK, BLK), BLK)
            back = lax.dot_general(
                qkv[:, rows],
                qkv_w[layer],
                (((0,), (1,)), ((), ())),
                preferred_element_type=f32,
            )
            dh = grad_hid[rows, :] + back
            if layer:
                centred, scale = norm_stats(stream[rows, :])
            else:
                centred, scale = norm_stats(block_input[rows, :].astype(f32))
            n = centred * scale
            product = dh * n
            vec_grad[layer, 0:1, :] += jnp.sum(product, axis=0, keepdims=True)
            vec_grad[layer, 1:2, :] += jnp.sum(dh, axis=0, keepdims=True)
            e = dh * gain_row
            mean_e = jnp.mean(e, axis=-1, keepdims=True)
            mean_en = jnp.mean(product * gain_row, axis=-1, keepdims=True)
            total = grad[rows, :] + scale * (e - mean_e - n * mean_en)
            grad[rows, :] = total
            if layer:
                grad_low[rows, :] = total.astype(bf16)
            return carry

        lax.fori_loop(0, blocks, norm_block, 0)
        if layer:
            att_loads = load_att(layer - 1)


VMEM = pl.BlockSpec(memory_space=pltpu.VMEM)
SMEM = pl.BlockSpec(memory_space=pltpu.SMEM)
ANY = pl.BlockSpec(memory_space=pl.ANY)


def run_forward(lens, block_input, gain, bias, qkv_b, out_b, up_b, down_b, qkv_w, out_w, up_w, down_w):
    tokens, width = block_input.shape
    layers = gain.shape[0]
    units = up_w.shape[2]
    shape = jax.ShapeDtypeStruct
    v = pltpu.VMEM
    return pl.pallas_call(
        forward_kernel,
        out_shape=(
            shape((tokens, width), bf16),
            shape((tokens, width), f32),
            shape((layers, width, tokens), bf16),
            shape((layers, 3 * width, tokens), bf16),
            shape((layers, width, tokens), bf16),
            shape((layers, HEADS, tokens), f32),
            shape((layers, tokens, units), bf16),
            shape((layers, tokens, units), bf16),
        ),
        in_specs=[SMEM] + [VMEM] * 7 + [ANY] * 4,
        out_specs=(VMEM,) + (ANY,) * 7,
        scratch_shapes=[
            v((tokens, width), f32),
            v((tokens, width), bf16),
            v((width, tokens), bf16),
            v((3 * width, tokens), bf16),
            v((width, tokens), bf16),
            v((HEADS, tokens), f32),
            v((tokens, units), bf16),
            v((tokens, units), bf16),
            v((layers, width, 3 * width), bf16),
            v((layers, width, width), bf16),
            v((layers, width, units), bf16),
            v((layers, units, width), bf16),
            v((3 * width, 128), f32),
            v((BLK, units), f32),
            v((16, tokens), bf16),
            v((16, tokens), bf16),
            v((HALF, tokens), f32),
            v((HALF, tokens), f32),
            v((BLK, BLK), f32),
            v((4, tokens, 128), bf16),
            v((2, tokens // BLK, tokens, BLK), f32),
            v((2, tokens // BLK, tokens, BLK), bf16),
            pltpu.SemaphoreType.DMA((layers, 4)),
            pltpu.SemaphoreType.DMA((7,)),
        ],
        compiler_params=pltpu.CompilerParams(vmem_limit_bytes=63 * 2**20),
        name="forward",
    )(lens, block_input, gain, bias, qkv_b, out_b, up_b, down_b, qkv_w, out_w, up_w, down_w)


def run_backward(lens, block_input, out_grad, gain, bias, qkv_w, out_w, up_w, down_w, saved):
    tokens, width = block_input.shape
    layers = gain.shape[0]
    units = up_w.shape[2]
    shape = jax.ShapeDtypeStruct
    v = pltpu.VMEM
    return pl.pallas_call(
        backward_kernel,
        out_shape=(
            shape((tokens, width), f32),
            shape((layers, 2, units, width), bf16),
            shape((layers, 4 * width, width), bf16),
            shape((layers, 16, width), f32),
        ),
        in_specs=[SMEM] + [VMEM] * 4 + [ANY] * 11,
        out_specs=(VMEM,) * 4,
        scratch_shapes=[
            v((tokens, width), f32),
            v((tokens, width), bf16),
            v((width, tokens), bf16),
            v((tokens, width), f32),
            v((layers, width + 16, tokens), bf16),
            v((3 * width, tokens), bf16),
            v((width, tokens), bf16),
            v((HEADS, tokens), f32),
            v((tokens, units), bf16),
            v((tokens, units), bf16),
            v((layers, width, 3 * width), bf16),
            v((layers, width, width), bf16),
            v((width, units), bf16),
            v((units, width), bf16),
            v((16, tokens), bf16),
            v((16, tokens), bf16),
            v((HALF, tokens), f32),
            v((HALF, tokens), f32),
            v((BLK, BLK), f32),
            v((2, tokens, 128), bf16),
            v((2, tokens, 128), bf16),
            v((2, 128, tokens), bf16),
            v((2, 128, tokens), bf16),
            v((2, tokens, tokens), bf16),
            v((2, tokens, tokens), bf16),
            pltpu.SemaphoreType.DMA((layers, 11)),
        ],
        compiler_params=pltpu.CompilerParams(vmem_limit_bytes=63 * 2**20),
        name="backward",
    )(lens, block_input, out_grad, gain, bias, qkv_w, out_w, up_w, down_w, *saved)


def body(
    block_input,
    doc_lengths,
    norm_gain,
    norm_bias,
    qkv_weight,
    qkv_bias,
    out_weight,
    out_bias,
    up_weight,
    up_bias,
    down_weight,
    down_bias,
    out_grad,
):
    layers, width = norm_gain.shape
    up_all = lax.all_gather(up_weight, "mlp", axis=2, tiled=True)
    down_all = lax.all_gather(down_weight, "mlp", axis=1, tiled=True)
    up_bias_all = lax.all_gather(up_bias, "mlp", axis=1, tiled=True)
    block_output, *saved = run_forward(
        doc_lengths,
        block_input,
        norm_gain,
        norm_bias,
        qkv_bias,
        out_bias,
        up_bias_all,
        down_bias,
        qkv_weight,
        out_weight,
        up_all,
        down_all,
    )
    input_grad, mlp_grad, att_grad, vec_grad = run_backward(
        doc_lengths,
        block_input,
        out_grad,
        norm_gain,
        norm_bias,
        qkv_weight,
        out_weight,
        up_all,
        down_all,
        saved,
    )
    mlp_grad = lax.psum_scatter(mlp_grad, "mlp", scatter_dimension=1, tiled=False)
    mlp_grad = lax.psum(mlp_grad, "dp").astype(f32)
    att_grad = lax.psum(att_grad, ("dp", "mlp")).astype(f32)
    vec_grad = lax.psum(vec_grad, ("dp", "mlp"))
    return finish(block_output, input_grad, mlp_grad, att_grad, vec_grad)


def finish(block_output, input_grad, mlp_grad, att_grad, vec_grad):
    layers, units, width = mlp_grad.shape
    half = units // 2
    up_grad = jnp.concatenate(
        [mlp_grad[:, at : at + width] for at in range(0, half, width)], axis=2
    )
    down_grad = mlp_grad[:, half:]
    qkv_grad = jnp.concatenate(
        [att_grad[:, at : at + width] for at in range(0, 3 * width, width)], axis=2
    )
    out_w_grad = att_grad[:, 3 * width :]
    out_b_grad = vec_grad[:, 5]
    up_b_all = vec_grad[:, 6 : 6 + units // width].reshape(layers, -1)
    up_b_grad = lax.dynamic_slice_in_dim(up_b_all, lax.axis_index("mlp") * half, half, 1)
    return (
        block_output,
        input_grad,
        vec_grad[:, 0],
        vec_grad[:, 1],
        qkv_grad,
        vec_grad[:, 2:5].reshape(layers, -1),
        out_w_grad,
        out_b_grad,
        up_grad,
        up_b_grad,
        down_grad,
        out_b_grad,
    )


def solution(mesh):
    rows = P(("dp", "mlp"), None)
    return jax.shard_map(
        body,
        mesh=mesh,
        in_specs=(
            rows,
            rows,
            P(),
            P(),
            P(),
            P(),
            P(),
            P(),
            P(None, None, "mlp"),
            P(None, "mlp"),
            P(None, "mlp", None),
            P(),
            rows,
        ),
        out_specs=(
            rows,
            rows,
            P(),
            P(),
            P(),
            P(),
            P(),
            P(),
            P(None, None, "mlp"),
            P(None, "mlp"),
            P(None, "mlp", None),
            P(),
        ),
        check_vma=False,
    )
```

```python
import functools
import math

import jax
import jax.numpy as jnp
from jax import lax
from jax.experimental import pallas as pl
from jax.experimental.pallas import tpu as pltpu
from jax.sharding import PartitionSpec as P

HEADS = 8
ROT = 16
HALF = ROT // 2
BLK = 256
norm_eps = 1e-05
rotary_base = 10000.0
bf16 = jnp.bfloat16
f32 = jnp.float32
NEG = -1e30
LOG2E = math.log2(math.e)
LN2 = math.log(2.0)


def dot_nn(a, b):
    return lax.dot_general(a, b, (((1,), (0,)), ((), ())), preferred_element_type=f32)


def dot_nt(a, b):
    return lax.dot_general(a, b, (((1,), (1,)), ((), ())), preferred_element_type=f32)


def dot_tn(a, b):
    return lax.dot_general(a, b, (((0,), (0,)), ((), ())), preferred_element_type=f32)


def row_of(ref, layer):
    return ref[...].astype(f32)[layer : layer + 1, :]


def doc_tables(lens, rows):
    lane = lax.broadcasted_iota(jnp.int32, (HALF, rows), 1)
    sub = lax.broadcasted_iota(jnp.int32, (HALF, rows), 0)
    start = jnp.int32(0)
    hot = jnp.zeros((HALF, rows), f32)
    first = jnp.zeros((HALF, rows), jnp.int32)
    for slot in range(lens.shape[1]):
        end = start + lens[0, slot]
        inside = (lane >= start) & (lane < end)
        hot = jnp.where(inside & (sub == slot), 1.0, hot)
        first = jnp.where(inside, start, first)
        start = end
    return hot, lane - first


def rotary_tables(position):
    index = lax.broadcasted_iota(jnp.int32, position.shape, 0).astype(f32)
    freqs = jnp.exp(index * (-2.0 / ROT * math.log(rotary_base)))
    angles = position.astype(f32) * freqs
    return jnp.cos(angles), jnp.sin(angles)


def rotate(values, cosines, sines):
    size = 64
    heads = values.shape[0] // size
    split = values.reshape(heads, size, values.shape[1])
    first, second, rest = split[:, :HALF], split[:, HALF:ROT], split[:, ROT:]
    turned = jnp.concatenate(
        [first * cosines - second * sines, second * cosines + first * sines, rest], axis=1
    )
    return turned.reshape(values.shape)


def mask_rows(hot):
    sub = lax.broadcasted_iota(jnp.int32, hot.shape, 0)
    rows = jnp.where(sub < 4, jnp.where(hot > 0.0, 0.0, NEG), jnp.where(sub < 7, 1.0, 0.0))
    return rows


def causal_bias():
    row = lax.broadcasted_iota(jnp.int32, (BLK, BLK), 0)
    col = lax.broadcasted_iota(jnp.int32, (BLK, BLK), 1)
    return jnp.where(row <= col, 0.0, NEG)


def norm_stats(values):
    centre = jnp.mean(values, axis=-1, keepdims=True)
    centred = values - centre
    spread = jnp.mean(centred * centred, axis=-1, keepdims=True)
    return centred, lax.rsqrt(spread + norm_eps)


def split3(value):
    a = value.astype(bf16).astype(f32)
    rest = value - a
    b = rest.astype(bf16).astype(f32)
    return jnp.concatenate([a, b, rest - b], axis=0)


MESH = pl.DeviceIdType.MESH
LINK_US_PER_MB = 20.0
CORE_US_PER_MB = 1.6


class Group:
    def __init__(self, bits, far=False):
        self.bits = bits
        self.size = 2 ** len(bits)
        self.values = [(lax.axis_index(axis) // 2**bit) % 2 for axis, bit in bits]
        self.me = sum(value * 2**i for i, value in enumerate(self.values))
        self.far = far

    def flips(self, k):
        return [(k >> i) & 1 for i in range(len(self.bits))]

    def index(self, k):
        total = 0
        for i, (value, flip) in enumerate(zip(self.values, self.flips(k))):
            total = total + (1 - value if flip else value) * 2**i
        return total

    def device(self, k):
        at = {"dp": lax.axis_index("dp"), "mlp": lax.axis_index("mlp")}
        for (axis, bit), value, flip in zip(self.bits, self.values, self.flips(k)):
            if flip:
                at[axis] = at[axis] + (1 - 2 * value) * 2**bit
        return (at["dp"], at["mlp"])

    def others(self):
        return range(1, self.size)


class Link:
    def __init__(self, src, dst, sems, index, device):
        self.parts = (src, dst, sems[0].at[index], sems[1].at[index], device)

    def copy(self):
        src, dst, send, recv, device = self.parts
        return pltpu.make_async_remote_copy(
            src_ref=src,
            dst_ref=dst,
            send_sem=send,
            recv_sem=recv,
            device_id=device,
            device_id_type=MESH,
        )


def add_rows(target, sources, start, count):
    step = count
    for size in (64, 48, 32, 16):
        if count % size == 0:
            step = size
            break

    def one(i, carry):
        at = pl.multiple_of(i * step, step)
        rows = pl.ds(pl.multiple_of(start + at, 16), step)
        total = target[rows, :].astype(f32)
        for source, first in sources:
            total = total + source[pl.ds(pl.multiple_of(first + at, 16), step), :].astype(f32)
        target[rows, :] = total.astype(bf16)
        return carry

    lax.fori_loop(0, count // step, one, 0)


class Unit:
    def __init__(self, grads, recv, groups, sems, first_sem, out, out_sem):
        self.steps = []
        self.first_sem = first_sem
        self.count = 0
        self.sems = sems
        halves = len(grads.shape) == 3
        start, rows = 0, grads.shape[-2]
        width = grads.shape[-1]
        used = 0
        backs = []
        mine = grads
        for group in groups:
            links, adds = [], []
            if halves and group.bits == [("mlp", 0)]:
                mine = grads.at[group.me]
                links.append(
                    self.link(
                        grads.at[group.index(1), pl.ds(start, rows), :],
                        recv.at[pl.ds(used, rows), :],
                        group.device(1),
                    )
                )
                adds.append((mine, [(recv, used)], start, rows))
                used += rows
                load = rows * width * 2
            else:
                part = rows // group.size
                where = [self.align(start + group.index(k) * part) for k in range(group.size)]
                targets = [grads.at[0], grads.at[1]] if len(mine.shape) == 3 else [mine]
                for target in targets:
                    sources = []
                    for k in group.others():
                        links.append(
                            self.link(
                                target.at[pl.ds(where[k], part), :],
                                recv.at[pl.ds(used, part), :],
                                group.device(k),
                            )
                        )
                        sources.append((recv, used))
                        used += part
                    adds.append((target, sources, where[0], part))
                load = part * width * 2 * len(targets)
                backs.append((where[0], part, group))
                start, rows = where[0], part
            self.steps.append((links, adds, group, load))
        self.reduced = len(self.steps)
        self.own = (mine.at[pl.ds(start, rows), :], out.at[pl.ds(start, rows), :], out_sem)
        source = mine
        for at, part, group in reversed(backs):
            links = [
                self.link(
                    source.at[pl.ds(at, part), :], out.at[pl.ds(at, part), :], group.device(k)
                )
                for k in group.others()
            ]
            source = out
            self.steps.append((links, [], group, part * width * 2))

    def align(self, at):
        return pl.multiple_of(at, 16)

    def link(self, src, dst, device):
        self.count += 1
        return Link(src, dst, self.sems, self.first_sem + self.count - 1, device)

    def start(self, at):
        for link in self.steps[at][0]:
            link.copy().start()
        if at == self.reduced:
            pltpu.make_async_copy(*self.own).start()

    def end(self, at):
        links, adds = self.steps[at][:2]
        if at == self.reduced:
            pltpu.make_async_copy(*self.own).wait()
        for link in links:
            copy = link.copy()
            copy.wait_send()
            copy.wait_recv()
        for target, sources, first, count in adds:
            add_rows(target, sources, first, count)

    def advance(self, at):
        if at >= 0:
            self.end(at)
        if at + 1 < len(self.steps):
            self.start(at + 1)


class Vector(Unit):
    def __init__(self, values, recv, groups, sems, first_sem):
        self.steps = []
        self.reduced = -1
        self.first_sem = first_sem
        self.count = 0
        self.sems = sems
        self.values = values
        self.recv = recv
        self.slots = []
        used = 0
        for stage, group in enumerate(groups):
            links = [
                self.link(values.at[stage], recv.at[used + group.me], group.device(k))
                for k in group.others()
            ]
            self.slots.append((used, group))
            used += group.size
            self.steps.append((links, [], group, 1))

    def start(self, at):
        used, group = self.slots[at]
        self.recv[used + group.me] = self.values[at]
        Unit.start(self, at)

    def end(self, at):
        Unit.end(self, at)
        used, group = self.slots[at]
        total = self.recv[used]
        for k in group.others():
            total = total + self.recv[used + k]
        self.values[at + 1] = total


def plan(slots, starts, units):
    free, state, actions = {}, {}, {name: [] for name, _ in slots}

    def begin(name, at, now):
        if at >= len(units[name].steps):
            state.pop(name)
            return
        _, _, group, load = units[name].steps[at]
        core = group.bits == [("dp", 0)]
        cost = load / 2**20 * (CORE_US_PER_MB if core else LINK_US_PER_MB)
        if group.size == 4:
            cost = cost * 2.0
        lag = 1.0 if core else (4.0 if group.far else 3.0)
        keys = [str(bit) for bit in group.bits] if not group.far else ["far"]
        ready = max([now] + [free.get(key, 0.0) for key in keys]) + cost
        for key in keys:
            free[key] = ready
        state[name] = (at, ready + lag)

    for slot, now in slots:
        for name in list(state):
            at, ready = state[name]
            if ready <= now:
                actions[slot].append((name, at))
                begin(name, at + 1, now)
        for name, slot_name in starts.items():
            if slot_name == slot:
                actions[slot].append((name, -1))
                begin(name, 0, now)
    now = slots[-1][1]
    last = slots[-1][0]
    while state:
        name = min(state, key=lambda key: state[key][1])
        at, ready = state[name]
        now = max(now, ready)
        actions[last].append((name, at))
        begin(name, at + 1, now)
    return actions


def bit_groups(pairs, join):
    core, mlp, first = ("dp", 0), ("mlp", 0), 1
    bits = list(range(1, pairs))
    stages = [Group([core])]
    if join and bits:
        stages.append(Group([mlp, ("dp", bits.pop(0))]))
    else:
        stages.append(Group([mlp]))
        if len(bits) % 2:
            stages.append(Group([("dp", bits.pop(0))]))
    while bits:
        take, bits = bits[:2], bits[2:]
        stages.append(Group([("dp", bit) for bit in take], far=True))
    return stages


def attention_forward(qkv, mix, lse, hot_s, mask_s, tri, krow, scores, probs, group, hook):
    tokens = qkv.shape[1]
    width = qkv.shape[0] // 3
    blocks = tokens // BLK

    def heads(step, carry):
        hook(step)
        tops = [{} for _ in range(group)]
        sums = [{} for _ in range(group)]
        rows = [pl.multiple_of((step * group + j) * 64, 64) for j in range(group)]
        for j in range(group):
            keyed = jnp.concatenate(
                [
                    qkv[pl.ds(width + rows[j], 64), :],
                    mask_s[...],
                    jnp.zeros((48, tokens), bf16),
                ],
                axis=0,
            )
            krow[j] = keyed.T
        for stage in range(group + 2):
            for i in range(blocks):
                n = (i + 1) * BLK
                at = slice(i * BLK, n)
                if stage < group:
                    j = stage
                    query = jnp.concatenate(
                        [qkv[pl.ds(rows[j], 64), at], hot_s[:, at], jnp.zeros((48, BLK), bf16)],
                        axis=0,
                    )
                    raw = dot_nn(krow[j, 0:n, :], query)
                    diagonal = raw[i * BLK :] + tri[...]
                    top = jnp.max(diagonal, axis=0, keepdims=True)
                    if i:
                        top = jnp.maximum(top, jnp.max(raw[: i * BLK], axis=0, keepdims=True))
                        scores[j % 2, i, 0 : i * BLK, :] = raw[: i * BLK]
                    scores[j % 2, i, i * BLK : n, :] = diagonal
                    tops[j][i] = top
                if 0 <= stage - 1 < group:
                    j = stage - 1
                    weights = jnp.exp2(scores[j % 2, i, 0:n, :] - tops[j][i])
                    sums[j][i] = jnp.sum(weights, axis=0, keepdims=True)
                    probs[j % 2, i, 0:n, :] = weights.astype(bf16)
                if 0 <= stage - 2 < group:
                    j = stage - 2
                    out = dot_nn(qkv[pl.ds(2 * width + rows[j], 64), 0:n], probs[j % 2, i, 0:n, :])
                    mix[pl.ds(rows[j], 64), at] = (out / sums[j][i]).astype(bf16)
                    lse[pl.ds(step * group + j, 1), at] = tops[j][i] + jnp.log2(sums[j][i])
        return carry

    lax.fori_loop(0, HEADS // group, heads, 0)


def forward_kernel(
    lens,
    block_input,
    gain,
    bias,
    qkv_bias,
    out_bias,
    up_bias,
    down_bias,
    qkv_w_h,
    out_w_h,
    up_w_h,
    down_w_h,
    block_output,
    stream_h,
    hid_h,
    qkv_h,
    mix_h,
    lse_h,
    act_h,
    slope_h,
    up_all_h,
    down_all_h,
    stream,
    hidden,
    hid,
    qkv,
    mix,
    lse,
    act,
    slope,
    qkv_w,
    out_w,
    up_w,
    down_w,
    qkv_b,
    up_b,
    pre,
    hot_s,
    mask_s,
    cos_s,
    sin_s,
    tri,
    krow,
    scores,
    probs,
    in_sem,
    out_sem,
    send_sem,
    recv_sem,
):
    tokens, width = block_input.shape
    layers = gain.shape[0]
    half = up_w.shape[3]
    blocks = tokens // BLK
    by_core, by_mlp, by_row = Group([("dp", 0)]), Group([("mlp", 0)]), Group([("dp", 1)])
    own, other = by_mlp.me, by_mlp.index(1)
    barrier = pltpu.get_barrier_semaphore()
    for group in (by_core, by_mlp, by_row):
        pl.semaphore_signal(barrier, inc=1, device_id=group.device(1), device_id_type=MESH)

    moves = {}
    sems = (send_sem, recv_sem)
    for layer in range(layers):
        for k, (src, dst) in enumerate(((up_w_h, up_w), (down_w_h, down_w))):
            quarter = src.shape[1] // 4
            first = pl.multiple_of((2 * by_core.me + by_row.me) * quarter, 16)
            pair = pl.multiple_of(2 * by_core.me * quarter, 16)
            mine = dst.at[layer, own, pl.ds(first, quarter), :]
            got = dst.at[layer, other, pl.ds(first, quarter), :]
            both = dst.at[layer, other, pl.ds(pair, 2 * quarter), :]
            at = (layer * 2 + k) * 3
            moves[layer, k] = [
                Link(src.at[layer, pl.ds(first, quarter), :], mine, sems, at, by_mlp.device(1)),
                Link(got, got, sems, at + 1, by_row.device(1)),
                Link(both, both, sems, at + 2, by_core.device(1)),
            ]
    bias_link = Link(up_b.at[own], up_b.at[own], sems, layers * 6, by_mlp.device(1))

    def begin(layer, k, step):
        moves[layer, k][step].copy().start()

    def end(layer, k, step):
        copy = moves[layer, k][step].copy()
        copy.wait_send()
        copy.wait_recv()

    loads = [
        [
            pltpu.make_async_copy(src.at[layer], dst, in_sem.at[layer, k])
            for k, (src, dst) in enumerate(
                (
                    (qkv_w_h, qkv_w.at[layer]),
                    (out_w_h, out_w.at[layer]),
                    (up_w_h, up_w.at[layer, own]),
                    (down_w_h, down_w.at[layer, own]),
                )
            )
        ]
        for layer in range(layers)
    ]
    for layer in range(layers):
        for copy in loads[layer]:
            copy.start()
    up_b[own, 0:layers, :] = up_bias[...].astype(f32)
    pl.semaphore_wait(barrier, 3)
    begin(0, 0, 0)
    begin(0, 1, 0)
    bias_link.copy().start()
    hot, position = doc_tables(lens, tokens)
    zeros8 = jnp.zeros_like(hot)
    hot_s[...] = jnp.concatenate([hot, zeros8], axis=0).astype(bf16)
    mask_s[...] = jnp.concatenate([mask_rows(hot), zeros8], axis=0).astype(bf16)
    cos_s[...], sin_s[...] = rotary_tables(position)
    tri[...] = causal_bias()
    stream[...] = block_input[...].astype(f32)
    stores = []
    for layer in range(layers):
        gain_row, bias_row = row_of(gain, layer), row_of(bias, layer)
        qkv_b[...] = jnp.broadcast_to(row_of(qkv_bias, layer), (128, 3 * width)).T

        for copy in stores:
            copy.wait()
        stores = []

        def norm_block(i, carry):
            rows = pl.ds(pl.multiple_of(i * BLK, BLK), BLK)
            centred, scale = norm_stats(stream[rows, :])
            low = (centred * scale * gain_row + bias_row).astype(bf16)
            hidden[rows, :] = low
            hid[:, rows] = low.T
            return carry

        lax.fori_loop(0, blocks, norm_block, 0)
        loads[layer][0].wait()
        for part in range(3):
            cols = slice(part * width, (part + 1) * width)
            for i in range(blocks):
                at = slice(i * BLK, (i + 1) * BLK)
                value = dot_tn(qkv_w[layer, :, cols], hid[:, at])
                column = qkv_b[cols, :]
                value = value + jnp.concatenate([column] * (BLK // 128), axis=1)
                if part < 2:
                    value = rotate(value, cos_s[:, at], sin_s[:, at])
                if part == 0:
                    value = value * (64**-0.5 * LOG2E)
                qkv[cols, at] = value.astype(bf16)

        def hook(step):
            if layer == 0:

                @pl.when(step == 1)
                def _():
                    end(0, 0, 0)
                    begin(0, 0, 1)

            else:
                for at in range(2):

                    @pl.when(step == at)
                    def _():
                        end(layer, at, 0)
                        begin(layer, at, 1)

        attention_forward(
            qkv, mix, lse, hot_s, mask_s, tri, krow, scores, probs, 4, hook
        )
        if layer == 0:
            end(0, 1, 0)
            begin(0, 1, 1)
            if layers > 1:
                begin(1, 0, 0)
                begin(1, 1, 0)
        else:
            for k in range(2):
                end(layer, k, 1)
                begin(layer, k, 2)


        def save(src, dst, k):
            copy = pltpu.make_async_copy(src, dst.at[layer], out_sem.at[k])
            copy.start()
            stores.append(copy)

        save(hid, hid_h, 0)
        save(qkv, qkv_h, 1)
        save(mix, mix_h, 2)
        save(lse, lse_h, 3)
        for k in range(1, 4):
            loads[layer][k].wait()
        shift = row_of(out_bias, layer) + row_of(down_bias, layer)
        chunk = 512

        def mlp_up(x, rows):
            row = up_b[x, layer : layer + 1, :]
            for c in range(half // chunk):
                cs = slice(c * chunk, (c + 1) * chunk)
                pre[:, cs] = dot_nn(hidden[rows, :], up_w[layer, x, :, cs]) + row[:, cs]
            for c in range(half // chunk):
                cs = slice(c * chunk, (c + 1) * chunk)
                u = pre[:, cs]
                cdf = 0.5 + 0.5 * lax.erf(u * (2.0**-0.5))
                pdf = jnp.exp2(u * u * (-0.5 * LOG2E)) * ((2.0 * math.pi) ** -0.5)
                act[x, rows, cs] = (u * cdf).astype(bf16)
                slope[x, rows, cs] = (cdf + u * pdf).astype(bf16)

        def own_block(i, carry):
            rows = pl.ds(pl.multiple_of(i * BLK, BLK), BLK)
            mlp_up(own, rows)
            total = dot_tn(mix[:, rows], out_w[layer]) + dot_nn(act[own, rows, :], down_w[layer, own])
            stream[rows, :] = stream[rows, :] + (total + shift)
            return carry

        def other_up(i, carry):
            mlp_up(other, pl.ds(pl.multiple_of(i * BLK, BLK), BLK))
            return carry

        def other_down(i, carry):
            rows = pl.ds(pl.multiple_of(i * BLK, BLK), BLK)
            stream[rows, :] = stream[rows, :] + dot_nn(act[other, rows, :], down_w[layer, other])
            return carry

        lax.fori_loop(0, blocks, own_block, 0)
        if layer == 0:
            copy = bias_link.copy()
            copy.wait_send()
            copy.wait_recv()
            for k in range(2):
                end(0, k, 1)
                begin(0, k, 2)
        end(layer, 0, 2)
        lax.fori_loop(0, blocks, other_up, 0)
        save(slope, slope_h, 5)
        save(up_w.at[layer], up_all_h, 7)
        end(layer, 1, 2)
        lax.fori_loop(0, blocks, other_down, 0)
        save(down_w.at[layer], down_all_h, 8)
        save(act, act_h, 4)
        if layer + 1 < layers:
            copy = pltpu.make_async_copy(stream, stream_h, out_sem.at[6])
            copy.start()
            stores.append(copy)
    block_output[...] = stream[...].astype(bf16)
    for copy in stores:
        copy.wait()


def attention_backward(qkv, mix, grad_mix, lse, hot_s, mask_s, tri, cos_s, sin_s, work, group, hook):
    krow, vrow, qext, gext, probs, dscore = work
    tokens = qkv.shape[1]
    width = qkv.shape[0] // 3
    blocks = tokens // BLK
    ones = jnp.where(lax.broadcasted_iota(jnp.int32, (64, tokens), 0) < 3, 1.0, 0.0).astype(bf16)

    def heads(step, carry):
        hook(step)
        rows = [pl.multiple_of((step * group + j) * 64, 64) for j in range(group)]
        for j in range(group):
            r = rows[j]
            keyed = jnp.concatenate(
                [qkv[pl.ds(width + r, 64), :], mask_s[...], jnp.zeros((48, tokens), bf16)], axis=0
            )
            krow[j] = keyed.T
            vrow[j] = jnp.concatenate([qkv[pl.ds(2 * width + r, 64), :], ones], axis=0).T
            grad = grad_mix[pl.ds(r, 64), :].astype(f32)
            total = jnp.sum(grad * mix[pl.ds(r, 64), :].astype(f32), axis=0, keepdims=True)
            qext[j] = jnp.concatenate(
                [
                    qkv[pl.ds(r, 64), :].astype(f32),
                    hot_s[0:4, :].astype(f32),
                    split3(-lse[pl.ds(step * group + j, 1), :]),
                    jnp.zeros((57, tokens), f32),
                ],
                axis=0,
            ).astype(bf16)
            gext[j] = jnp.concatenate(
                [grad, split3(-total), jnp.zeros((61, tokens), f32)], axis=0
            ).astype(bf16)
        for j in range(group):
            r = rows[j]
            for i in range(blocks):
                n = (i + 1) * BLK
                at = slice(i * BLK, n)
                raw = dot_nn(krow[j, 0:n, :], qext[j, :, at])
                if i:
                    raw = jnp.concatenate([raw[: i * BLK], raw[i * BLK :] + tri[...]], axis=0)
                else:
                    raw = raw + tri[...]
                weights = jnp.exp2(raw)
                slopes = dot_nn(vrow[j, 0:n, :], gext[j, :, at])
                dscore[0:n, at] = (weights * slopes).astype(bf16)
                probs[0:n, at] = weights.astype(bf16)
            dq, dk, dv = [], [], []
            for i in range(blocks):
                n = (i + 1) * BLK
                at = slice(i * BLK, n)
                dq.append(dot_nn(qkv[pl.ds(width + r, 64), 0:n], dscore[0:n, at]))
                dk.append(dot_nt(qkv[pl.ds(r, 64), i * BLK :], dscore[at, i * BLK :]))
                dv.append(dot_nt(grad_mix[pl.ds(r, 64), i * BLK :], probs[at, i * BLK :]))
            dq = jnp.concatenate(dq, axis=1) * 64**-0.5
            dk = jnp.concatenate(dk, axis=1) * LN2
            qkv[pl.ds(r, 64), :] = rotate(dq, cos_s[...], -sin_s[...]).astype(bf16)
            qkv[pl.ds(width + r, 64), :] = rotate(dk, cos_s[...], -sin_s[...]).astype(bf16)
            qkv[pl.ds(2 * width + r, 64), :] = jnp.concatenate(dv, axis=1).astype(bf16)
        return carry

    lax.fori_loop(0, HEADS // group, heads, 0)


def backward_kernel(
    pairs,
    lens,
    gain,
    block_input,
    out_grad,
    qkv_w_h,
    out_w_h,
    up_w_h,
    down_w_h,
    stream_h,
    hid_h,
    qkv_h,
    mix_h,
    lse_h,
    act_h,
    slope_h,
    input_grad,
    mlp_out,
    att_out,
    vec_out,
    stream,
    grad_low,
    grad_mix,
    grad_hid,
    hid,
    qkv,
    mix,
    lse,
    act,
    slope,
    qkv_w,
    out_w,
    up_w,
    down_w,
    hot_s,
    mask_s,
    cos_s,
    sin_s,
    tri,
    krow,
    vrow,
    qext,
    gext,
    probs,
    dscore,
    mlp_grad,
    att_grad,
    vec_grad,
    mlp_recv,
    att_recv,
    vec_recv,
    in_sem,
    out_sem,
    send_sem,
    recv_sem,
):
    tokens, width = grad_low.shape
    layers = gain.shape[0]
    half = up_w.shape[2]
    units = 2 * half
    blocks = tokens // BLK
    last = layers - 1
    grad = input_grad
    split = pairs <= 4

    def load(src, dst, layer, k):
        copy = pltpu.make_async_copy(src, dst, in_sem.at[layer, k])
        copy.start()
        return copy

    loads = {
        "act": lambda l: load(act_h.at[l], act, l, 0),
        "slope": lambda l: load(slope_h.at[l], slope, l, 1),
        "down": lambda l: load(down_w_h.at[l], down_w, l, 2),
        "up": lambda l: load(up_w_h.at[l], up_w, l, 3),
        "hid": lambda l: load(hid_h.at[l], hid.at[0:width, :], l, 4),
        "qkv": lambda l: load(qkv_h.at[l], qkv, l, 5),
        "mix": lambda l: load(mix_h.at[l], mix, l, 6),
        "lse": lambda l: load(lse_h.at[l], lse, l, 7),
        "out_w": lambda l: load(out_w_h.at[l], out_w, l, 8),
        "qkv_w": lambda l: load(qkv_w_h.at[l], qkv_w, l, 9),
    }
    first_load = load(out_grad, grad_low, 0, 10)
    flight = {}
    for name in ("act", "slope", "down", "up", "hid", "out_w", "mix", "qkv", "lse", "qkv_w"):
        flight[name] = loads[name](last)
    stream_load = load(stream_h, stream, 1, 10)

    slow, fast = bit_groups(pairs, False), bit_groups(pairs, True)
    barrier = pltpu.get_barrier_semaphore()
    known = []
    for group in slow + fast[1:2]:
        for k in group.others():
            flips = tuple(b for b, f in zip(group.bits, group.flips(k)) if f)
            if flips not in known:
                known.append(flips)
                pl.semaphore_signal(
                    barrier, inc=1, device_id=group.device(k), device_id_type=MESH
                )

    sems = (send_sem, recv_sem)
    travel, used_sems = {}, [0]

    def add(name, kind, *rest):
        values, recv, groups, *out = rest
        travel[name] = kind(values, recv, groups, sems, used_sems[0], *out)
        used_sems[0] += travel[name].count

    att_rows = att_grad.shape[1]
    cut = 5 * width
    for layer in range(layers):
        for k, name in enumerate(("up", "down")):
            rows = slice(k * half, (k + 1) * half)
            add(
                name + str(layer),
                Unit,
                mlp_grad.at[layer, :, rows, :],
                mlp_recv.at[layer, k],
                slow,
                mlp_out.at[layer, rows, :],
                out_sem.at[layer * 4 + k],
            )
        pieces = ((0, cut), (cut, att_rows)) if split else ((0, att_rows),)
        for k, (a, b) in enumerate(pieces):
            add(
                "att" + str(k) + str(layer),
                Unit,
                att_grad.at[layer, a:b, :],
                att_recv.at[layer, a:b, :],
                fast if layer == 0 else slow,
                att_out.at[layer, a:b, :],
                out_sem.at[layer * 4 + 2 + k],
            )
        stages = fast if layer == 0 else slow
        add(
            "vec" + str(layer),
            Vector,
            vec_grad.at[layer],
            vec_recv.at[layer],
            stages,
        )

    points, now, starts = [], 3.0, {}
    for layer in reversed(range(layers)):
        tag = str(layer)

        def point(name, cost):
            nonlocal now
            now += cost
            points.append((name + tag, now))

        point("down", 3.0)
        for i in range(blocks):
            point("mlp%d_" % i, 1.5)
        point("up", 3.0)
        for i in range(4):
            point("head%d_" % i, 2.0 if i == 0 else 4.2 if i == 2 else 3.5)
        point("att", 4.2)
        for i in range(blocks):
            point("norm%d_" % i, 0.7)
        point("end", 0.2)
        starts["down" + tag] = "down" + tag
        starts["up" + tag] = "up" + tag
        if split:
            starts["att0" + tag] = "head2_" + tag
            starts["att1" + tag] = "att" + tag
        else:
            starts["att0" + tag] = "att" + tag
        starts["vec" + tag] = "end" + tag
    actions = plan(points, starts, travel)

    def run(name):
        for unit, at in actions[name]:
            travel[unit].advance(at)

    def run_at(step, count, name, layer):
        for i in range(count):
            key = name % i + str(layer)
            if actions[key]:

                @pl.when(step == i)
                def _():
                    run(key)

    hot, position = doc_tables(lens, tokens)
    zeros8 = jnp.zeros_like(hot)
    hot_s[...] = jnp.concatenate([hot, zeros8], axis=0).astype(bf16)
    mask_s[...] = jnp.concatenate([mask_rows(hot), zeros8], axis=0).astype(bf16)
    cos_s[...], sin_s[...] = rotary_tables(position)
    tri[...] = causal_bias()
    hid[width : width + 16, :] = jnp.ones((16, tokens), bf16)
    first_load.wait()
    grad[...] = grad_low[...].astype(f32)
    pl.semaphore_wait(barrier, len(known))

    for layer in reversed(range(layers)):

        def ahead(*names):
            if layer:
                for name in names:
                    flight[name] = loads[name](layer - 1)

        flight["act"].wait()
        for c in range(units // 512):
            x, at = divmod(c * 512, half)
            mlp_grad[layer, x, half + at : half + at + 512, :] = dot_tn(
                act[x, :, at : at + 512], grad_low[...]
            ).astype(bf16)
        run("down" + str(layer))
        ahead("act")
        for name in ("slope", "down", "up"):
            flight[name].wait()

        def mlp_block(i, carry):
            rows = pl.ds(pl.multiple_of(i * BLK, BLK), BLK)
            for c in range(units // 512):
                x, at = divmod(c * 512, half)
                cs = slice(at, at + 512)
                da = dot_nt(grad_low[rows, :], down_w[x, cs, :])
                slope[x, rows, cs] = (slope[x, rows, cs].astype(f32) * da).astype(bf16)
            grad_hid[rows, :] = dot_nt(slope[0, rows, :], up_w[0]) + dot_nt(
                slope[1, rows, :], up_w[1]
            )
            run_at(i, blocks, "mlp%d_", layer)
            return carry

        lax.fori_loop(0, blocks, mlp_block, 0)
        ahead("down", "up")
        flight["hid"].wait()
        for c in range(units // 512):
            x, at = divmod(c * 512, half)
            up = dot_nn(hid[...], slope[x, :, at : at + 512])
            mlp_grad[layer, x, at : at + 512, :] = up[:width].astype(bf16)
            vec_grad[layer, 0, 6 + c : 7 + c, :] = up[width : width + 1]
        run("up" + str(layer))
        ahead("slope")
        for name in ("out_w", "mix", "qkv", "lse"):
            flight[name].wait()
        out_grads = dot_nn(mix[...], grad_low[...]).astype(bf16)
        att_grad[layer, 3 * width : 4 * width, :] = out_grads[:, : width // 2]
        att_grad[layer, 4 * width : 5 * width, :] = out_grads[:, width // 2 :]
        vec_grad[layer, 0, 5:6, :] = jnp.sum(grad_low[...].astype(f32), axis=0, keepdims=True)
        grad_mix[...] = dot_nt(out_w[...], grad_low[...]).astype(bf16)
        ahead("out_w")
        if layer == 0:
            input_load = load(block_input, grad_low, 0, 11)

        def qkv_grads(g):
            for part in range(3):
                first = part * width + g * (width // 2)
                got = dot_nt(hid[...], qkv[first : first + width // 2, :])
                to = (5 * g + part) * width
                att_grad[layer, to : to + width, :] = got[:width].astype(bf16)
                vec_grad[
                    layer, 0, 2 + part : 3 + part, g * (width // 2) : (g + 1) * (width // 2)
                ] = got[width : width + 1]

        def head_hook(step):
            @pl.when(step == 2)
            def _():
                qkv_grads(0)

            run_at(step, 4, "head%d_", layer)

        attention_backward(
            qkv,
            mix,
            grad_mix,
            lse,
            hot_s,
            mask_s,
            tri,
            cos_s,
            sin_s,
            (krow, vrow, qext, gext, probs, dscore),
            2,
            head_hook,
        )
        qkv_grads(1)
        run("att" + str(layer))
        ahead("hid", "mix", "lse")
        flight["qkv_w"].wait()
        if layer == last:
            stream_load.wait()
        if layer == 0:
            input_load.wait()
        gain_row = row_of(gain, layer)
        vec_grad[layer, 0, 0:2, :] = jnp.zeros((2, width), f32)
        vec_grad[layer, 0, 10:16, :] = jnp.zeros((6, width), f32)

        def norm_block(i, carry):
            rows = pl.ds(pl.multiple_of(i * BLK, BLK), BLK)
            back = lax.dot_general(
                qkv[:, rows], qkv_w[...], (((0,), (1,)), ((), ())), preferred_element_type=f32
            )
            dh = grad_hid[rows, :] + back
            if layer:
                centred, scale = norm_stats(stream[rows, :])
            else:
                centred, scale = norm_stats(grad_low[rows, :].astype(f32))
            n = centred * scale
            product = dh * n
            vec_grad[layer, 0, 0:1, :] += jnp.sum(product, axis=0, keepdims=True)
            vec_grad[layer, 0, 1:2, :] += jnp.sum(dh, axis=0, keepdims=True)
            e = dh * gain_row
            mean_e = jnp.mean(e, axis=-1, keepdims=True)
            mean_en = jnp.mean(product * gain_row, axis=-1, keepdims=True)
            total = grad[rows, :] + scale * (e - mean_e - n * mean_en)
            grad[rows, :] = total
            if layer:
                grad_low[rows, :] = total.astype(bf16)
            run_at(i, blocks, "norm%d_", layer)
            return carry

        lax.fori_loop(0, blocks, norm_block, 0)
        ahead("qkv", "qkv_w")
        run("end" + str(layer))
    for layer in range(layers):
        vec_out[layer] = vec_grad[layer, len(travel["vec" + str(layer)].steps)]


VMEM = pl.BlockSpec(memory_space=pltpu.VMEM)
SMEM = pl.BlockSpec(memory_space=pltpu.SMEM)
ANY = pl.BlockSpec(memory_space=pl.ANY)


def run_forward(lens, block_input, gain, bias, qkv_b, out_b, up_b, down_b, qkv_w, out_w, up_w, down_w):
    tokens, width = block_input.shape
    layers = gain.shape[0]
    half = up_w.shape[2]
    shape = jax.ShapeDtypeStruct
    v = pltpu.VMEM
    return pl.pallas_call(
        forward_kernel,
        out_shape=(
            shape((tokens, width), bf16),
            shape((tokens, width), f32),
            shape((layers, width, tokens), bf16),
            shape((layers, 3 * width, tokens), bf16),
            shape((layers, width, tokens), bf16),
            shape((layers, HEADS, tokens), f32),
            shape((layers, 2, tokens, half), bf16),
            shape((layers, 2, tokens, half), bf16),
            shape((layers, 2, width, half), bf16),
            shape((layers, 2, half, width), bf16),
        ),
        in_specs=[SMEM] + [VMEM] * 7 + [ANY] * 4,
        out_specs=(VMEM,) + (ANY,) * 9,
        scratch_shapes=[
            v((tokens, width), f32),
            v((tokens, width), bf16),
            v((width, tokens), bf16),
            v((3 * width, tokens), bf16),
            v((width, tokens), bf16),
            v((HEADS, tokens), f32),
            v((2, tokens, half), bf16),
            v((2, tokens, half), bf16),
            v((layers, width, 3 * width), bf16),
            v((layers, width, width), bf16),
            v((layers, 2, width, half), bf16),
            v((layers, 2, half, width), bf16),
            v((3 * width, 128), f32),
            v((2, 8, half), f32),
            v((BLK, half), f32),
            v((16, tokens), bf16),
            v((16, tokens), bf16),
            v((HALF, tokens), f32),
            v((HALF, tokens), f32),
            v((BLK, BLK), f32),
            v((4, tokens, 128), bf16),
            v((2, tokens // BLK, tokens, BLK), f32),
            v((2, tokens // BLK, tokens, BLK), bf16),
            pltpu.SemaphoreType.DMA((layers, 4)),
            pltpu.SemaphoreType.DMA((9,)),
            pltpu.SemaphoreType.DMA((layers * 6 + 1,)),
            pltpu.SemaphoreType.DMA((layers * 6 + 1,)),
        ],
        compiler_params=pltpu.CompilerParams(
            vmem_limit_bytes=63 * 2**20, collective_id=1, has_side_effects=True
        ),
        name="forward",
    )(lens, block_input, gain, bias, qkv_b, out_b, up_b, down_b, qkv_w, out_w, up_w, down_w)


def run_backward(lens, block_input, out_grad, gain, qkv_w, out_w, up_w, down_w, saved):
    tokens, width = block_input.shape
    layers = gain.shape[0]
    half = up_w.shape[3]
    units = 2 * half
    shape = jax.ShapeDtypeStruct
    v = pltpu.VMEM
    pairs = lax.axis_size("dp").bit_length() - 1
    mlp_rows, att_rows = units, 8 * width
    n_sems = 160
    return pl.pallas_call(
        functools.partial(backward_kernel, pairs),
        out_shape=(
            shape((tokens, width), f32),
            shape((layers, units, width), bf16),
            shape((layers, 8 * width, width // 2), bf16),
            shape((layers, 16, width), f32),
        ),
        in_specs=[SMEM, VMEM] + [ANY] * 13,
        out_specs=(VMEM, ANY, ANY, VMEM),
        scratch_shapes=[
            v((tokens, width), f32),
            v((tokens, width), bf16),
            v((width, tokens), bf16),
            v((tokens, width), f32),
            v((width + 16, tokens), bf16),
            v((3 * width, tokens), bf16),
            v((width, tokens), bf16),
            v((HEADS, tokens), f32),
            v((2, tokens, half), bf16),
            v((2, tokens, half), bf16),
            v((width, 3 * width), bf16),
            v((width, width), bf16),
            v((2, width, half), bf16),
            v((2, half, width), bf16),
            v((16, tokens), bf16),
            v((16, tokens), bf16),
            v((HALF, tokens), f32),
            v((HALF, tokens), f32),
            v((BLK, BLK), f32),
            v((2, tokens, 128), bf16),
            v((2, tokens, 128), bf16),
            v((2, 128, tokens), bf16),
            v((2, 128, tokens), bf16),
            v((tokens, tokens), bf16),
            v((tokens, tokens), bf16),
            v((layers, 2, units, width), bf16),
            v((layers, 8 * width, width // 2), bf16),
            v((layers, 8, 16, width), f32),
            v((layers, 2, units, width), bf16),
            v((layers, 8 * width, width // 2), bf16),
            v((layers, 16, 16, width), f32),
            pltpu.SemaphoreType.DMA((layers, 12)),
            pltpu.SemaphoreType.DMA((4 * layers,)),
            pltpu.SemaphoreType.DMA((n_sems,)),
            pltpu.SemaphoreType.DMA((n_sems,)),
        ],
        compiler_params=pltpu.CompilerParams(
            vmem_limit_bytes=63 * 2**20, collective_id=0, has_side_effects=True
        ),
        name="backward",
    )(lens, gain, block_input, out_grad, qkv_w, out_w, up_w, down_w, *saved)


def body(
    block_input,
    doc_lengths,
    norm_gain,
    norm_bias,
    qkv_weight,
    qkv_bias,
    out_weight,
    out_bias,
    up_weight,
    up_bias,
    down_weight,
    down_bias,
    out_grad,
):
    layers, width = norm_gain.shape
    block_output, *saved, up_all, down_all = run_forward(
        doc_lengths,
        block_input,
        norm_gain,
        norm_bias,
        qkv_bias,
        out_bias,
        up_bias,
        down_bias,
        qkv_weight,
        out_weight,
        up_weight,
        down_weight,
    )
    input_grad, mlp_grad, att_grad, vec_grad = run_backward(
        doc_lengths,
        block_input,
        out_grad,
        norm_gain,
        qkv_weight,
        out_weight,
        up_all,
        down_all,
        saved,
    )
    return finish(block_output, input_grad, mlp_grad, att_grad, vec_grad)


def finish(block_output, input_grad, mlp_grad, att_grad, vec_grad):
    layers, units, width = mlp_grad.shape
    half = units // 2
    low = [mlp_grad[:, at : at + width] for at in range(0, half, width)]
    up_grad = jnp.concatenate(low, axis=2).astype(f32)
    down_grad = mlp_grad[:, half:].astype(f32)
    order = (0, 5, 1, 6, 2, 7)
    low = [att_grad[:, at * width : (at + 1) * width] for at in order]
    qkv_grad = jnp.concatenate(low, axis=2).astype(f32)
    low = [att_grad[:, at * width : (at + 1) * width] for at in (3, 4)]
    out_w_grad = jnp.concatenate(low, axis=2).astype(f32)
    out_b_grad = vec_grad[:, 5]
    up_b_all = vec_grad[:, 6 : 6 + units // width].reshape(layers, -1)
    up_b_grad = lax.dynamic_slice_in_dim(up_b_all, lax.axis_index("mlp") * half, half, 1)
    return (
        block_output,
        input_grad,
        vec_grad[:, 0],
        vec_grad[:, 1],
        qkv_grad,
        vec_grad[:, 2:5].reshape(layers, -1),
        out_w_grad,
        out_b_grad,
        up_grad,
        up_b_grad,
        down_grad,
        out_b_grad,
    )


def solution(mesh):
    rows = P(("dp", "mlp"), None)
    return jax.shard_map(
        body,
        mesh=mesh,
        in_specs=(
            rows,
            rows,
            P(),
            P(),
            P(),
            P(),
            P(),
            P(),
            P(None, None, "mlp"),
            P(None, "mlp"),
            P(None, "mlp", None),
            P(),
            rows,
        ),
        out_specs=(
            rows,
            rows,
            P(),
            P(),
            P(),
            P(),
            P(),
            P(),
            P(None, None, "mlp"),
            P(None, "mlp"),
            P(None, "mlp", None),
            P(),
        ),
        check_vma=False,
    )
```

```python
import functools
import math

import jax
import jax.numpy as jnp
from jax import lax
from jax.experimental import pallas as pl
from jax.experimental.pallas import tpu as pltpu
from jax.sharding import PartitionSpec as P

HEADS = 8
ROT = 16
HALF = ROT // 2
BLK = 256
norm_eps = 1e-05
rotary_base = 10000.0
bf16 = jnp.bfloat16
f32 = jnp.float32
NEG = -1e30
LOG2E = math.log2(math.e)
LN2 = math.log(2.0)


def dot_nn(a, b):
    return lax.dot_general(a, b, (((1,), (0,)), ((), ())), preferred_element_type=f32)


def dot_nt(a, b):
    return lax.dot_general(a, b, (((1,), (1,)), ((), ())), preferred_element_type=f32)


def dot_tn(a, b):
    return lax.dot_general(a, b, (((0,), (0,)), ((), ())), preferred_element_type=f32)


def row_of(ref, layer):
    return ref[...].astype(f32)[layer : layer + 1, :]


def doc_tables(lens, rows):
    lane = lax.broadcasted_iota(jnp.int32, (HALF, rows), 1)
    sub = lax.broadcasted_iota(jnp.int32, (HALF, rows), 0)
    start = jnp.int32(0)
    hot = jnp.zeros((HALF, rows), f32)
    first = jnp.zeros((HALF, rows), jnp.int32)
    for slot in range(lens.shape[1]):
        end = start + lens[0, slot]
        inside = (lane >= start) & (lane < end)
        hot = jnp.where(inside & (sub == slot), 1.0, hot)
        first = jnp.where(inside, start, first)
        start = end
    return hot, lane - first


def rotary_tables(position):
    index = lax.broadcasted_iota(jnp.int32, position.shape, 0).astype(f32)
    freqs = jnp.exp(index * (-2.0 / ROT * math.log(rotary_base)))
    angles = position.astype(f32) * freqs
    return jnp.cos(angles), jnp.sin(angles)


def rotate(values, cosines, sines):
    size = 64
    heads = values.shape[0] // size
    split = values.reshape(heads, size, values.shape[1])
    first, second, rest = split[:, :HALF], split[:, HALF:ROT], split[:, ROT:]
    turned = jnp.concatenate(
        [first * cosines - second * sines, second * cosines + first * sines, rest], axis=1
    )
    return turned.reshape(values.shape)


def mask_rows(hot):
    sub = lax.broadcasted_iota(jnp.int32, hot.shape, 0)
    rows = jnp.where(sub < 4, jnp.where(hot > 0.0, 0.0, NEG), jnp.where(sub < 7, 1.0, 0.0))
    return rows


def causal_bias():
    row = lax.broadcasted_iota(jnp.int32, (BLK, BLK), 0)
    col = lax.broadcasted_iota(jnp.int32, (BLK, BLK), 1)
    return jnp.where(row <= col, 0.0, NEG)


def norm_stats(values):
    centre = jnp.mean(values, axis=-1, keepdims=True)
    centred = values - centre
    spread = jnp.mean(centred * centred, axis=-1, keepdims=True)
    return centred, lax.rsqrt(spread + norm_eps)


def split3(value):
    a = value.astype(bf16).astype(f32)
    rest = value - a
    b = rest.astype(bf16).astype(f32)
    return jnp.concatenate([a, b, rest - b], axis=0)


MESH = pl.DeviceIdType.MESH

BITS = {
    "C": (("dp", 0),),
    "X": (("mlp", 0),),
    "Y": (("dp", 1),),
    "a": (("dp", 2),),
    "b": (("dp", 3),),
    "Z": (("dp", 2), ("dp", 3)),
    "W": (("mlp", 0), ("dp", 1)),
}
COST = {
    "C": ({"C": 1.6}, 1.1),
    "X": ({"X": 24.0}, 2.8),
    "Y": ({"Y": 24.0}, 2.6),
    "a": ({"outer": 24.0}, 2.6),
    "b": ({"middle": 48.0, "outer": 24.0}, 2.9),
    "Z": ({"middle": 96.0, "outer": 72.0}, 2.4),
    "W": ({"X": 52.0, "Y": 52.0}, 3.0),
}
ORDERS = {
    "down0_1": "YXZ",
    "down1_1": "XYZ",
    "up0_1": "YXZ",
    "up1_1": "XYZ",
    "out_1": "XYab",
    "a_1": "XYab",
    "b_1": "YXab",
    "c_1": "XYab",
    "vec_1": "XYZ",
    "down0_0": "YXZ",
    "down1_0": "XYZ",
    "up0_0": "aXYb",
    "up1_0": "XYab",
    "out_0": "aWb",
    "a_0": "XYZ",
    "b_0": "YXZ",
    "c_0": "YXZ",
    "vec_0": "WZ",
}


def groups_of(order, pairs):
    groups, left = [], set(range(1, pairs))
    for name in order:
        bits = [bit for bit in BITS[name] if bit[0] == "mlp" or bit[1] < pairs]
        left -= {bit for axis, bit in bits if axis == "dp"}
        if bits:
            groups.append(Group(name, bits))
    left = sorted(left)
    while left:
        take, left = left[:2], left[2:]
        groups.append(Group("Z", [("dp", bit) for bit in take]))
    return groups


class Group:
    def __init__(self, name, bits):
        self.name = name
        self.bits = bits
        self.size = 2 ** len(bits)
        self.values = [(lax.axis_index(axis) // 2**bit) % 2 for axis, bit in bits]
        self.me = sum(value * 2**i for i, value in enumerate(self.values))

    def flips(self, k):
        return [(k >> i) & 1 for i in range(len(self.bits))]

    def index(self, k):
        total = 0
        for i, (value, flip) in enumerate(zip(self.values, self.flips(k))):
            total = total + (1 - value if flip else value) * 2**i
        return total

    def device(self, k):
        at = {"dp": lax.axis_index("dp"), "mlp": lax.axis_index("mlp")}
        for (axis, bit), value, flip in zip(self.bits, self.values, self.flips(k)):
            if flip:
                at[axis] = at[axis] + (1 - 2 * value) * 2**bit
        return (at["dp"], at["mlp"])

    def others(self):
        return range(1, self.size)


class Link:
    def __init__(self, src, dst, sems, index, device):
        self.parts = (src, dst, sems[0].at[index], sems[1].at[index], device)

    def copy(self):
        src, dst, send, recv, device = self.parts
        return pltpu.make_async_remote_copy(
            src_ref=src,
            dst_ref=dst,
            send_sem=send,
            recv_sem=recv,
            device_id=device,
            device_id_type=MESH,
        )

    def start(self):
        self.copy().start()

    def wait(self):
        copy = self.copy()
        copy.wait_send()
        copy.wait_recv()


def add_rows(target, sources, start, count):
    step = count
    for size in (64, 48, 32, 16):
        if count % size == 0:
            step = size
            break

    def one(i, carry):
        at = pl.multiple_of(i * step, step)
        rows = pl.ds(pl.multiple_of(start + at, 16), step)
        total = target[rows, :].astype(f32)
        for source, first in sources:
            total = total + source[pl.ds(pl.multiple_of(first + at, 16), step), :].astype(f32)
        target[rows, :] = total.astype(bf16)
        return carry

    lax.fori_loop(0, count // step, one, 0)


class Unit:
    def __init__(self, sems, first_sem, grads, start, rows, recv, groups, core, out, out_sem):
        self.steps = []
        self.first_sem = first_sem
        self.count = 0
        self.sems = sems
        width = grads.shape[-1]
        mib = width * 2 / 2**20
        used = 0
        backs = [(start, rows, core)]
        mine = grads
        for group in groups:
            links, adds = [], []
            if len(mine.shape) == 3 and group.bits == [("mlp", 0)]:
                mine = grads.at[group.me]
                links.append(
                    self.link(
                        grads.at[group.index(1), pl.ds(start, rows), :],
                        recv.at[pl.ds(used, rows), :],
                        group.device(1),
                    )
                )
                adds.append((mine, [(recv, used)], start, rows))
                used += rows
                load = added = rows * mib
            else:
                part = rows // group.size
                where = [
                    pl.multiple_of(start + group.index(k) * part, 16) for k in range(group.size)
                ]
                targets = [grads.at[0], grads.at[1]] if len(mine.shape) == 3 else [mine]
                for target in targets:
                    sources = []
                    for k in group.others():
                        links.append(
                            self.link(
                                target.at[pl.ds(where[k], part), :],
                                recv.at[pl.ds(used, part), :],
                                group.device(k),
                            )
                        )
                        sources.append((recv, used))
                        used += part
                    adds.append((target, sources, where[0], part))
                load = part * mib * len(targets)
                added = load * (group.size - 1)
                start, rows = where[0], part
                backs.append((start, rows, group))
            self.steps.append((links, adds, group, load, added))
        self.reduced = len(self.steps)
        self.own = (mine.at[pl.ds(start, rows), :], out.at[pl.ds(start, rows), :], out_sem)
        source = mine
        for at, part, group in reversed(backs):
            links = [
                self.link(
                    source.at[pl.ds(at, part), :], out.at[pl.ds(at, part), :], group.device(k)
                )
                for k in group.others()
            ]
            source = out
            self.steps.append((links, [], group, part * mib, 0.0))

    def link(self, src, dst, device):
        self.count += 1
        return Link(src, dst, self.sems, self.first_sem + self.count - 1, device)

    def start(self, at):
        for link in self.steps[at][0]:
            link.copy().start()
        if at == self.reduced:
            pltpu.make_async_copy(*self.own).start()

    def end(self, at):
        links, adds = self.steps[at][:2]
        if at == self.reduced:
            pltpu.make_async_copy(*self.own).wait()
        for link in links:
            link.wait()
        for target, sources, first, count in adds:
            add_rows(target, sources, first, count)

    def advance(self, at):
        if at >= 0:
            self.end(at)
        if at + 1 < len(self.steps):
            self.start(at + 1)


class Vector(Unit):
    def __init__(self, sems, first_sem, values, recv, groups):
        self.steps = []
        self.reduced = -1
        self.first_sem = first_sem
        self.count = 0
        self.sems = sems
        self.values = values
        self.recv = recv
        self.slots = []
        used = 0
        for stage, group in enumerate(groups):
            links = [
                self.link(values.at[stage], recv.at[used + group.me], group.device(k))
                for k in group.others()
            ]
            self.slots.append((used, group))
            used += group.size
            self.steps.append((links, [], group, 0.03, 0.03))

    def start(self, at):
        used, group = self.slots[at]
        self.recv[used + group.me] = self.values[at]
        Unit.start(self, at)

    def end(self, at):
        Unit.end(self, at)
        used, group = self.slots[at]
        total = self.recv[used]
        for k in group.others():
            total = total + self.recv[used + k]
        self.values[at + 1] = total


def plan(points, starts, units):
    free, state, actions = {}, {}, {name: [] for name, _ in points}
    now = 0.0

    def begin(name, at):
        if at >= len(units[name].steps):
            state.pop(name, None)
            return
        group, load = units[name].steps[at][2:4]
        links, lag = COST[group.name]
        first = max([now] + [free.get(key, 0.0) for key in links])
        for key, cost in links.items():
            free[key] = first + cost * load
        state[name] = (at, max(free[key] for key in links) + lag + 0.2)

    def end(name, at, point):
        nonlocal now
        actions[point].append((name, at))
        now += 0.05 + 0.1 * units[name].steps[at][4]
        begin(name, at + 1)

    for point, cost in points:
        now += cost
        for name in sorted(state, key=lambda key: state[key][1]):
            at, ready = state[name]
            if ready <= now:
                end(name, at, point)
        for name, at_point in starts.items():
            if at_point == point:
                actions[point].append((name, -1))
                begin(name, 0)
    while state:
        name = min(state, key=lambda key: state[key][1])
        at, ready = state[name]
        now = max(now, ready)
        end(name, at, points[-1][0])
    return actions


def attention_forward(qkv, mix, lse, hot_s, mask_s, tri, krow, scores, probs, group, hook):
    tokens = qkv.shape[1]
    width = qkv.shape[0] // 3
    blocks = tokens // BLK

    def heads(step, carry):
        hook(step)
        tops = [{} for _ in range(group)]
        sums = [{} for _ in range(group)]
        rows = [pl.multiple_of((step * group + j) * 64, 64) for j in range(group)]
        for j in range(group):
            keyed = jnp.concatenate(
                [
                    qkv[pl.ds(width + rows[j], 64), :],
                    mask_s[...],
                    jnp.zeros((48, tokens), bf16),
                ],
                axis=0,
            )
            krow[j] = keyed.T
        for stage in range(group + 2):
            for i in range(blocks):
                n = (i + 1) * BLK
                at = slice(i * BLK, n)
                if stage < group:
                    j = stage
                    query = jnp.concatenate(
                        [qkv[pl.ds(rows[j], 64), at], hot_s[:, at], jnp.zeros((48, BLK), bf16)],
                        axis=0,
                    )
                    raw = dot_nn(krow[j, 0:n, :], query)
                    diagonal = raw[i * BLK :] + tri[...]
                    top = jnp.max(diagonal, axis=0, keepdims=True)
                    if i:
                        top = jnp.maximum(top, jnp.max(raw[: i * BLK], axis=0, keepdims=True))
                        scores[j % 2, i, 0 : i * BLK, :] = raw[: i * BLK]
                    scores[j % 2, i, i * BLK : n, :] = diagonal
                    tops[j][i] = top
                if 0 <= stage - 1 < group:
                    j = stage - 1
                    weights = jnp.exp2(scores[j % 2, i, 0:n, :] - tops[j][i])
                    sums[j][i] = jnp.sum(weights, axis=0, keepdims=True)
                    probs[j % 2, i, 0:n, :] = weights.astype(bf16)
                if 0 <= stage - 2 < group:
                    j = stage - 2
                    out = dot_nn(qkv[pl.ds(2 * width + rows[j], 64), 0:n], probs[j % 2, i, 0:n, :])
                    mix[pl.ds(rows[j], 64), at] = (out / sums[j][i]).astype(bf16)
                    lse[pl.ds(step * group + j, 1), at] = tops[j][i] + jnp.log2(sums[j][i])
        return carry

    lax.fori_loop(0, HEADS // group, heads, 0)


def forward_kernel(
    lens,
    block_input,
    gain,
    bias,
    qkv_bias,
    out_bias,
    up_bias,
    down_bias,
    qkv_w_h,
    out_w_h,
    up_w_h,
    down_w_h,
    block_output,
    stream_h,
    hid_h,
    qkv_h,
    mix_h,
    lse_h,
    act_h,
    slope_h,
    up_all_h,
    down_all_h,
    stream,
    hidden,
    hid,
    qkv,
    mix,
    lse,
    act,
    slope,
    qkv_w,
    out_w,
    up_w,
    down_w,
    qkv_b,
    up_b,
    pre,
    hot_s,
    mask_s,
    cos_s,
    sin_s,
    tri,
    krow,
    scores,
    probs,
    in_sem,
    out_sem,
    send_sem,
    recv_sem,
):
    tokens, width = block_input.shape
    layers = gain.shape[0]
    half = up_w.shape[3]
    blocks = tokens // BLK
    by_core, by_mlp, by_row = (Group(name, list(BITS[name])) for name in "CXY")
    own, other = by_mlp.me, by_mlp.index(1)
    barrier = pltpu.get_barrier_semaphore()
    for group in (by_core, by_mlp, by_row):
        pl.semaphore_signal(barrier, inc=1, device_id=group.device(1), device_id_type=MESH)

    moves = {}
    sems = (send_sem, recv_sem)
    for layer in range(layers):
        for k, (src, dst) in enumerate(((up_w_h, up_w), (down_w_h, down_w))):
            quarter = src.shape[1] // 4
            first = pl.multiple_of((2 * by_core.me + by_row.me) * quarter, 16)
            pair = pl.multiple_of(2 * by_core.me * quarter, 16)
            mine = dst.at[layer, own, pl.ds(first, quarter), :]
            got = dst.at[layer, other, pl.ds(first, quarter), :]
            both = dst.at[layer, other, pl.ds(pair, 2 * quarter), :]
            at = (layer * 2 + k) * 3
            moves[layer, k] = [
                Link(src.at[layer, pl.ds(first, quarter), :], mine, sems, at, by_mlp.device(1)),
                Link(got, got, sems, at + 1, by_row.device(1)),
                Link(both, both, sems, at + 2, by_core.device(1)),
            ]
    bias_link = Link(up_b.at[own], up_b.at[own], sems, layers * 6, by_mlp.device(1))

    def begin(layer, k, step):
        moves[layer, k][step].copy().start()

    def end(layer, k, step):
        copy = moves[layer, k][step].copy()
        copy.wait_send()
        copy.wait_recv()

    loads = [
        [
            pltpu.make_async_copy(src.at[layer], dst, in_sem.at[layer, k])
            for k, (src, dst) in enumerate(
                (
                    (qkv_w_h, qkv_w.at[layer]),
                    (out_w_h, out_w.at[layer]),
                    (up_w_h, up_w.at[layer, own]),
                    (down_w_h, down_w.at[layer, own]),
                )
            )
        ]
        for layer in range(layers)
    ]
    for layer in range(layers):
        for copy in loads[layer]:
            copy.start()
    up_b[own, 0:layers, :] = up_bias[...].astype(f32)
    pl.semaphore_wait(barrier, 3)
    begin(0, 0, 0)
    begin(0, 1, 0)
    bias_link.copy().start()
    hot, position = doc_tables(lens, tokens)
    zeros8 = jnp.zeros_like(hot)
    hot_s[...] = jnp.concatenate([hot, zeros8], axis=0).astype(bf16)
    mask_s[...] = jnp.concatenate([mask_rows(hot), zeros8], axis=0).astype(bf16)
    cos_s[...], sin_s[...] = rotary_tables(position)
    tri[...] = causal_bias()
    stream[...] = block_input[...].astype(f32)
    stores = []
    for layer in range(layers):
        gain_row, bias_row = row_of(gain, layer), row_of(bias, layer)
        qkv_b[...] = jnp.broadcast_to(row_of(qkv_bias, layer), (128, 3 * width)).T

        for copy in stores:
            copy.wait()
        stores = []

        def norm_block(i, carry):
            rows = pl.ds(pl.multiple_of(i * BLK, BLK), BLK)
            centred, scale = norm_stats(stream[rows, :])
            low = (centred * scale * gain_row + bias_row).astype(bf16)
            hidden[rows, :] = low
            hid[:, rows] = low.T
            return carry

        lax.fori_loop(0, blocks, norm_block, 0)
        loads[layer][0].wait()
        for part in range(3):
            cols = slice(part * width, (part + 1) * width)
            for i in range(blocks):
                at = slice(i * BLK, (i + 1) * BLK)
                value = dot_tn(qkv_w[layer, :, cols], hid[:, at])
                column = qkv_b[cols, :]
                value = value + jnp.concatenate([column] * (BLK // 128), axis=1)
                if part < 2:
                    value = rotate(value, cos_s[:, at], sin_s[:, at])
                if part == 0:
                    value = value * (64**-0.5 * LOG2E)
                qkv[cols, at] = value.astype(bf16)

        def hook(step):
            if layer == 0:

                @pl.when(step == 1)
                def _():
                    end(0, 0, 0)
                    begin(0, 0, 1)

            else:
                for at in range(2):

                    @pl.when(step == at)
                    def _():
                        end(layer, at, 0)
                        begin(layer, at, 1)

        attention_forward(
            qkv, mix, lse, hot_s, mask_s, tri, krow, scores, probs, 4, hook
        )
        if layer == 0:
            end(0, 1, 0)
            begin(0, 1, 1)
            if layers > 1:
                begin(1, 0, 0)
                begin(1, 1, 0)
        else:
            for k in range(2):
                end(layer, k, 1)
                begin(layer, k, 2)


        def save(src, dst, k):
            copy = pltpu.make_async_copy(src, dst.at[layer], out_sem.at[k])
            copy.start()
            stores.append(copy)

        save(hid, hid_h, 0)
        save(qkv, qkv_h, 1)
        save(mix, mix_h, 2)
        save(lse, lse_h, 3)
        for k in range(1, 4):
            loads[layer][k].wait()
        shift = row_of(out_bias, layer) + row_of(down_bias, layer)
        chunk = 512

        def mlp_up(x, rows):
            row = up_b[x, layer : layer + 1, :]
            for c in range(half // chunk):
                cs = slice(c * chunk, (c + 1) * chunk)
                pre[:, cs] = dot_nn(hidden[rows, :], up_w[layer, x, :, cs]) + row[:, cs]
            for c in range(half // chunk):
                cs = slice(c * chunk, (c + 1) * chunk)
                u = pre[:, cs]
                cdf = 0.5 + 0.5 * lax.erf(u * (2.0**-0.5))
                pdf = jnp.exp2(u * u * (-0.5 * LOG2E)) * ((2.0 * math.pi) ** -0.5)
                act[x, rows, cs] = (u * cdf).astype(bf16)
                slope[x, rows, cs] = (cdf + u * pdf).astype(bf16)

        def own_block(i, carry):
            rows = pl.ds(pl.multiple_of(i * BLK, BLK), BLK)
            mlp_up(own, rows)
            total = dot_tn(mix[:, rows], out_w[layer]) + dot_nn(act[own, rows, :], down_w[layer, own])
            stream[rows, :] = stream[rows, :] + (total + shift)
            return carry

        def other_up(i, carry):
            mlp_up(other, pl.ds(pl.multiple_of(i * BLK, BLK), BLK))
            return carry

        def other_down(i, carry):
            rows = pl.ds(pl.multiple_of(i * BLK, BLK), BLK)
            stream[rows, :] = stream[rows, :] + dot_nn(act[other, rows, :], down_w[layer, other])
            return carry

        lax.fori_loop(0, blocks, own_block, 0)
        if layer == 0:
            copy = bias_link.copy()
            copy.wait_send()
            copy.wait_recv()
            for k in range(2):
                end(0, k, 1)
                begin(0, k, 2)
        end(layer, 0, 2)
        lax.fori_loop(0, blocks, other_up, 0)
        save(slope, slope_h, 5)
        save(up_w.at[layer], up_all_h, 7)
        end(layer, 1, 2)
        lax.fori_loop(0, blocks, other_down, 0)
        save(down_w.at[layer], down_all_h, 8)
        save(act, act_h, 4)
        if layer + 1 < layers:
            copy = pltpu.make_async_copy(stream, stream_h, out_sem.at[6])
            copy.start()
            stores.append(copy)
    block_output[...] = stream[...].astype(bf16)
    for copy in stores:
        copy.wait()


def attention_backward(qkv, mix, grad_mix, lse, hot_s, mask_s, tri, cos_s, sin_s, work, group, hook):
    krow, vrow, qext, gext, probs, dscore = work
    tokens = qkv.shape[1]
    width = qkv.shape[0] // 3
    blocks = tokens // BLK
    ones = jnp.where(lax.broadcasted_iota(jnp.int32, (64, tokens), 0) < 3, 1.0, 0.0).astype(bf16)

    def heads(step, carry):
        hook(step, 0)
        rows = [pl.multiple_of((step * group + j) * 64, 64) for j in range(group)]
        for j in range(group):
            r = rows[j]
            keyed = jnp.concatenate(
                [qkv[pl.ds(width + r, 64), :], mask_s[...], jnp.zeros((48, tokens), bf16)], axis=0
            )
            krow[j] = keyed.T
            vrow[j] = jnp.concatenate([qkv[pl.ds(2 * width + r, 64), :], ones], axis=0).T
            grad = grad_mix[pl.ds(r, 64), :].astype(f32)
            total = jnp.sum(grad * mix[pl.ds(r, 64), :].astype(f32), axis=0, keepdims=True)
            qext[j] = jnp.concatenate(
                [
                    qkv[pl.ds(r, 64), :].astype(f32),
                    hot_s[0:4, :].astype(f32),
                    split3(-lse[pl.ds(step * group + j, 1), :]),
                    jnp.zeros((57, tokens), f32),
                ],
                axis=0,
            ).astype(bf16)
            gext[j] = jnp.concatenate(
                [grad, split3(-total), jnp.zeros((61, tokens), f32)], axis=0
            ).astype(bf16)
        for j in range(group):
            r = rows[j]
            if j:
                hook(step, j)
            for i in range(blocks):
                n = (i + 1) * BLK
                at = slice(i * BLK, n)
                raw = dot_nn(krow[j, 0:n, :], qext[j, :, at])
                if i:
                    raw = jnp.concatenate([raw[: i * BLK], raw[i * BLK :] + tri[...]], axis=0)
                else:
                    raw = raw + tri[...]
                weights = jnp.exp2(raw)
                slopes = dot_nn(vrow[j, 0:n, :], gext[j, :, at])
                dscore[0:n, at] = (weights * slopes).astype(bf16)
                probs[0:n, at] = weights.astype(bf16)
            dq, dk, dv = [], [], []
            for i in range(blocks):
                n = (i + 1) * BLK
                at = slice(i * BLK, n)
                dq.append(dot_nn(qkv[pl.ds(width + r, 64), 0:n], dscore[0:n, at]))
                dk.append(dot_nt(qkv[pl.ds(r, 64), i * BLK :], dscore[at, i * BLK :]))
                dv.append(dot_nt(grad_mix[pl.ds(r, 64), i * BLK :], probs[at, i * BLK :]))
            dq = jnp.concatenate(dq, axis=1) * 64**-0.5
            dk = jnp.concatenate(dk, axis=1) * LN2
            qkv[pl.ds(r, 64), :] = rotate(dq, cos_s[...], -sin_s[...]).astype(bf16)
            qkv[pl.ds(width + r, 64), :] = rotate(dk, cos_s[...], -sin_s[...]).astype(bf16)
            qkv[pl.ds(2 * width + r, 64), :] = jnp.concatenate(dv, axis=1).astype(bf16)
        return carry

    lax.fori_loop(0, HEADS // group, heads, 0)


def backward_kernel(
    pairs,
    lens,
    gain,
    block_input,
    out_grad,
    qkv_w_h,
    out_w_h,
    up_w_h,
    down_w_h,
    stream_h,
    hid_h,
    qkv_h,
    mix_h,
    lse_h,
    act_h,
    slope_h,
    input_grad,
    mlp_out,
    att_out,
    vec_out,
    stream,
    grad_low,
    grad_mix,
    hid,
    qkv,
    mix,
    lse,
    act,
    slope,
    qkv_w,
    out_w,
    up_w,
    down_w,
    hot_s,
    mask_s,
    cos_s,
    sin_s,
    tri,
    krow,
    vrow,
    qext,
    gext,
    probs,
    dscore,
    mlp_grad,
    att_grad,
    vec_grad,
    mlp_core,
    att_core,
    mlp_recv,
    att_recv,
    vec_recv,
    in_sem,
    out_sem,
    send_sem,
    recv_sem,
):
    tokens, width = grad_low.shape
    layers = gain.shape[0]
    half = up_w.shape[2]
    units = 2 * half
    blocks = tokens // BLK
    last = layers - 1
    grad = input_grad
    split = pairs <= 4

    def load(src, dst, layer, k):
        copy = pltpu.make_async_copy(src, dst, in_sem.at[layer, k])
        copy.start()
        return copy

    loads = {
        "act": lambda l: load(act_h.at[l], act, l, 0),
        "slope": lambda l: load(slope_h.at[l], slope, l, 1),
        "down": lambda l: load(down_w_h.at[l], down_w, l, 2),
        "up": lambda l: load(up_w_h.at[l], up_w, l, 3),
        "hid": lambda l: load(hid_h.at[l], hid.at[0:width, :], l, 4),
        "qkv": lambda l: load(qkv_h.at[l], qkv, l, 5),
        "mix": lambda l: load(mix_h.at[l], mix, l, 6),
        "lse": lambda l: load(lse_h.at[l], lse, l, 7),
        "out_w": lambda l: load(out_w_h.at[l], out_w, l, 8),
        "qkv_w": lambda l: load(qkv_w_h.at[l], qkv_w, l, 9),
    }
    first_load = load(out_grad, grad_low, 0, 10)
    flight = {}
    for name in ("act", "slope", "down", "up", "hid", "out_w", "mix", "qkv", "lse", "qkv_w"):
        flight[name] = loads[name](last)
    stream_load = load(stream_h, stream, 1, 10)

    sems = (send_sem, recv_sem)
    core = Group("C", list(BITS["C"]))
    here, there = core.me, core.index(1)
    met, used_sems, travel, swaps = {}, [0], {}, {}

    def meet(groups):
        for group in groups:
            for k in group.others():
                met[tuple(b for b, f in zip(group.bits, group.flips(k)) if f)] = (group, k)
        return groups

    def add(name, kind, *rest):
        travel[name] = kind(sems, used_sems[0], *rest)
        used_sems[0] += travel[name].count

    def swap(name, src, dst):
        swaps[name] = Link(src, dst, sems, used_sems[0], core.device(1))
        used_sems[0] += 1

    meet([core])
    hh, hw = half // 2, width // 2
    att_rows = 4 * width
    pieces = {
        "out": (0, width, 0, hw),
        "a": (width, 5 * hw, 0, hw),
        "b": (5 * hw, att_rows, 0, hw // 2),
        "c": (5 * hw, att_rows, hw // 2, hw),
    }
    whole = {"c": (0, att_rows, 0, hw)}
    starts = {}
    for layer in reversed(range(layers)):
        tag = "_" + str(layer)

        def stages(name):
            return meet(groups_of(ORDERS[name + tag], pairs))

        for kind, name in enumerate(("up", "down")):
            for x in range(2):
                swap(
                    (name, x, layer),
                    mlp_grad.at[layer, x, pl.ds(pl.multiple_of(kind * half + there * hh, 16), hh), :],
                    mlp_core.at[layer, kind, x],
                )
            subs = 2 if split else 1
            for sub in range(subs):
                count = hh // subs
                add(
                    name + str(sub) + tag,
                    Unit,
                    mlp_grad.at[layer],
                    pl.multiple_of(kind * half + here * hh + sub * count, 16),
                    count,
                    mlp_recv.at[layer, kind, sub],
                    stages(name + str(sub)),
                    core,
                    mlp_out.at[layer],
                    out_sem.at[layer, kind * 2 + sub],
                )
                starts[name + str(sub) + tag] = name + "3" + tag
        for name, (a, b, lo, hi) in pieces.items():
            swap(
                (name, layer),
                att_grad.at[
                    layer, pl.ds(pl.multiple_of(there * att_rows + a, 16), b - a), lo:hi
                ],
                att_core.at[layer, a:b, lo:hi],
            )
        for k, (name, (a, b, lo, hi)) in enumerate((pieces if split else whole).items()):
            add(
                name + tag,
                Unit,
                att_grad.at[layer, :, lo:hi],
                pl.multiple_of(here * att_rows + a, 16),
                b - a,
                att_recv.at[layer, a:b, lo:hi],
                stages(name),
                core,
                att_out.at[layer, :, lo:hi],
                out_sem.at[layer, 4 + k],
            )
            starts[name + tag] = {"out": "out", "a": "head2_1", "b": "head3_1", "c": "att"}[name] + tag
        add(
            "vec" + tag,
            Vector,
            vec_grad.at[layer],
            vec_recv.at[layer],
            [core] + stages("vec"),
        )
        starts["vec" + tag] = "norm%d" % (blocks - 1) + tag

    barrier = pltpu.get_barrier_semaphore()
    for group, k in met.values():
        pl.semaphore_signal(barrier, inc=1, device_id=group.device(k), device_id_type=MESH)

    points = [("start", 4.0)]
    for layer in reversed(range(layers)):
        tag = "_" + str(layer)
        points += [("down%d" % c + tag, 1.32 if c == 2 else 0.825) for c in range(4)]
        points += [("out" + tag, 0.55)]
        points += [("mlp%d" % i + tag, 1.1) for i in range(blocks)]
        points += [("up0" + tag, 0.825), ("up1" + tag, 0.825), ("mix" + tag, 0.99)]
        points += [("up2" + tag, 0.825), ("up3" + tag, 0.825)]
        for i in range(HEADS // 2):
            extra = {2: 0.6, 3: 0.5}.get(i, 0.0)
            points += [("head%d_0" % i + tag, 2.035 + extra if i else 0.33)]
            points += [("head%d_1" % i + tag, 1.925 + extra)]
        points += [("att" + tag, 3.3)]
        points += [("norm%d" % i + tag, 1.375) for i in range(blocks)]
    actions = plan(points, starts, travel)

    def run(name):
        for unit, at in actions[name]:
            travel[unit].advance(at)

    def run_at(step, count, name):
        for i in range(count):
            if actions[name % i]:

                @pl.when(step == i)
                def _():
                    run(name % i)

    hot, position = doc_tables(lens, tokens)
    zeros8 = jnp.zeros_like(hot)
    hot_s[...] = jnp.concatenate([hot, zeros8], axis=0).astype(bf16)
    mask_s[...] = jnp.concatenate([mask_rows(hot), zeros8], axis=0).astype(bf16)
    cos_s[...], sin_s[...] = rotary_tables(position)
    tri[...] = causal_bias()
    hid[width : width + 16, :] = jnp.ones((16, tokens), bf16)
    first_load.wait()
    grad[...] = grad_low[...].astype(f32)
    pl.semaphore_wait(barrier, len(met))
    run("start")

    for layer in reversed(range(layers)):

        def ahead(*names):
            if layer:
                for name in names:
                    flight[name] = loads[name](layer - 1)

        tag = "_" + str(layer)

        def join(value, own, name, target, rows, received):
            if own:
                swaps[name].wait()
                target[rows, :] = (value + received[...].astype(f32)).astype(bf16)
            else:
                target[rows, :] = value.astype(bf16)
                swaps[name].start()

        def down_grads(own, x):
            at = pl.multiple_of((here if own else there) * hh, 256)
            join(
                dot_tn(act[x, :, pl.ds(at, hh)], grad_low[...]),
                own,
                ("down", x, layer),
                mlp_grad.at[layer, x],
                pl.ds(pl.multiple_of(half + at, 256), hh),
                mlp_core.at[layer, 1, x],
            )

        def out_grads(own):
            side = here if own else there
            value = dot_nn(mix[pl.ds(pl.multiple_of(side * hw, 256), hw), :], grad_low[...])
            join(
                jnp.concatenate([value[:, :hw], value[:, hw:]], axis=0),
                own,
                ("out", layer),
                att_grad.at[layer],
                pl.ds(pl.multiple_of(side * att_rows, 256), width),
                att_core.at[layer, 0:width],
            )

        def up_grads(own, x):
            side = here if own else there
            at = pl.multiple_of(side * hh, 256)
            up = dot_nn(hid[...], slope[x, :, pl.ds(at, hh)])
            vec_grad[layer, 0, pl.ds(6 + 2 * x + side, 1), :] = up[width : width + 1]
            join(
                up[:width],
                own,
                ("up", x, layer),
                mlp_grad.at[layer, x],
                pl.ds(at, hh),
                mlp_core.at[layer, 0, x],
            )

        flight["act"].wait()
        down_grads(False, 0)
        run("down0" + tag)
        down_grads(False, 1)
        run("down1" + tag)
        flight["mix"].wait()
        out_grads(False)
        down_grads(True, 0)
        run("down2" + tag)
        down_grads(True, 1)
        run("down3" + tag)
        ahead("act")
        out_grads(True)
        run("out" + tag)
        for name in ("slope", "down"):
            flight[name].wait()

        def mlp_block(i, carry):
            rows = pl.ds(pl.multiple_of(i * BLK, BLK), BLK)
            for c in range(units // 512):
                x, at = divmod(c * 512, half)
                cs = slice(at, at + 512)
                da = dot_nt(grad_low[rows, :], down_w[x, cs, :])
                slope[x, rows, cs] = (slope[x, rows, cs].astype(f32) * da).astype(bf16)
            run_at(i, blocks, "mlp%d" + tag)
            return carry

        lax.fori_loop(0, blocks, mlp_block, 0)
        ahead("down")
        flight["hid"].wait()
        up_grads(False, 0)
        run("up0" + tag)
        up_grads(False, 1)
        run("up1" + tag)
        for name in ("out_w", "qkv", "lse"):
            flight[name].wait()
        vec_grad[layer, 0, 5:6, :] = jnp.sum(grad_low[...].astype(f32), axis=0, keepdims=True)
        grad_mix[...] = dot_nt(out_w[...], grad_low[...]).astype(bf16)
        run("mix" + tag)
        ahead("out_w")
        if layer == 0:
            input_load = load(block_input, grad_low, 0, 11)
        up_grads(True, 0)
        run("up2" + tag)
        up_grads(True, 1)
        run("up3" + tag)

        heads_of = {"a": (0, hw), "b": (hw, 3 * hw // 2), "c": (3 * hw // 2, width)}

        def qkv_part(name, part):
            first, last = heads_of[name]
            return qkv[part * width + first : part * width + last, :]

        def qkv_grads(name, own):
            a, b, first, last = pieces[name]
            side = here if own else there
            left = hid[pl.ds(pl.multiple_of(side * hw, 256), hw), :]
            join(
                jnp.concatenate([dot_nt(left, qkv_part(name, part)) for part in range(3)], axis=0),
                own,
                (name, layer),
                att_grad.at[layer, :, first:last],
                pl.ds(pl.multiple_of(side * att_rows + a, 256), b - a),
                att_core.at[layer, a:b, first:last],
            )

        def qkv_sums(name):
            first, last = heads_of[name]
            for part in range(3):
                total = dot_nt(hid[width : width + 16, :], qkv_part(name, part))
                vec_grad[layer, 0, 2 + part : 3 + part, first:last] = total[:1]

        def head_hook(step, j):
            for at, name in ((2, "a"), (3, "b")):

                @pl.when(step == at)
                def _():
                    qkv_grads(name, j > 0)

            run_at(step, HEADS // 2, "head%d_" + str(j) + tag)

        attention_backward(
            qkv,
            mix,
            grad_mix,
            lse,
            hot_s,
            mask_s,
            tri,
            cos_s,
            sin_s,
            (krow, vrow, qext, gext, probs, dscore),
            2,
            head_hook,
        )
        qkv_grads("c", False)
        for name in heads_of:
            qkv_sums(name)
        qkv_grads("c", True)
        run("att" + tag)
        ahead("hid", "mix", "lse")
        flight["up"].wait()
        flight["qkv_w"].wait()
        if layer == last:
            stream_load.wait()
        if layer == 0:
            input_load.wait()
        gain_row = row_of(gain, layer)
        vec_grad[layer, 0, 0:2, :] = jnp.zeros((2, width), f32)
        vec_grad[layer, 0, 10:16, :] = jnp.zeros((6, width), f32)

        def norm_block(i, carry):
            rows = pl.ds(pl.multiple_of(i * BLK, BLK), BLK)
            back = lax.dot_general(
                qkv[:, rows], qkv_w[...], (((0,), (1,)), ((), ())), preferred_element_type=f32
            )
            dh = back + (dot_nt(slope[0, rows, :], up_w[0]) + dot_nt(slope[1, rows, :], up_w[1]))
            if layer:
                centred, scale = norm_stats(stream[rows, :])
            else:
                centred, scale = norm_stats(grad_low[rows, :].astype(f32))
            n = centred * scale
            product = dh * n
            vec_grad[layer, 0, 0:1, :] += jnp.sum(product, axis=0, keepdims=True)
            vec_grad[layer, 0, 1:2, :] += jnp.sum(dh, axis=0, keepdims=True)
            e = dh * gain_row
            mean_e = jnp.mean(e, axis=-1, keepdims=True)
            mean_en = jnp.mean(product * gain_row, axis=-1, keepdims=True)
            total = grad[rows, :] + scale * (e - mean_e - n * mean_en)
            grad[rows, :] = total
            if layer:
                grad_low[rows, :] = total.astype(bf16)
            run_at(i, blocks, "norm%d" + tag)
            return carry

        lax.fori_loop(0, blocks, norm_block, 0)
        ahead("slope", "up", "qkv", "qkv_w")
    mine = lax.axis_index("mlp")
    for layer in range(layers):
        done = len(travel["vec_" + str(layer)].steps)
        total = vec_grad[layer, done]
        vec_out[layer] = total
        vec_out[layer, 6:8, :] = jnp.where(mine == 0, total[6:8], total[8:10])


VMEM = pl.BlockSpec(memory_space=pltpu.VMEM)
SMEM = pl.BlockSpec(memory_space=pltpu.SMEM)
ANY = pl.BlockSpec(memory_space=pl.ANY)


def run_forward(lens, block_input, gain, bias, qkv_b, out_b, up_b, down_b, qkv_w, out_w, up_w, down_w):
    tokens, width = block_input.shape
    layers = gain.shape[0]
    half = up_w.shape[2]
    shape = jax.ShapeDtypeStruct
    v = pltpu.VMEM
    return pl.pallas_call(
        forward_kernel,
        out_shape=(
            shape((tokens, width), bf16),
            shape((tokens, width), f32),
            shape((layers, width, tokens), bf16),
            shape((layers, 3 * width, tokens), bf16),
            shape((layers, width, tokens), bf16),
            shape((layers, HEADS, tokens), f32),
            shape((layers, 2, tokens, half), bf16),
            shape((layers, 2, tokens, half), bf16),
            shape((layers, 2, width, half), bf16),
            shape((layers, 2, half, width), bf16),
        ),
        in_specs=[SMEM] + [VMEM] * 7 + [ANY] * 4,
        out_specs=(VMEM,) + (ANY,) * 9,
        scratch_shapes=[
            v((tokens, width), f32),
            v((tokens, width), bf16),
            v((width, tokens), bf16),
            v((3 * width, tokens), bf16),
            v((width, tokens), bf16),
            v((HEADS, tokens), f32),
            v((2, tokens, half), bf16),
            v((2, tokens, half), bf16),
            v((layers, width, 3 * width), bf16),
            v((layers, width, width), bf16),
            v((layers, 2, width, half), bf16),
            v((layers, 2, half, width), bf16),
            v((3 * width, 128), f32),
            v((2, 8, half), f32),
            v((BLK, half), f32),
            v((16, tokens), bf16),
            v((16, tokens), bf16),
            v((HALF, tokens), f32),
            v((HALF, tokens), f32),
            v((BLK, BLK), f32),
            v((4, tokens, 128), bf16),
            v((2, tokens // BLK, tokens, BLK), f32),
            v((2, tokens // BLK, tokens, BLK), bf16),
            pltpu.SemaphoreType.DMA((layers, 4)),
            pltpu.SemaphoreType.DMA((9,)),
            pltpu.SemaphoreType.DMA((layers * 6 + 1,)),
            pltpu.SemaphoreType.DMA((layers * 6 + 1,)),
        ],
        compiler_params=pltpu.CompilerParams(
            vmem_limit_bytes=63 * 2**20, collective_id=1, has_side_effects=True
        ),
        name="forward",
    )(lens, block_input, gain, bias, qkv_b, out_b, up_b, down_b, qkv_w, out_w, up_w, down_w)


def run_backward(lens, block_input, out_grad, gain, qkv_w, out_w, up_w, down_w, saved):
    tokens, width = block_input.shape
    layers = gain.shape[0]
    half = up_w.shape[3]
    units = 2 * half
    shape = jax.ShapeDtypeStruct
    v = pltpu.VMEM
    pairs = lax.axis_size("dp").bit_length() - 1
    subs = 2 if pairs <= 4 else 1
    n_sems = 240
    return pl.pallas_call(
        functools.partial(backward_kernel, pairs),
        out_shape=(
            shape((tokens, width), f32),
            shape((layers, units, width), bf16),
            shape((layers, 8 * width, width // 2), bf16),
            shape((layers, 16, width), f32),
        ),
        in_specs=[SMEM, VMEM] + [ANY] * 13,
        out_specs=(VMEM, ANY, ANY, VMEM),
        scratch_shapes=[
            v((tokens, width), f32),
            v((tokens, width), bf16),
            v((width, tokens), bf16),
            v((width + 16, tokens), bf16),
            v((3 * width, tokens), bf16),
            v((width, tokens), bf16),
            v((HEADS, tokens), f32),
            v((2, tokens, half), bf16),
            v((2, tokens, half), bf16),
            v((width, 3 * width), bf16),
            v((width, width), bf16),
            v((2, width, half), bf16),
            v((2, half, width), bf16),
            v((16, tokens), bf16),
            v((16, tokens), bf16),
            v((HALF, tokens), f32),
            v((HALF, tokens), f32),
            v((BLK, BLK), f32),
            v((2, tokens, 128), bf16),
            v((2, tokens, 128), bf16),
            v((2, 128, tokens), bf16),
            v((2, 128, tokens), bf16),
            v((tokens, tokens), bf16),
            v((tokens, tokens), bf16),
            v((layers, 2, units, width), bf16),
            v((layers, 8 * width, width // 2), bf16),
            v((layers, 8, 16, width), f32),
            v((layers, 2, 2, half // 2, width), bf16),
            v((layers, 4 * width, width // 2), bf16),
            v((layers, 2, subs, half // subs, width), bf16),
            v((layers, 4 * width, width // 2), bf16),
            v((layers, 16, 16, width), f32),
            pltpu.SemaphoreType.DMA((layers, 12)),
            pltpu.SemaphoreType.DMA((layers, 8)),
            pltpu.SemaphoreType.DMA((n_sems,)),
            pltpu.SemaphoreType.DMA((n_sems,)),
        ],
        compiler_params=pltpu.CompilerParams(
            vmem_limit_bytes=63 * 2**20, collective_id=0, has_side_effects=True
        ),
        name="backward",
    )(lens, gain, block_input, out_grad, qkv_w, out_w, up_w, down_w, *saved)


def body(
    block_input,
    doc_lengths,
    norm_gain,
    norm_bias,
    qkv_weight,
    qkv_bias,
    out_weight,
    out_bias,
    up_weight,
    up_bias,
    down_weight,
    down_bias,
    out_grad,
):
    layers, width = norm_gain.shape
    block_output, *saved, up_all, down_all = run_forward(
        doc_lengths,
        block_input,
        norm_gain,
        norm_bias,
        qkv_bias,
        out_bias,
        up_bias,
        down_bias,
        qkv_weight,
        out_weight,
        up_weight,
        down_weight,
    )
    input_grad, mlp_grad, att_grad, vec_grad = run_backward(
        doc_lengths,
        block_input,
        out_grad,
        norm_gain,
        qkv_weight,
        out_weight,
        up_all,
        down_all,
        saved,
    )
    return finish(block_output, input_grad, mlp_grad, att_grad, vec_grad)


def finish_kernel(
    vec,
    block_output,
    input_grad,
    mlp_low,
    att_low,
    block_out,
    input_out,
    gain_out,
    bias_out,
    qkv_out,
    qkv_b_out,
    out_w_out,
    out_b_out,
    up_out,
    up_b_out,
    down_out,
    down_b_out,
    mlp_s,
    att_s,
    qkv_s,
    out_w_s,
    up_s,
    down_s,
    block_s,
    input_s,
    in_sem,
    out_sem,
    pass_sem,
):
    layers, units, width = mlp_low.shape
    half, hw = units // 2, width // 2
    rows = 4 * width
    count = [0]

    def store(src, dst):
        copy = pltpu.make_async_copy(src, dst, out_sem.at[count[0]])
        count[0] += 1
        copy.start()
        return copy

    loads = []
    for layer in range(layers):
        for k, (src, dst) in enumerate(((mlp_low, mlp_s), (att_low, att_s))):
            for part in range(2):
                size = src.shape[1] // 2
                at = pl.ds(part * size, size)
                copy = pltpu.make_async_copy(
                    src.at[layer, at, :], dst.at[layer, at, :], in_sem.at[layer, k, part]
                )
                copy.start()
                loads.append(copy)
    passed = []
    for k, (src, dst) in enumerate(((block_output, block_s), (input_grad, input_s))):
        copy = pltpu.make_async_copy(src, dst, pass_sem.at[k])
        copy.start()
        passed.append(copy)
    stores = []
    for layer in range(layers):
        one = slice(layer, layer + 1)
        gain_out[one, :] = vec[layer, 0:1, :]
        bias_out[one, :] = vec[layer, 1:2, :]
        for part in range(3):
            qkv_b_out[one, part * width : (part + 1) * width] = vec[layer, 2 + part : 3 + part, :]
        out_b_out[one, :] = vec[layer, 5:6, :]
        down_b_out[one, :] = vec[layer, 5:6, :]
        for part in range(half // width):
            up_b_out[one, part * width : (part + 1) * width] = vec[layer, 6 + part : 7 + part, :]
    for layer in range(layers):
        up_load, down_load, first_load, second_load = loads[4 * layer : 4 * layer + 4]
        up_load.wait()
        for c in range(half // width):
            at = slice(c * width, (c + 1) * width)
            up_s[layer, :, at] = mlp_s[layer, at, :].astype(f32)
        stores.append(store(up_s.at[layer], up_out.at[layer]))
        down_load.wait()
        down_s[layer] = mlp_s[layer, half:units, :].astype(f32)
        stores.append(store(down_s.at[layer], down_out.at[layer]))
        for side, load in enumerate((first_load, second_load)):
            load.wait()
            to = slice(side * hw, (side + 1) * hw)
            base = side * rows
            for c in range(2):
                out_w_s[layer, to, c * hw : (c + 1) * hw] = att_s[
                    layer, base + c * hw : base + (c + 1) * hw, :
                ].astype(f32)
                for part in range(3):
                    first = base + width + (c * 3 + part) * hw
                    qkv_s[layer, to, part * width + c * hw : part * width + (c + 1) * hw] = att_s[
                        layer, first : first + hw, :
                    ].astype(f32)
            stores.append(store(out_w_s.at[layer, to, :], out_w_out.at[layer, to, :]))
            stores.append(store(qkv_s.at[layer, to, :], qkv_out.at[layer, to, :]))
    for copy, src, dst in zip(passed, (block_s, input_s), (block_out, input_out)):
        copy.wait()
        stores.append(store(src, dst))
    for copy in stores:
        copy.wait()


def finish(block_output, input_grad, mlp_low, att_low, vec):
    layers, units, width = mlp_low.shape
    half = units // 2
    shape = jax.ShapeDtypeStruct
    v = pltpu.VMEM
    row = shape((layers, width), f32)
    big = {
        "qkv": (layers, width, 3 * width),
        "out": (layers, width, width),
        "up": (layers, width, half),
        "down": (layers, half, width),
    }
    return pl.pallas_call(
        finish_kernel,
        out_shape=(
            shape(block_output.shape, bf16),
            shape(input_grad.shape, f32),
            row,
            row,
            shape(big["qkv"], f32),
            shape((layers, 3 * width), f32),
            shape(big["out"], f32),
            row,
            shape(big["up"], f32),
            shape((layers, half), f32),
            shape(big["down"], f32),
            row,
        ),
        in_specs=[VMEM] + [ANY] * 4,
        out_specs=(ANY, ANY, VMEM, VMEM, ANY, VMEM, ANY, VMEM, ANY, VMEM, ANY, VMEM),
        scratch_shapes=[v(mlp_low.shape, bf16), v(att_low.shape, bf16)]
        + [v(dims, f32) for dims in big.values()]
        + [v(block_output.shape, bf16), v(input_grad.shape, f32)]
        + [
            pltpu.SemaphoreType.DMA((layers, 2, 2)),
            pltpu.SemaphoreType.DMA((2 + 6 * layers,)),
            pltpu.SemaphoreType.DMA((2,)),
        ],
        compiler_params=pltpu.CompilerParams(vmem_limit_bytes=63 * 2**20),
        name="finish",
    )(vec, block_output, input_grad, mlp_low, att_low)


def solution(mesh):
    rows = P(("dp", "mlp"), None)
    return jax.shard_map(
        body,
        mesh=mesh,
        in_specs=(
            rows,
            rows,
            P(),
            P(),
            P(),
            P(),
            P(),
            P(),
            P(None, None, "mlp"),
            P(None, "mlp"),
            P(None, "mlp", None),
            P(),
            rows,
        ),
        out_specs=(
            rows,
            rows,
            P(),
            P(),
            P(),
            P(),
            P(),
            P(),
            P(None, None, "mlp"),
            P(None, "mlp"),
            P(None, "mlp", None),
            P(),
        ),
        check_vma=False,
    )
```

```python
import functools
import math

import jax
import jax.numpy as jnp
from jax import lax
from jax.experimental import pallas as pl
from jax.experimental.pallas import tpu as pltpu
from jax.sharding import PartitionSpec as P

HEADS = 8
ROT = 16
HALF = ROT // 2
BLK = 256
norm_eps = 1e-05
rotary_base = 10000.0
bf16 = jnp.bfloat16
f32 = jnp.float32
NEG = -1e30
LOG2E = math.log2(math.e)
LN2 = math.log(2.0)


def dot_nn(a, b):
    return lax.dot_general(a, b, (((1,), (0,)), ((), ())), preferred_element_type=f32)


def dot_nt(a, b):
    return lax.dot_general(a, b, (((1,), (1,)), ((), ())), preferred_element_type=f32)


def dot_tn(a, b):
    return lax.dot_general(a, b, (((0,), (0,)), ((), ())), preferred_element_type=f32)


def row_of(ref, layer):
    return ref[...].astype(f32)[layer : layer + 1, :]


def doc_tables(lens, rows):
    lane = lax.broadcasted_iota(jnp.int32, (HALF, rows), 1)
    sub = lax.broadcasted_iota(jnp.int32, (HALF, rows), 0)
    start = jnp.int32(0)
    hot = jnp.zeros((HALF, rows), f32)
    first = jnp.zeros((HALF, rows), jnp.int32)
    for slot in range(lens.shape[1]):
        end = start + lens[0, slot]
        inside = (lane >= start) & (lane < end)
        hot = jnp.where(inside & (sub == slot), 1.0, hot)
        first = jnp.where(inside, start, first)
        start = end
    return hot, lane - first


def rotary_tables(position):
    index = lax.broadcasted_iota(jnp.int32, position.shape, 0).astype(f32)
    freqs = jnp.exp(index * (-2.0 / ROT * math.log(rotary_base)))
    angles = position.astype(f32) * freqs
    return jnp.cos(angles), jnp.sin(angles)


def rotate(values, cosines, sines):
    size = 64
    heads = values.shape[0] // size
    split = values.reshape(heads, size, values.shape[1])
    first, second, rest = split[:, :HALF], split[:, HALF:ROT], split[:, ROT:]
    turned = jnp.concatenate(
        [first * cosines - second * sines, second * cosines + first * sines, rest], axis=1
    )
    return turned.reshape(values.shape)


def mask_rows(hot):
    sub = lax.broadcasted_iota(jnp.int32, hot.shape, 0)
    rows = jnp.where(sub < 4, jnp.where(hot > 0.0, 0.0, NEG), jnp.where(sub < 7, 1.0, 0.0))
    return rows


def causal_bias():
    row = lax.broadcasted_iota(jnp.int32, (BLK, BLK), 0)
    col = lax.broadcasted_iota(jnp.int32, (BLK, BLK), 1)
    return jnp.where(row <= col, 0.0, NEG)


def norm_stats(values):
    centre = jnp.mean(values, axis=-1, keepdims=True)
    centred = values - centre
    spread = jnp.mean(centred * centred, axis=-1, keepdims=True)
    return centred, lax.rsqrt(spread + norm_eps)


def split3(value):
    a = value.astype(bf16).astype(f32)
    rest = value - a
    b = rest.astype(bf16).astype(f32)
    return jnp.concatenate([a, b, rest - b], axis=0)


MESH = pl.DeviceIdType.MESH

BITS = {
    "C": (("dp", 0),),
    "X": (("mlp", 0),),
    "Y": (("dp", 1),),
    "a": (("dp", 2),),
    "b": (("dp", 3),),
    "Z": (("dp", 2), ("dp", 3)),
    "W": (("mlp", 0), ("dp", 1)),
}
COST = {
    "C": ({"C": 1.6}, 1.1),
    "X": ({"X": 24.0}, 2.8),
    "Y": ({"Y": 24.0}, 2.6),
    "a": ({"outer": 24.0}, 2.6),
    "b": ({"middle": 48.0, "outer": 24.0}, 2.9),
    "Z": ({"middle": 96.0, "outer": 72.0}, 2.4),
    "W": ({"X": 52.0, "Y": 52.0}, 3.0),
}
ORDERS = {
    "down0_1": "YXZ",
    "down1_1": "XYZ",
    "up0_1": "YXZ",
    "up1_1": "XYZ",
    "out_1": "XYab",
    "a_1": "XYab",
    "b_1": "YXab",
    "c_1": "XYab",
    "vec_1": "XYZ",
    "down0_0": "YXZ",
    "down1_0": "XYZ",
    "up0_0": "aXYb",
    "up1_0": "XYab",
    "out_0": "aWb",
    "a_0": "XYZ",
    "b_0": "YXZ",
    "c_0": "YXZ",
    "vec_0": "WZ",
}


def groups_of(order, pairs):
    groups, left = [], set(range(1, pairs))
    for name in order:
        bits = [bit for bit in BITS[name] if bit[0] == "mlp" or bit[1] < pairs]
        left -= {bit for axis, bit in bits if axis == "dp"}
        if bits:
            groups.append(Group(name, bits))
    left = sorted(left)
    while left:
        take, left = left[:2], left[2:]
        groups.append(Group("Z", [("dp", bit) for bit in take]))
    return groups


class Group:
    def __init__(self, name, bits):
        self.name = name
        self.bits = bits
        self.size = 2 ** len(bits)
        self.values = [(lax.axis_index(axis) // 2**bit) % 2 for axis, bit in bits]
        self.me = sum(value * 2**i for i, value in enumerate(self.values))

    def flips(self, k):
        return [(k >> i) & 1 for i in range(len(self.bits))]

    def index(self, k):
        total = 0
        for i, (value, flip) in enumerate(zip(self.values, self.flips(k))):
            total = total + (1 - value if flip else value) * 2**i
        return total

    def device(self, k):
        at = {"dp": lax.axis_index("dp"), "mlp": lax.axis_index("mlp")}
        for (axis, bit), value, flip in zip(self.bits, self.values, self.flips(k)):
            if flip:
                at[axis] = at[axis] + (1 - 2 * value) * 2**bit
        return (at["dp"], at["mlp"])

    def others(self):
        return range(1, self.size)


class Link:
    def __init__(self, src, dst, sems, index, device):
        self.parts = (src, dst, sems[0].at[index], sems[1].at[index], device)

    def copy(self):
        src, dst, send, recv, device = self.parts
        return pltpu.make_async_remote_copy(
            src_ref=src,
            dst_ref=dst,
            send_sem=send,
            recv_sem=recv,
            device_id=device,
            device_id_type=MESH,
        )

    def start(self):
        self.copy().start()

    def wait(self):
        copy = self.copy()
        copy.wait_send()
        copy.wait_recv()


def add_rows(target, sources, start, count):
    step = count
    for size in (64, 48, 32, 16):
        if count % size == 0:
            step = size
            break

    def one(i, carry):
        at = pl.multiple_of(i * step, step)
        rows = pl.ds(pl.multiple_of(start + at, 16), step)
        total = target[rows, :].astype(f32)
        for source, first in sources:
            total = total + source[pl.ds(pl.multiple_of(first + at, 16), step), :].astype(f32)
        target[rows, :] = total.astype(bf16)
        return carry

    lax.fori_loop(0, count // step, one, 0)


class Unit:
    def __init__(self, sems, first_sem, grads, start, rows, recv, groups, core, out, out_sem):
        self.steps = []
        self.first_sem = first_sem
        self.count = 0
        self.sems = sems
        width = grads.shape[-1]
        mib = width * 2 / 2**20
        used = 0
        backs = [(start, rows, core)]
        mine = grads
        for group in groups:
            links, adds = [], []
            if len(mine.shape) == 3 and group.bits == [("mlp", 0)]:
                mine = grads.at[group.me]
                links.append(
                    self.link(
                        grads.at[group.index(1), pl.ds(start, rows), :],
                        recv.at[pl.ds(used, rows), :],
                        group.device(1),
                    )
                )
                adds.append((mine, [(recv, used)], start, rows))
                used += rows
                load = added = rows * mib
            else:
                part = rows // group.size
                where = [
                    pl.multiple_of(start + group.index(k) * part, 16) for k in range(group.size)
                ]
                targets = [grads.at[0], grads.at[1]] if len(mine.shape) == 3 else [mine]
                for target in targets:
                    sources = []
                    for k in group.others():
                        links.append(
                            self.link(
                                target.at[pl.ds(where[k], part), :],
                                recv.at[pl.ds(used, part), :],
                                group.device(k),
                            )
                        )
                        sources.append((recv, used))
                        used += part
                    adds.append((target, sources, where[0], part))
                load = part * mib * len(targets)
                added = load * (group.size - 1)
                start, rows = where[0], part
                backs.append((start, rows, group))
            self.steps.append((links, adds, group, load, added))
        self.reduced = len(self.steps)
        self.own = (mine.at[pl.ds(start, rows), :], out.at[pl.ds(start, rows), :], out_sem)
        source = mine
        for at, part, group in reversed(backs):
            links = [
                self.link(
                    source.at[pl.ds(at, part), :], out.at[pl.ds(at, part), :], group.device(k)
                )
                for k in group.others()
            ]
            source = out
            self.steps.append((links, [], group, part * mib, 0.0))

    def link(self, src, dst, device):
        self.count += 1
        return Link(src, dst, self.sems, self.first_sem + self.count - 1, device)

    def start(self, at):
        for link in self.steps[at][0]:
            link.copy().start()
        if at == self.reduced:
            pltpu.make_async_copy(*self.own).start()

    def end(self, at):
        links, adds = self.steps[at][:2]
        if at == self.reduced:
            pltpu.make_async_copy(*self.own).wait()
        for link in links:
            link.wait()
        for target, sources, first, count in adds:
            add_rows(target, sources, first, count)

    def advance(self, at):
        if at >= 0:
            self.end(at)
        if at + 1 < len(self.steps):
            self.start(at + 1)


class Vector(Unit):
    def __init__(self, sems, first_sem, values, recv, groups):
        self.steps = []
        self.reduced = -1
        self.first_sem = first_sem
        self.count = 0
        self.sems = sems
        self.values = values
        self.recv = recv
        self.slots = []
        used = 0
        for stage, group in enumerate(groups):
            links = [
                self.link(values.at[stage], recv.at[used + group.me], group.device(k))
                for k in group.others()
            ]
            self.slots.append((used, group))
            used += group.size
            self.steps.append((links, [], group, 0.03, 0.03))

    def start(self, at):
        used, group = self.slots[at]
        self.recv[used + group.me] = self.values[at]
        Unit.start(self, at)

    def end(self, at):
        Unit.end(self, at)
        used, group = self.slots[at]
        total = self.recv[used]
        for k in group.others():
            total = total + self.recv[used + k]
        self.values[at + 1] = total


def plan(points, starts, units):
    free, state, actions = {}, {}, {name: [] for name, _ in points}
    now = 0.0

    def begin(name, at):
        if at >= len(units[name].steps):
            state.pop(name, None)
            return
        group, load = units[name].steps[at][2:4]
        links, lag = COST[group.name]
        first = max([now] + [free.get(key, 0.0) for key in links])
        for key, cost in links.items():
            free[key] = first + cost * load
        state[name] = (at, max(free[key] for key in links) + lag + 0.2)

    def end(name, at, point):
        nonlocal now
        actions[point].append((name, at))
        now += 0.05 + 0.1 * units[name].steps[at][4]
        begin(name, at + 1)

    for point, cost in points:
        now += cost
        for name in sorted(state, key=lambda key: state[key][1]):
            at, ready = state[name]
            if ready <= now:
                end(name, at, point)
        for name, at_point in starts.items():
            if at_point == point:
                actions[point].append((name, -1))
                begin(name, 0)
    while state:
        name = min(state, key=lambda key: state[key][1])
        at, ready = state[name]
        now = max(now, ready)
        end(name, at, points[-1][0])
    return actions


def attention_forward(qkv, mix, lse, hot_s, mask_s, tri, krow, scores, probs, group, hook):
    tokens = qkv.shape[1]
    width = qkv.shape[0] // 3
    blocks = tokens // BLK

    def heads(step, carry):
        hook(step)
        tops = [{} for _ in range(group)]
        sums = [{} for _ in range(group)]
        rows = [pl.multiple_of((step * group + j) * 64, 64) for j in range(group)]
        for j in range(group):
            keyed = jnp.concatenate(
                [
                    qkv[pl.ds(width + rows[j], 64), :],
                    mask_s[...],
                    jnp.zeros((48, tokens), bf16),
                ],
                axis=0,
            )
            krow[j] = keyed.T
        for stage in range(group + 2):
            for i in range(blocks):
                n = (i + 1) * BLK
                at = slice(i * BLK, n)
                if stage < group:
                    j = stage
                    query = jnp.concatenate(
                        [qkv[pl.ds(rows[j], 64), at], hot_s[:, at], jnp.zeros((48, BLK), bf16)],
                        axis=0,
                    )
                    raw = dot_nn(krow[j, 0:n, :], query)
                    diagonal = raw[i * BLK :] + tri[...]
                    top = jnp.max(diagonal, axis=0, keepdims=True)
                    if i:
                        top = jnp.maximum(top, jnp.max(raw[: i * BLK], axis=0, keepdims=True))
                        scores[j % 2, i, 0 : i * BLK, :] = raw[: i * BLK]
                    scores[j % 2, i, i * BLK : n, :] = diagonal
                    tops[j][i] = top
                if 0 <= stage - 1 < group:
                    j = stage - 1
                    weights = jnp.exp2(scores[j % 2, i, 0:n, :] - tops[j][i])
                    sums[j][i] = jnp.sum(weights, axis=0, keepdims=True)
                    probs[j % 2, i, 0:n, :] = weights.astype(bf16)
                if 0 <= stage - 2 < group:
                    j = stage - 2
                    out = dot_nn(qkv[pl.ds(2 * width + rows[j], 64), 0:n], probs[j % 2, i, 0:n, :])
                    mix[pl.ds(rows[j], 64), at] = (out / sums[j][i]).astype(bf16)
                    lse[pl.ds(step * group + j, 1), at] = tops[j][i] + jnp.log2(sums[j][i])
        return carry

    lax.fori_loop(0, HEADS // group, heads, 0)


def forward_kernel(
    lens,
    block_input,
    gain,
    bias,
    qkv_bias,
    out_bias,
    up_bias,
    down_bias,
    qkv_w_h,
    out_w_h,
    up_w_h,
    down_w_h,
    stream_h,
    hid_h,
    qkv_h,
    mix_h,
    lse_h,
    act_h,
    slope_h,
    up_all_h,
    down_all_h,
    stream,
    hidden,
    hid,
    qkv,
    mix,
    lse,
    act,
    slope,
    qkv_w,
    out_w,
    up_w,
    down_w,
    qkv_b,
    up_b,
    pre,
    hot_s,
    mask_s,
    cos_s,
    sin_s,
    tri,
    krow,
    scores,
    probs,
    in_sem,
    out_sem,
    send_sem,
    recv_sem,
):
    tokens, width = block_input.shape
    layers = gain.shape[0]
    half = up_w.shape[3]
    blocks = tokens // BLK
    by_core, by_mlp, by_row = (Group(name, list(BITS[name])) for name in "CXY")
    own, other = by_mlp.me, by_mlp.index(1)
    barrier = pltpu.get_barrier_semaphore()
    for group in (by_core, by_mlp, by_row):
        pl.semaphore_signal(barrier, inc=1, device_id=group.device(1), device_id_type=MESH)

    moves = {}
    sems = (send_sem, recv_sem)
    for layer in range(layers):
        for k, (src, dst) in enumerate(
            ((up_w_h, up_w), (up_w_h, up_w), (down_w_h, down_w), (down_w_h, down_w))
        ):
            part = src.shape[1] // 2
            quarter = part // 4
            pair = pl.multiple_of((k % 2) * part + 2 * by_core.me * quarter, 16)
            first = pl.multiple_of(pair + by_row.me * quarter, 16)
            mine = dst.at[layer, own, pl.ds(first, quarter), :]
            got = dst.at[layer, other, pl.ds(first, quarter), :]
            both = dst.at[layer, other, pl.ds(pair, 2 * quarter), :]
            at = (layer * 4 + k) * 3
            moves[layer, k] = [
                Link(src.at[layer, pl.ds(first, quarter), :], mine, sems, at, by_mlp.device(1)),
                Link(got, got, sems, at + 1, by_row.device(1)),
                Link(both, both, sems, at + 2, by_core.device(1)),
            ]
    bias_link = Link(up_b.at[own], up_b.at[own], sems, layers * 12, by_mlp.device(1))

    def begin(layer, k, step):
        moves[layer, k][step].copy().start()

    def end(layer, k, step):
        moves[layer, k][step].wait()

    def on(layer, k, step):
        end(layer, k, step)
        begin(layer, k, step + 1)

    loads = [
        [
            pltpu.make_async_copy(src.at[layer], dst, in_sem.at[layer, k])
            for k, (src, dst) in enumerate(
                (
                    (qkv_w_h, qkv_w.at[layer]),
                    (out_w_h, out_w.at[layer]),
                    (up_w_h, up_w.at[layer, own]),
                    (down_w_h, down_w.at[layer, own]),
                )
            )
        ]
        for layer in range(layers)
    ]
    loads[0][0].start()
    up_b[own, 0:layers, :] = up_bias[...].astype(f32)
    pl.semaphore_wait(barrier, 3)
    begin(0, 0, 0)
    bias_link.start()
    begin(0, 1, 0)
    hot, position = doc_tables(lens, tokens)
    zeros8 = jnp.zeros_like(hot)
    hot_s[...] = jnp.concatenate([hot, zeros8], axis=0).astype(bf16)
    mask_s[...] = jnp.concatenate([mask_rows(hot), zeros8], axis=0).astype(bf16)
    cos_s[...], sin_s[...] = rotary_tables(position)
    tri[...] = causal_bias()
    stream[...] = block_input[...].astype(f32)
    stores = []
    for layer in range(layers):
        gain_row, bias_row = row_of(gain, layer), row_of(bias, layer)
        qkv_b[...] = jnp.broadcast_to(row_of(qkv_bias, layer), (128, 3 * width)).T

        for copy in stores:
            copy.wait()
        stores = []

        def norm_block(i, carry):
            rows = pl.ds(pl.multiple_of(i * BLK, BLK), BLK)
            centred, scale = norm_stats(stream[rows, :])
            low = (centred * scale * gain_row + bias_row).astype(bf16)
            hidden[rows, :] = low
            hid[:, rows] = low.T
            return carry

        lax.fori_loop(0, blocks, norm_block, 0)
        loads[layer][0].wait()
        if layer == 0:
            for copy in loads[0][1:]:
                copy.start()
        for part in range(3):
            cols = slice(part * width, (part + 1) * width)
            for i in range(blocks):
                at = slice(i * BLK, (i + 1) * BLK)
                value = dot_tn(qkv_w[layer, :, cols], hid[:, at])
                column = qkv_b[cols, :]
                value = value + jnp.concatenate([column] * (BLK // 128), axis=1)
                if part < 2:
                    value = rotate(value, cos_s[:, at], sin_s[:, at])
                if part == 0:
                    value = value * (64**-0.5 * LOG2E)
                qkv[cols, at] = value.astype(bf16)

        if layer:
            on(layer, 0, 0)
            on(layer, 1, 0)

        def hook(step):
            for at in range(2):

                @pl.when(step == at)
                def _():
                    if layer == 0:
                        on(0, at, 0)
                        begin(0, 2 + at, 0)
                    else:
                        on(layer, 2 + at, 0)

        attention_forward(qkv, mix, lse, hot_s, mask_s, tri, krow, scores, probs, 4, hook)
        if layer == 0:
            on(0, 2, 0)
        else:
            on(layer, 0, 1)
            on(layer, 1, 1)

        def save(src, dst, k, part=None):
            to = dst.at[layer] if part is None else dst.at[layer, part]
            copy = pltpu.make_async_copy(src, to, out_sem.at[k])
            copy.start()
            stores.append(copy)

        save(hid, hid_h, 0)
        save(qkv, qkv_h, 1)
        save(mix, mix_h, 2)
        save(lse, lse_h, 3)
        for k in range(1, 4):
            loads[layer][k].wait()
        if layer + 1 < layers:
            for copy in loads[layer + 1]:
                copy.start()
        shift = row_of(out_bias, layer) + row_of(down_bias, layer)
        chunk = 512

        def mlp_up(x, rows):
            row = up_b[x, layer : layer + 1, :]
            for c in range(half // chunk):
                cs = slice(c * chunk, (c + 1) * chunk)
                pre[:, cs] = dot_nn(hidden[rows, :], up_w[layer, x, :, cs]) + row[:, cs]
            for c in range(half // chunk):
                cs = slice(c * chunk, (c + 1) * chunk)
                u = pre[:, cs]
                cdf = 0.5 + 0.5 * lax.erf(u * (2.0**-0.5))
                pdf = jnp.exp2(u * u * (-0.5 * LOG2E)) * ((2.0 * math.pi) ** -0.5)
                act[x, rows, cs] = (u * cdf).astype(bf16)
                slope[x, rows, cs] = (cdf + u * pdf).astype(bf16)

        def own_block(i, carry):
            rows = pl.ds(pl.multiple_of(i * BLK, BLK), BLK)
            mlp_up(own, rows)
            if layer < layers - 1:
                total = dot_tn(mix[:, rows], out_w[layer]) + dot_nn(
                    act[own, rows, :], down_w[layer, own]
                )
                stream[rows, :] = stream[rows, :] + (total + shift)
            if layer == 0:

                @pl.when(i == 1)
                def _():
                    on(0, 0, 1)

                @pl.when(i == 3)
                def _():
                    on(0, 3, 0)
                    on(0, 1, 1)
                    if layers > 1:
                        begin(1, 0, 0)
                        begin(1, 1, 0)

            else:

                @pl.when(i == 2)
                def _():
                    on(layer, 2, 1)

            return carry

        def other_up(i, carry):
            mlp_up(other, pl.ds(pl.multiple_of(i * BLK, BLK), BLK))
            if layer == 0:

                @pl.when(i == 1)
                def _():
                    on(0, 2, 1)

            return carry

        def other_down(i, carry):
            rows = pl.ds(pl.multiple_of(i * BLK, BLK), BLK)
            stream[rows, :] = stream[rows, :] + dot_nn(act[other, rows, :], down_w[layer, other])
            return carry

        lax.fori_loop(0, blocks, own_block, 0)
        save(act.at[own], act_h, 4, own)
        save(slope.at[own], slope_h, 5, own)
        if layer == 0:
            bias_link.wait()
        else:
            on(layer, 3, 1)
        end(layer, 0, 2)
        end(layer, 1, 2)
        save(up_w.at[layer], up_all_h, 7)
        lax.fori_loop(0, blocks, other_up, 0)
        save(act.at[other], act_h, 9, other)
        save(slope.at[other], slope_h, 10, other)
        if layer == 0:
            on(0, 3, 1)
            if layers > 1:
                begin(1, 2, 0)
                begin(1, 3, 0)
        end(layer, 2, 2)
        end(layer, 3, 2)
        save(down_w.at[layer], down_all_h, 8)
        if layer < layers - 1:
            lax.fori_loop(0, blocks, other_down, 0)
        if layer + 1 < layers:
            copy = pltpu.make_async_copy(stream, stream_h, out_sem.at[6])
            copy.start()
            stores.append(copy)
    for copy in stores:
        copy.wait()


def attention_backward(qkv, mix, grad_mix, lse, hot_s, mask_s, tri, cos_s, sin_s, work, group, hook):
    krow, vrow, qext, gext, probs, dscore = work
    tokens = qkv.shape[1]
    width = qkv.shape[0] // 3
    blocks = tokens // BLK
    ones = jnp.where(lax.broadcasted_iota(jnp.int32, (64, tokens), 0) < 3, 1.0, 0.0).astype(bf16)

    def heads(step, carry):
        hook(step, 0)
        rows = [pl.multiple_of((step * group + j) * 64, 64) for j in range(group)]
        for j in range(group):
            r = rows[j]
            keyed = jnp.concatenate(
                [qkv[pl.ds(width + r, 64), :], mask_s[...], jnp.zeros((48, tokens), bf16)], axis=0
            )
            krow[j] = keyed.T
            vrow[j] = jnp.concatenate([qkv[pl.ds(2 * width + r, 64), :], ones], axis=0).T
            grad = grad_mix[pl.ds(r, 64), :].astype(f32)
            total = jnp.sum(grad * mix[pl.ds(r, 64), :].astype(f32), axis=0, keepdims=True)
            qext[j] = jnp.concatenate(
                [
                    qkv[pl.ds(r, 64), :].astype(f32),
                    hot_s[0:4, :].astype(f32),
                    split3(-lse[pl.ds(step * group + j, 1), :]),
                    jnp.zeros((57, tokens), f32),
                ],
                axis=0,
            ).astype(bf16)
            gext[j] = jnp.concatenate(
                [grad, split3(-total), jnp.zeros((61, tokens), f32)], axis=0
            ).astype(bf16)
        for j in range(group):
            r = rows[j]
            if j:
                hook(step, j)
            for i in range(blocks):
                n = (i + 1) * BLK
                at = slice(i * BLK, n)
                raw = dot_nn(krow[j, 0:n, :], qext[j, :, at])
                if i:
                    raw = jnp.concatenate([raw[: i * BLK], raw[i * BLK :] + tri[...]], axis=0)
                else:
                    raw = raw + tri[...]
                weights = jnp.exp2(raw)
                slopes = dot_nn(vrow[j, 0:n, :], gext[j, :, at])
                dscore[0:n, at] = (weights * slopes).astype(bf16)
                probs[0:n, at] = weights.astype(bf16)
            dq, dk, dv = [], [], []
            for i in range(blocks):
                n = (i + 1) * BLK
                at = slice(i * BLK, n)
                dq.append(dot_nn(qkv[pl.ds(width + r, 64), 0:n], dscore[0:n, at]))
                dk.append(dot_nt(qkv[pl.ds(r, 64), i * BLK :], dscore[at, i * BLK :]))
                dv.append(dot_nt(grad_mix[pl.ds(r, 64), i * BLK :], probs[at, i * BLK :]))
            dq = jnp.concatenate(dq, axis=1) * 64**-0.5
            dk = jnp.concatenate(dk, axis=1) * LN2
            qkv[pl.ds(r, 64), :] = rotate(dq, cos_s[...], -sin_s[...]).astype(bf16)
            qkv[pl.ds(width + r, 64), :] = rotate(dk, cos_s[...], -sin_s[...]).astype(bf16)
            qkv[pl.ds(2 * width + r, 64), :] = jnp.concatenate(dv, axis=1).astype(bf16)
        return carry

    lax.fori_loop(0, HEADS // group, heads, 0)


def backward_kernel(
    pairs,
    lens,
    gain,
    out_bias,
    down_bias,
    block_input,
    out_grad,
    qkv_w_h,
    out_w_h,
    up_w_h,
    down_w_h,
    stream_h,
    hid_h,
    qkv_h,
    mix_h,
    lse_h,
    act_h,
    slope_h,
    block_output,
    input_grad,
    mlp_out,
    att_out,
    vec_out,
    stream,
    grad_low,
    grad_mix,
    hid,
    qkv,
    mix,
    lse,
    act,
    slope,
    qkv_w,
    out_w,
    up_w,
    down_w,
    hot_s,
    mask_s,
    cos_s,
    sin_s,
    tri,
    krow,
    vrow,
    qext,
    gext,
    probs,
    dscore,
    mlp_grad,
    att_grad,
    vec_grad,
    mlp_core,
    att_core,
    mlp_recv,
    att_recv,
    vec_recv,
    in_sem,
    out_sem,
    send_sem,
    recv_sem,
):
    tokens, width = grad_low.shape
    layers = gain.shape[0]
    half = up_w.shape[2]
    units = 2 * half
    blocks = tokens // BLK
    last = layers - 1
    grad = input_grad
    split = pairs <= 4

    def load(src, dst, layer, k):
        copy = pltpu.make_async_copy(src, dst, in_sem.at[layer, k])
        copy.start()
        return copy

    loads = {
        "act": lambda l: load(act_h.at[l], act, l, 0),
        "slope": lambda l: load(slope_h.at[l], slope, l, 1),
        "down": lambda l: load(down_w_h.at[l], down_w, l, 2),
        "up": lambda l: load(up_w_h.at[l], up_w, l, 3),
        "hid": lambda l: load(hid_h.at[l], hid.at[0:width, :], l, 4),
        "qkv": lambda l: load(qkv_h.at[l], qkv, l, 5),
        "mix": lambda l: load(mix_h.at[l], mix, l, 6),
        "lse": lambda l: load(lse_h.at[l], lse, l, 7),
        "out_w": lambda l: load(out_w_h.at[l], out_w, l, 8),
        "qkv_w": lambda l: load(qkv_w_h.at[l], qkv_w, l, 9),
    }
    first_load = load(out_grad, grad_low, 0, 10)
    flight = {}
    flight["act"] = loads["act"](last)
    flight["mix"] = loads["mix"](last)

    sems = (send_sem, recv_sem)
    core = Group("C", list(BITS["C"]))
    here, there = core.me, core.index(1)
    met, used_sems, travel, swaps = {}, [0], {}, {}

    def meet(groups):
        for group in groups:
            for k in group.others():
                met[tuple(b for b, f in zip(group.bits, group.flips(k)) if f)] = (group, k)
        return groups

    def add(name, kind, *rest):
        travel[name] = kind(sems, used_sems[0], *rest)
        used_sems[0] += travel[name].count

    def swap(name, src, dst):
        swaps[name] = Link(src, dst, sems, used_sems[0], core.device(1))
        used_sems[0] += 1

    meet([core])
    hh, hw = half // 2, width // 2
    att_rows = 4 * width
    pieces = {
        "out": (0, width, 0, hw),
        "a": (width, 5 * hw, 0, hw),
        "b": (5 * hw, att_rows, 0, hw // 2),
        "c": (5 * hw, att_rows, hw // 2, hw),
    }
    whole = {"c": (0, att_rows, 0, hw)}
    starts = {}
    for layer in reversed(range(layers)):
        tag = "_" + str(layer)

        def stages(name):
            return meet(groups_of(ORDERS[name + tag], pairs))

        for kind, name in enumerate(("up", "down")):
            for x in range(2):
                swap(
                    (name, x, layer),
                    mlp_grad.at[layer, x, pl.ds(pl.multiple_of(kind * half + there * hh, 16), hh), :],
                    mlp_core.at[layer, kind, x],
                )
            subs = 2 if split else 1
            for sub in range(subs):
                count = hh // subs
                add(
                    name + str(sub) + tag,
                    Unit,
                    mlp_grad.at[layer],
                    pl.multiple_of(kind * half + here * hh + sub * count, 16),
                    count,
                    mlp_recv.at[layer, kind, sub],
                    stages(name + str(sub)),
                    core,
                    mlp_out.at[layer],
                    out_sem.at[layer, kind * 2 + sub],
                )
                starts[name + str(sub) + tag] = name + "3" + tag
        for name, (a, b, lo, hi) in pieces.items():
            swap(
                (name, layer),
                att_grad.at[
                    layer, pl.ds(pl.multiple_of(there * att_rows + a, 16), b - a), lo:hi
                ],
                att_core.at[layer, a:b, lo:hi],
            )
        for k, (name, (a, b, lo, hi)) in enumerate((pieces if split else whole).items()):
            add(
                name + tag,
                Unit,
                att_grad.at[layer, :, lo:hi],
                pl.multiple_of(here * att_rows + a, 16),
                b - a,
                att_recv.at[layer, a:b, lo:hi],
                stages(name),
                core,
                att_out.at[layer, :, lo:hi],
                out_sem.at[layer, 4 + k],
            )
            starts[name + tag] = {"out": "out", "a": "head2_1", "b": "head3_1", "c": "att"}[name] + tag
        add(
            "vec" + tag,
            Vector,
            vec_grad.at[layer],
            vec_recv.at[layer],
            [core] + stages("vec"),
        )
        starts["vec" + tag] = "norm%d" % (blocks - 1) + tag

    barrier = pltpu.get_barrier_semaphore()
    for group, k in met.values():
        pl.semaphore_signal(barrier, inc=1, device_id=group.device(k), device_id_type=MESH)

    points = [("start", 4.0)]
    for layer in reversed(range(layers)):
        tag = "_" + str(layer)
        points += [("down%d" % c + tag, 1.32 if c == 2 else 0.825) for c in range(4)]
        points += [("out" + tag, 0.55)]
        points += [("mlp%d" % i + tag, 1.1) for i in range(blocks)]
        points += [("up0" + tag, 0.825), ("up1" + tag, 0.825), ("mix" + tag, 0.99)]
        points += [("up2" + tag, 0.825), ("up3" + tag, 0.825)]
        for i in range(HEADS // 2):
            extra = {2: 0.6, 3: 0.5}.get(i, 0.0)
            points += [("head%d_0" % i + tag, 2.035 + extra if i else 0.33)]
            points += [("head%d_1" % i + tag, 1.925 + extra)]
        points += [("att" + tag, 3.3)]
        points += [("norm%d" % i + tag, 1.375) for i in range(blocks)]
    points += [("last%d" % i, 1.0) for i in range(blocks)]
    actions = plan(points, starts, travel)

    again = {
        "act": (act_h.at[last], act),
        "down": (down_w_h.at[last], down_w),
        "out_w": (out_w_h.at[last], out_w),
        "mix": (mix_h.at[last], mix),
    }
    flight_again = []

    def run(name):
        for unit, at in actions[name]:
            travel[unit].advance(at)

    def run_at(step, count, name):
        for i in range(count):
            if actions[name % i]:

                @pl.when(step == i)
                def _():
                    run(name % i)

    hot, position = doc_tables(lens, tokens)
    zeros8 = jnp.zeros_like(hot)
    hot_s[...] = jnp.concatenate([hot, zeros8], axis=0).astype(bf16)
    mask_s[...] = jnp.concatenate([mask_rows(hot), zeros8], axis=0).astype(bf16)
    cos_s[...], sin_s[...] = rotary_tables(position)
    tri[...] = causal_bias()
    hid[width : width + 16, :] = jnp.ones((16, tokens), bf16)
    first_load.wait()
    grad[...] = grad_low[...].astype(f32)
    pl.semaphore_wait(barrier, len(met))
    run("start")

    for layer in reversed(range(layers)):

        def ahead(*names):
            for name in names:
                if layer:
                    flight[name] = loads[name](layer - 1)
                elif name in ("act", "down", "out_w", "mix"):
                    flight[name] = load(*again[name], 1, 12 + len(flight_again))
                    flight_again.append(flight[name])

        tag = "_" + str(layer)

        def join(value, own, name, target, rows, received):
            if own:
                swaps[name].wait()
                target[rows, :] = (value + received[...].astype(f32)).astype(bf16)
            else:
                target[rows, :] = value.astype(bf16)
                swaps[name].start()

        def down_grads(own, x):
            at = pl.multiple_of((here if own else there) * hh, 256)
            join(
                dot_tn(act[x, :, pl.ds(at, hh)], grad_low[...]),
                own,
                ("down", x, layer),
                mlp_grad.at[layer, x],
                pl.ds(pl.multiple_of(half + at, 256), hh),
                mlp_core.at[layer, 1, x],
            )

        def out_grads(own):
            side = here if own else there
            value = dot_nn(mix[pl.ds(pl.multiple_of(side * hw, 256), hw), :], grad_low[...])
            join(
                jnp.concatenate([value[:, :hw], value[:, hw:]], axis=0),
                own,
                ("out", layer),
                att_grad.at[layer],
                pl.ds(pl.multiple_of(side * att_rows, 256), width),
                att_core.at[layer, 0:width],
            )

        def up_grads(own, x):
            side = here if own else there
            at = pl.multiple_of(side * hh, 256)
            up = dot_nn(hid[...], slope[x, :, pl.ds(at, hh)])
            vec_grad[layer, 0, pl.ds(6 + 2 * x + side, 1), :] = up[width : width + 1]
            join(
                up[:width],
                own,
                ("up", x, layer),
                mlp_grad.at[layer, x],
                pl.ds(at, hh),
                mlp_core.at[layer, 0, x],
            )

        flight["act"].wait()
        if layer == last:
            for name in ("slope", "down", "hid", "out_w", "qkv", "lse"):
                flight[name] = loads[name](last)
        down_grads(False, 0)
        run("down0" + tag)
        down_grads(False, 1)
        run("down1" + tag)
        flight["mix"].wait()
        out_grads(False)
        down_grads(True, 0)
        run("down2" + tag)
        down_grads(True, 1)
        run("down3" + tag)
        ahead("act")
        out_grads(True)
        run("out" + tag)
        for name in ("slope", "down"):
            flight[name].wait()
        if layer == last:
            for name in ("up", "qkv_w"):
                flight[name] = loads[name](last)
            stream_load = load(stream_h, stream, 1, 10)

        def mlp_block(i, carry):
            rows = pl.ds(pl.multiple_of(i * BLK, BLK), BLK)
            for c in range(units // 512):
                x, at = divmod(c * 512, half)
                cs = slice(at, at + 512)
                da = dot_nt(grad_low[rows, :], down_w[x, cs, :])
                slope[x, rows, cs] = (slope[x, rows, cs].astype(f32) * da).astype(bf16)
            run_at(i, blocks, "mlp%d" + tag)
            return carry

        lax.fori_loop(0, blocks, mlp_block, 0)
        ahead("down")
        flight["hid"].wait()
        up_grads(False, 0)
        run("up0" + tag)
        up_grads(False, 1)
        run("up1" + tag)
        for name in ("out_w", "qkv", "lse"):
            flight[name].wait()
        vec_grad[layer, 0, 5:6, :] = jnp.sum(grad_low[...].astype(f32), axis=0, keepdims=True)
        grad_mix[...] = dot_nt(out_w[...], grad_low[...]).astype(bf16)
        run("mix" + tag)
        ahead("out_w")
        if layer == 0:
            input_load = load(block_input, grad_low, 0, 11)
        up_grads(True, 0)
        run("up2" + tag)
        up_grads(True, 1)
        run("up3" + tag)

        heads_of = {"a": (0, hw), "b": (hw, 3 * hw // 2), "c": (3 * hw // 2, width)}

        def qkv_part(name, part):
            first, last = heads_of[name]
            return qkv[part * width + first : part * width + last, :]

        def qkv_grads(name, own):
            a, b, first, last = pieces[name]
            side = here if own else there
            left = hid[pl.ds(pl.multiple_of(side * hw, 256), hw), :]
            join(
                jnp.concatenate([dot_nt(left, qkv_part(name, part)) for part in range(3)], axis=0),
                own,
                (name, layer),
                att_grad.at[layer, :, first:last],
                pl.ds(pl.multiple_of(side * att_rows + a, 256), b - a),
                att_core.at[layer, a:b, first:last],
            )

        def qkv_sums(name):
            first, last = heads_of[name]
            for part in range(3):
                total = dot_nt(hid[width : width + 16, :], qkv_part(name, part))
                vec_grad[layer, 0, 2 + part : 3 + part, first:last] = total[:1]

        def head_hook(step, j):
            for at, name in ((2, "a"), (3, "b")):

                @pl.when(step == at)
                def _():
                    qkv_grads(name, j > 0)

            run_at(step, HEADS // 2, "head%d_" + str(j) + tag)

        attention_backward(
            qkv,
            mix,
            grad_mix,
            lse,
            hot_s,
            mask_s,
            tri,
            cos_s,
            sin_s,
            (krow, vrow, qext, gext, probs, dscore),
            2,
            head_hook,
        )
        qkv_grads("c", False)
        for name in heads_of:
            qkv_sums(name)
        qkv_grads("c", True)
        run("att" + tag)
        ahead("hid", "mix", "lse")
        flight["up"].wait()
        flight["qkv_w"].wait()
        if layer == last:
            stream_load.wait()
        if layer == 0:
            input_load.wait()
        gain_row = row_of(gain, layer)
        vec_grad[layer, 0, 0:2, :] = jnp.zeros((2, width), f32)
        vec_grad[layer, 0, 10:16, :] = jnp.zeros((6, width), f32)

        def norm_block(i, carry):
            rows = pl.ds(pl.multiple_of(i * BLK, BLK), BLK)
            back = lax.dot_general(
                qkv[:, rows], qkv_w[...], (((0,), (1,)), ((), ())), preferred_element_type=f32
            )
            dh = back + (dot_nt(slope[0, rows, :], up_w[0]) + dot_nt(slope[1, rows, :], up_w[1]))
            if layer:
                centred, scale = norm_stats(stream[rows, :])
            else:
                centred, scale = norm_stats(grad_low[rows, :].astype(f32))
            n = centred * scale
            product = dh * n
            vec_grad[layer, 0, 0:1, :] += jnp.sum(product, axis=0, keepdims=True)
            vec_grad[layer, 0, 1:2, :] += jnp.sum(dh, axis=0, keepdims=True)
            e = dh * gain_row
            mean_e = jnp.mean(e, axis=-1, keepdims=True)
            mean_en = jnp.mean(product * gain_row, axis=-1, keepdims=True)
            total = grad[rows, :] + scale * (e - mean_e - n * mean_en)
            grad[rows, :] = total
            if layer:
                grad_low[rows, :] = total.astype(bf16)
            run_at(i, blocks, "norm%d" + tag)
            return carry

        lax.fori_loop(0, blocks, norm_block, 0)
        ahead("slope", "up", "qkv", "qkv_w")
    for copy in flight_again:
        copy.wait()
    shift = row_of(out_bias, last) + row_of(down_bias, last)

    def last_block(i, carry):
        rows = pl.ds(pl.multiple_of(i * BLK, BLK), BLK)
        total = dot_tn(mix[:, rows], out_w[...])
        for x in range(2):
            total = total + dot_nn(act[x, rows, :], down_w[x])
        grad_low[rows, :] = (stream[rows, :] + (total + shift)).astype(bf16)
        run_at(i, blocks - 1, "last%d")
        return carry

    lax.fori_loop(0, blocks, last_block, 0)
    result = load(grad_low, block_output, 0, 12)
    run("last%d" % (blocks - 1))
    result.wait()
    mine = lax.axis_index("mlp")
    for layer in range(layers):
        done = len(travel["vec_" + str(layer)].steps)
        total = vec_grad[layer, done]
        vec_out[layer] = total
        vec_out[layer, 6:8, :] = jnp.where(mine == 0, total[6:8], total[8:10])


VMEM = pl.BlockSpec(memory_space=pltpu.VMEM)
SMEM = pl.BlockSpec(memory_space=pltpu.SMEM)
ANY = pl.BlockSpec(memory_space=pl.ANY)


def run_forward(lens, block_input, gain, bias, qkv_b, out_b, up_b, down_b, qkv_w, out_w, up_w, down_w):
    tokens, width = block_input.shape
    layers = gain.shape[0]
    half = up_w.shape[2]
    shape = jax.ShapeDtypeStruct
    v = pltpu.VMEM
    return pl.pallas_call(
        forward_kernel,
        out_shape=(
            shape((tokens, width), f32),
            shape((layers, width, tokens), bf16),
            shape((layers, 3 * width, tokens), bf16),
            shape((layers, width, tokens), bf16),
            shape((layers, HEADS, tokens), f32),
            shape((layers, 2, tokens, half), bf16),
            shape((layers, 2, tokens, half), bf16),
            shape((layers, 2, width, half), bf16),
            shape((layers, 2, half, width), bf16),
        ),
        in_specs=[SMEM] + [VMEM] * 7 + [ANY] * 4,
        out_specs=(ANY,) * 9,
        scratch_shapes=[
            v((tokens, width), f32),
            v((tokens, width), bf16),
            v((width, tokens), bf16),
            v((3 * width, tokens), bf16),
            v((width, tokens), bf16),
            v((HEADS, tokens), f32),
            v((2, tokens, half), bf16),
            v((2, tokens, half), bf16),
            v((layers, width, 3 * width), bf16),
            v((layers, width, width), bf16),
            v((layers, 2, width, half), bf16),
            v((layers, 2, half, width), bf16),
            v((3 * width, 128), f32),
            v((2, 8, half), f32),
            v((BLK, half), f32),
            v((16, tokens), bf16),
            v((16, tokens), bf16),
            v((HALF, tokens), f32),
            v((HALF, tokens), f32),
            v((BLK, BLK), f32),
            v((4, tokens, 128), bf16),
            v((2, tokens // BLK, tokens, BLK), f32),
            v((2, tokens // BLK, tokens, BLK), bf16),
            pltpu.SemaphoreType.DMA((layers, 4)),
            pltpu.SemaphoreType.DMA((11,)),
            pltpu.SemaphoreType.DMA((layers * 12 + 1,)),
            pltpu.SemaphoreType.DMA((layers * 12 + 1,)),
        ],
        compiler_params=pltpu.CompilerParams(
            vmem_limit_bytes=63 * 2**20, collective_id=1, has_side_effects=True
        ),
        name="forward",
    )(lens, block_input, gain, bias, qkv_b, out_b, up_b, down_b, qkv_w, out_w, up_w, down_w)


def run_backward(lens, gain, out_b, down_b, block_input, out_grad, qkv_w, out_w, up_w, down_w, saved):
    tokens, width = block_input.shape
    layers = gain.shape[0]
    half = up_w.shape[3]
    units = 2 * half
    shape = jax.ShapeDtypeStruct
    v = pltpu.VMEM
    pairs = lax.axis_size("dp").bit_length() - 1
    subs = 2 if pairs <= 4 else 1
    n_sems = 240
    return pl.pallas_call(
        functools.partial(backward_kernel, pairs),
        out_shape=(
            shape((tokens, width), bf16),
            shape((tokens, width), f32),
            shape((layers, units, width), bf16),
            shape((layers, 8 * width, width // 2), bf16),
            shape((layers, 16, width), f32),
        ),
        in_specs=[SMEM] + [VMEM] * 3 + [ANY] * 13,
        out_specs=(ANY, VMEM, ANY, ANY, VMEM),
        scratch_shapes=[
            v((tokens, width), f32),
            v((tokens, width), bf16),
            v((width, tokens), bf16),
            v((width + 16, tokens), bf16),
            v((3 * width, tokens), bf16),
            v((width, tokens), bf16),
            v((HEADS, tokens), f32),
            v((2, tokens, half), bf16),
            v((2, tokens, half), bf16),
            v((width, 3 * width), bf16),
            v((width, width), bf16),
            v((2, width, half), bf16),
            v((2, half, width), bf16),
            v((16, tokens), bf16),
            v((16, tokens), bf16),
            v((HALF, tokens), f32),
            v((HALF, tokens), f32),
            v((BLK, BLK), f32),
            v((2, tokens, 128), bf16),
            v((2, tokens, 128), bf16),
            v((2, 128, tokens), bf16),
            v((2, 128, tokens), bf16),
            v((tokens, tokens), bf16),
            v((tokens, tokens), bf16),
            v((layers, 2, units, width), bf16),
            v((layers, 8 * width, width // 2), bf16),
            v((layers, 8, 16, width), f32),
            v((layers, 2, 2, half // 2, width), bf16),
            v((layers, 4 * width, width // 2), bf16),
            v((layers, 2, subs, half // subs, width), bf16),
            v((layers, 4 * width, width // 2), bf16),
            v((layers, 16, 16, width), f32),
            pltpu.SemaphoreType.DMA((layers, 16)),
            pltpu.SemaphoreType.DMA((layers, 8)),
            pltpu.SemaphoreType.DMA((n_sems,)),
            pltpu.SemaphoreType.DMA((n_sems,)),
        ],
        compiler_params=pltpu.CompilerParams(
            vmem_limit_bytes=63 * 2**20, collective_id=0, has_side_effects=True
        ),
        name="backward",
    )(lens, gain, out_b, down_b, block_input, out_grad, qkv_w, out_w, up_w, down_w, *saved)


def body(
    block_input,
    doc_lengths,
    norm_gain,
    norm_bias,
    qkv_weight,
    qkv_bias,
    out_weight,
    out_bias,
    up_weight,
    up_bias,
    down_weight,
    down_bias,
    out_grad,
):
    layers, width = norm_gain.shape
    *saved, up_all, down_all = run_forward(
        doc_lengths,
        block_input,
        norm_gain,
        norm_bias,
        qkv_bias,
        out_bias,
        up_bias,
        down_bias,
        qkv_weight,
        out_weight,
        up_weight,
        down_weight,
    )
    block_output, input_grad, mlp_grad, att_grad, vec_grad = run_backward(
        doc_lengths,
        norm_gain,
        out_bias,
        down_bias,
        block_input,
        out_grad,
        qkv_weight,
        out_weight,
        up_all,
        down_all,
        saved,
    )
    return finish(block_output, input_grad, mlp_grad, att_grad, vec_grad)


def finish_kernel(
    vec,
    block_output,
    input_grad,
    mlp_low,
    att_low,
    block_out,
    input_out,
    gain_out,
    bias_out,
    qkv_out,
    qkv_b_out,
    out_w_out,
    out_b_out,
    up_out,
    up_b_out,
    down_out,
    down_b_out,
    mlp_s,
    att_s,
    qkv_s,
    out_w_s,
    up_s,
    down_s,
    block_s,
    input_s,
    in_sem,
    out_sem,
    pass_sem,
):
    layers, units, width = mlp_low.shape
    half, hw = units // 2, width // 2
    rows = 4 * width
    count = [0]

    def store(src, dst):
        copy = pltpu.make_async_copy(src, dst, out_sem.at[count[0]])
        count[0] += 1
        copy.start()
        return copy

    loads = []
    for layer in range(layers):
        for k, (src, dst) in enumerate(((mlp_low, mlp_s), (att_low, att_s))):
            for part in range(2):
                size = src.shape[1] // 2
                at = pl.ds(part * size, size)
                copy = pltpu.make_async_copy(
                    src.at[layer, at, :], dst.at[layer, at, :], in_sem.at[layer, k, part]
                )
                copy.start()
                loads.append(copy)
    passed = []
    for k, (src, dst) in enumerate(((block_output, block_s), (input_grad, input_s))):
        copy = pltpu.make_async_copy(src, dst, pass_sem.at[k])
        copy.start()
        passed.append(copy)
    stores = []
    for layer in range(layers):
        one = slice(layer, layer + 1)
        gain_out[one, :] = vec[layer, 0:1, :]
        bias_out[one, :] = vec[layer, 1:2, :]
        for part in range(3):
            qkv_b_out[one, part * width : (part + 1) * width] = vec[layer, 2 + part : 3 + part, :]
        out_b_out[one, :] = vec[layer, 5:6, :]
        down_b_out[one, :] = vec[layer, 5:6, :]
        for part in range(half // width):
            up_b_out[one, part * width : (part + 1) * width] = vec[layer, 6 + part : 7 + part, :]
    for layer in range(layers):
        up_load, down_load, first_load, second_load = loads[4 * layer : 4 * layer + 4]
        up_load.wait()
        for c in range(half // width):
            at = slice(c * width, (c + 1) * width)
            up_s[layer, :, at] = mlp_s[layer, at, :].astype(f32)
        stores.append(store(up_s.at[layer], up_out.at[layer]))
        down_load.wait()
        down_s[layer] = mlp_s[layer, half:units, :].astype(f32)
        stores.append(store(down_s.at[layer], down_out.at[layer]))
        for side, load in enumerate((first_load, second_load)):
            load.wait()
            to = slice(side * hw, (side + 1) * hw)
            base = side * rows
            for c in range(2):
                out_w_s[layer, to, c * hw : (c + 1) * hw] = att_s[
                    layer, base + c * hw : base + (c + 1) * hw, :
                ].astype(f32)
                for part in range(3):
                    first = base + width + (c * 3 + part) * hw
                    qkv_s[layer, to, part * width + c * hw : part * width + (c + 1) * hw] = att_s[
                        layer, first : first + hw, :
                    ].astype(f32)
            stores.append(store(out_w_s.at[layer, to, :], out_w_out.at[layer, to, :]))
            stores.append(store(qkv_s.at[layer, to, :], qkv_out.at[layer, to, :]))
    for copy, src, dst in zip(passed, (block_s, input_s), (block_out, input_out)):
        copy.wait()
        stores.append(store(src, dst))
    for copy in stores:
        copy.wait()


def finish(block_output, input_grad, mlp_low, att_low, vec):
    layers, units, width = mlp_low.shape
    half = units // 2
    shape = jax.ShapeDtypeStruct
    v = pltpu.VMEM
    row = shape((layers, width), f32)
    big = {
        "qkv": (layers, width, 3 * width),
        "out": (layers, width, width),
        "up": (layers, width, half),
        "down": (layers, half, width),
    }
    return pl.pallas_call(
        finish_kernel,
        out_shape=(
            shape(block_output.shape, bf16),
            shape(input_grad.shape, f32),
            row,
            row,
            shape(big["qkv"], f32),
            shape((layers, 3 * width), f32),
            shape(big["out"], f32),
            row,
            shape(big["up"], f32),
            shape((layers, half), f32),
            shape(big["down"], f32),
            row,
        ),
        in_specs=[VMEM] + [ANY] * 4,
        out_specs=(ANY, ANY, VMEM, VMEM, ANY, VMEM, ANY, VMEM, ANY, VMEM, ANY, VMEM),
        scratch_shapes=[v(mlp_low.shape, bf16), v(att_low.shape, bf16)]
        + [v(dims, f32) for dims in big.values()]
        + [v(block_output.shape, bf16), v(input_grad.shape, f32)]
        + [
            pltpu.SemaphoreType.DMA((layers, 2, 2)),
            pltpu.SemaphoreType.DMA((2 + 6 * layers,)),
            pltpu.SemaphoreType.DMA((2,)),
        ],
        compiler_params=pltpu.CompilerParams(vmem_limit_bytes=63 * 2**20),
        name="finish",
    )(vec, block_output, input_grad, mlp_low, att_low)


def solution(mesh):
    rows = P(("dp", "mlp"), None)
    return jax.shard_map(
        body,
        mesh=mesh,
        in_specs=(
            rows,
            rows,
            P(),
            P(),
            P(),
            P(),
            P(),
            P(),
            P(None, None, "mlp"),
            P(None, "mlp"),
            P(None, "mlp", None),
            P(),
            rows,
        ),
        out_specs=(
            rows,
            rows,
            P(),
            P(),
            P(),
            P(),
            P(),
            P(),
            P(None, None, "mlp"),
            P(None, "mlp"),
            P(None, "mlp", None),
            P(),
        ),
        check_vma=False,
    )
```

```python
import functools
import math

import jax
import jax.numpy as jnp
from jax import lax
from jax.experimental import pallas as pl
from jax.experimental.pallas import tpu as pltpu
from jax.sharding import PartitionSpec as P

HEADS = 8
ROT = 16
HALF = ROT // 2
BLK = 256
norm_eps = 1e-05
rotary_base = 10000.0
bf16 = jnp.bfloat16
f32 = jnp.float32
NEG = -1e30
LOG2E = math.log2(math.e)
LN2 = math.log(2.0)
UP_OWN, UP_OTHER, DOWN_OWN, DOWN_OTHER = range(4)


def dot_nn(a, b):
    return lax.dot_general(a, b, (((1,), (0,)), ((), ())), preferred_element_type=f32)


def dot_nt(a, b):
    return lax.dot_general(a, b, (((1,), (1,)), ((), ())), preferred_element_type=f32)


def dot_tn(a, b):
    return lax.dot_general(a, b, (((0,), (0,)), ((), ())), preferred_element_type=f32)


def row_of(ref, layer):
    return ref[...].astype(f32)[layer : layer + 1, :]


def doc_tables(lens, rows):
    lane = lax.broadcasted_iota(jnp.int32, (HALF, rows), 1)
    sub = lax.broadcasted_iota(jnp.int32, (HALF, rows), 0)
    start = jnp.int32(0)
    hot = jnp.zeros((HALF, rows), f32)
    first = jnp.zeros((HALF, rows), jnp.int32)
    for slot in range(lens.shape[1]):
        end = start + lens[0, slot]
        inside = (lane >= start) & (lane < end)
        hot = jnp.where(inside & (sub == slot), 1.0, hot)
        first = jnp.where(inside, start, first)
        start = end
    return hot, lane - first


def rotary_tables(position):
    index = lax.broadcasted_iota(jnp.int32, position.shape, 0).astype(f32)
    freqs = jnp.exp(index * (-2.0 / ROT * math.log(rotary_base)))
    angles = position.astype(f32) * freqs
    return jnp.cos(angles), jnp.sin(angles)


def rotate(values, cosines, sines):
    size = 64
    heads = values.shape[0] // size
    split = values.reshape(heads, size, values.shape[1])
    first, second, rest = split[:, :HALF], split[:, HALF:ROT], split[:, ROT:]
    turned = jnp.concatenate(
        [first * cosines - second * sines, second * cosines + first * sines, rest], axis=1
    )
    return turned.reshape(values.shape)


def mask_rows(hot):
    sub = lax.broadcasted_iota(jnp.int32, hot.shape, 0)
    rows = jnp.where(sub < 4, jnp.where(hot > 0.0, 0.0, NEG), jnp.where(sub < 7, 1.0, 0.0))
    return rows


def causal_bias():
    row = lax.broadcasted_iota(jnp.int32, (BLK, BLK), 0)
    col = lax.broadcasted_iota(jnp.int32, (BLK, BLK), 1)
    return jnp.where(row <= col, 0.0, NEG)


def norm_stats(values):
    centre = jnp.mean(values, axis=-1, keepdims=True)
    centred = values - centre
    spread = jnp.mean(centred * centred, axis=-1, keepdims=True)
    return centred, lax.rsqrt(spread + norm_eps)


def split3(value):
    a = value.astype(bf16).astype(f32)
    rest = value - a
    b = rest.astype(bf16).astype(f32)
    return jnp.concatenate([a, b, rest - b], axis=0)


MESH = pl.DeviceIdType.MESH

BITS = {
    "C": (("dp", 0),),
    "X": (("mlp", 0),),
    "Y": (("dp", 1),),
    "a": (("dp", 2),),
    "b": (("dp", 3),),
    "Z": (("dp", 2), ("dp", 3)),
    "W": (("mlp", 0), ("dp", 1)),
}
COST = {
    "C": ({"C": 1.6}, 1.1),
    "X": ({"X": 24.0}, 2.8),
    "Y": ({"Y": 24.0}, 2.6),
    "a": ({"outer": 24.0}, 2.6),
    "b": ({"middle": 48.0, "outer": 24.0}, 2.9),
    "Z": ({"middle": 96.0, "outer": 72.0}, 2.4),
    "W": ({"X": 52.0, "Y": 52.0}, 3.0),
}
ORDERS = {
    "down0_1": "abXY",
    "down1_1": "aXbY",
    "down2_1": "aXbY",
    "down3_1": "YXab",
    "up0_1": "XYZ",
    "up1_1": "aYXb",
    "up2_1": "XYZ",
    "up3_1": "YXZ",
    "out_1": "WZ",
    "a_1": "XYZ",
    "b_1": "XaYb",
    "c_1": "XYZ",
    "vec_1": "XYZ",
    "down0_0": "aXYb",
    "down1_0": "YXab",
    "down2_0": "XaYb",
    "down3_0": "YXZ",
    "up0_0": "XYZ",
    "up1_0": "XYab",
    "up2_0": "YXZ",
    "up3_0": "aYXb",
    "out_0": "XYZ",
    "a_0": "WZ",
    "b_0": "WZ",
    "c_0": "WZ",
    "vec_0": "WZ",
}


def groups_of(order, pairs):
    groups, left = [], set(range(1, pairs))
    for name in order:
        bits = [bit for bit in BITS[name] if bit[0] == "mlp" or bit[1] < pairs]
        left -= {bit for axis, bit in bits if axis == "dp"}
        if bits:
            groups.append(Group(name, bits))
    left = sorted(left)
    while left:
        take, left = left[:2], left[2:]
        groups.append(Group("Z", [("dp", bit) for bit in take]))
    return groups


class Group:
    def __init__(self, name, bits):
        self.name = name
        self.bits = bits
        self.size = 2 ** len(bits)
        self.values = [(lax.axis_index(axis) // 2**bit) % 2 for axis, bit in bits]
        self.me = sum(value * 2**i for i, value in enumerate(self.values))

    def flips(self, k):
        return [(k >> i) & 1 for i in range(len(self.bits))]

    def index(self, k):
        total = 0
        for i, (value, flip) in enumerate(zip(self.values, self.flips(k))):
            total = total + (1 - value if flip else value) * 2**i
        return total

    def device(self, k):
        at = {"dp": lax.axis_index("dp"), "mlp": lax.axis_index("mlp")}
        for (axis, bit), value, flip in zip(self.bits, self.values, self.flips(k)):
            if flip:
                at[axis] = at[axis] + (1 - 2 * value) * 2**bit
        return (at["dp"], at["mlp"])

    def others(self):
        return range(1, self.size)


class Link:
    def __init__(self, src, dst, sems, index, device):
        self.parts = (src, dst, sems[0].at[index], sems[1].at[index], device)

    def copy(self):
        src, dst, send, recv, device = self.parts
        return pltpu.make_async_remote_copy(
            src_ref=src,
            dst_ref=dst,
            send_sem=send,
            recv_sem=recv,
            device_id=device,
            device_id_type=MESH,
        )

    def start(self):
        self.copy().start()

    def wait(self):
        copy = self.copy()
        copy.wait_send()
        copy.wait_recv()


def add_rows(target, sources, start, count):
    step = count
    for size in (64, 48, 32, 16):
        if count % size == 0:
            step = size
            break

    def one(i, carry):
        at = pl.multiple_of(i * step, step)
        rows = pl.ds(pl.multiple_of(start + at, 16), step)
        total = target[rows, :].astype(f32)
        for source, first in sources:
            total = total + source[pl.ds(pl.multiple_of(first + at, 16), step), :].astype(f32)
        target[rows, :] = total.astype(bf16)
        return carry

    lax.fori_loop(0, count // step, one, 0)


class Unit:
    def __init__(self, sems, first_sem, grads, start, rows, recv, groups, core, out, out_sem):
        self.steps = []
        self.first_sem = first_sem
        self.count = 0
        self.sems = sems
        width = grads.shape[-1]
        mib = width * 2 / 2**20
        used = 0
        backs = [(start, rows, core)]
        mine = grads
        for group in groups:
            links, adds = [], []
            if len(mine.shape) == 3 and group.bits == [("mlp", 0)]:
                mine = grads.at[group.me]
                links.append(
                    self.link(
                        grads.at[group.index(1), pl.ds(start, rows), :],
                        recv.at[pl.ds(used, rows), :],
                        group.device(1),
                    )
                )
                adds.append((mine, [(recv, used)], start, rows))
                used += rows
                load = added = rows * mib
            else:
                part = rows // group.size
                where = [
                    pl.multiple_of(start + group.index(k) * part, 16) for k in range(group.size)
                ]
                targets = [grads.at[0], grads.at[1]] if len(mine.shape) == 3 else [mine]
                for target in targets:
                    sources = []
                    for k in group.others():
                        links.append(
                            self.link(
                                target.at[pl.ds(where[k], part), :],
                                recv.at[pl.ds(used, part), :],
                                group.device(k),
                            )
                        )
                        sources.append((recv, used))
                        used += part
                    adds.append((target, sources, where[0], part))
                load = part * mib * len(targets)
                added = load * (group.size - 1)
                start, rows = where[0], part
                backs.append((start, rows, group))
            self.steps.append((links, adds, group, load, added))
        self.reduced = len(self.steps)
        self.own = (mine.at[pl.ds(start, rows), :], out.at[pl.ds(start, rows), :], out_sem)
        source = mine
        for at, part, group in reversed(backs):
            links = [
                self.link(
                    source.at[pl.ds(at, part), :], out.at[pl.ds(at, part), :], group.device(k)
                )
                for k in group.others()
            ]
            source = out
            self.steps.append((links, [], group, part * mib, 0.0))

    def link(self, src, dst, device):
        self.count += 1
        return Link(src, dst, self.sems, self.first_sem + self.count - 1, device)

    def start(self, at):
        for link in self.steps[at][0]:
            link.copy().start()
        if at == self.reduced:
            pltpu.make_async_copy(*self.own).start()

    def end(self, at):
        links, adds = self.steps[at][:2]
        if at == self.reduced:
            pltpu.make_async_copy(*self.own).wait()
        for link in links:
            link.wait()
        for target, sources, first, count in adds:
            add_rows(target, sources, first, count)

    def advance(self, at):
        if at >= 0:
            self.end(at)
        if at + 1 < len(self.steps):
            self.start(at + 1)


class Vector(Unit):
    def __init__(self, sems, first_sem, values, recv, groups):
        self.steps = []
        self.reduced = -1
        self.first_sem = first_sem
        self.count = 0
        self.sems = sems
        self.values = values
        self.recv = recv
        self.slots = []
        used = 0
        for stage, group in enumerate(groups):
            links = [
                self.link(values.at[stage], recv.at[used + group.me], group.device(k))
                for k in group.others()
            ]
            self.slots.append((used, group))
            used += group.size
            self.steps.append((links, [], group, 0.03, 0.03))

    def start(self, at):
        used, group = self.slots[at]
        self.recv[used + group.me] = self.values[at]
        Unit.start(self, at)

    def end(self, at):
        Unit.end(self, at)
        used, group = self.slots[at]
        total = self.recv[used]
        for k in group.others():
            total = total + self.recv[used + k]
        self.values[at + 1] = total


def plan(points, starts, units):
    free, state, actions = {}, {}, {name: [] for name, _ in points}
    now = 0.0

    def begin(name, at):
        if at >= len(units[name].steps):
            state.pop(name, None)
            return
        group, load = units[name].steps[at][2:4]
        links, lag = COST[group.name]
        first = max([now] + [free.get(key, 0.0) for key in links])
        for key, cost in links.items():
            free[key] = first + cost * load
        state[name] = (at, max(free[key] for key in links) + lag + 0.2)

    def end(name, at, point):
        nonlocal now
        actions[point].append((name, at))
        now += 0.05 + 0.1 * units[name].steps[at][4]
        begin(name, at + 1)

    for point, cost in points:
        now += cost
        for name in sorted(state, key=lambda key: state[key][1]):
            at, ready = state[name]
            if ready <= now:
                end(name, at, point)
        for name, at_point in starts.items():
            if at_point == point:
                actions[point].append((name, -1))
                begin(name, 0)
    while state:
        name = min(state, key=lambda key: state[key][1])
        at, ready = state[name]
        now = max(now, ready)
        end(name, at, points[-1][0])
    return actions


def attention_forward(qkv, mix, lse, hot_s, mask_s, tri, krow, scores, probs, group, hook):
    tokens = qkv.shape[1]
    width = qkv.shape[0] // 3
    blocks = tokens // BLK

    def heads(step, carry):
        hook(step)
        tops = [{} for _ in range(group)]
        sums = [{} for _ in range(group)]
        rows = [pl.multiple_of((step * group + j) * 64, 64) for j in range(group)]
        for j in range(group):
            keyed = jnp.concatenate(
                [
                    qkv[pl.ds(width + rows[j], 64), :],
                    mask_s[...],
                    jnp.zeros((48, tokens), bf16),
                ],
                axis=0,
            )
            krow[j][...] = keyed.T
        for stage in range(group + 2):
            for i in range(blocks):
                n = (i + 1) * BLK
                at = slice(i * BLK, n)
                first = i * (i + 1) // 2 * BLK
                if 0 <= stage - 1 < group:
                    j = stage - 1
                    weights = jnp.exp2(scores[first : first + n, :] - tops[j][i])
                    sums[j][i] = jnp.sum(weights, axis=0, keepdims=True)
                    probs[j % 2][0:n, at] = weights.astype(bf16)
                if stage < group:
                    j = stage
                    query = jnp.concatenate(
                        [qkv[pl.ds(rows[j], 64), at], hot_s[:, at], jnp.zeros((48, BLK), bf16)],
                        axis=0,
                    )
                    raw = dot_nn(krow[j][0:n, :], query)
                    diagonal = raw[i * BLK :] + tri[...]
                    top = jnp.max(diagonal, axis=0, keepdims=True)
                    if i:
                        top = jnp.maximum(top, jnp.max(raw[: i * BLK], axis=0, keepdims=True))
                        scores[first : first + i * BLK, :] = raw[: i * BLK]
                    scores[first + i * BLK : first + n, :] = diagonal
                    tops[j][i] = top
                if 0 <= stage - 2 < group:
                    j = stage - 2
                    out = dot_nn(qkv[pl.ds(2 * width + rows[j], 64), 0:n], probs[j % 2][0:n, at])
                    mix[pl.ds(rows[j], 64), at] = (out / sums[j][i]).astype(bf16)
                    lse[pl.ds(step * group + j, 1), at] = tops[j][i] + jnp.log2(sums[j][i])
        return carry

    lax.fori_loop(0, HEADS // group, heads, 0)


def attention_backward(qkv, mix, grad_mix, lse, hot_s, mask_s, tri, cos_s, sin_s, work, group, hook):
    krow, vrow, qext, gext, probs, dscore = work
    tokens = qkv.shape[1]
    width = qkv.shape[0] // 3
    blocks = tokens // BLK
    ones = jnp.where(lax.broadcasted_iota(jnp.int32, (64, tokens), 0) < 3, 1.0, 0.0).astype(bf16)

    def heads(step, carry):
        hook(step, 0)
        rows = [pl.multiple_of((step * group + j) * 64, 64) for j in range(group)]
        for j in range(group):
            r = rows[j]
            keyed = jnp.concatenate(
                [qkv[pl.ds(width + r, 64), :], mask_s[...], jnp.zeros((48, tokens), bf16)], axis=0
            )
            krow[j] = keyed.T
            vrow[j] = jnp.concatenate([qkv[pl.ds(2 * width + r, 64), :], ones], axis=0).T
            grad = grad_mix[pl.ds(r, 64), :].astype(f32)
            total = jnp.sum(grad * mix[pl.ds(r, 64), :].astype(f32), axis=0, keepdims=True)
            qext[j] = jnp.concatenate(
                [
                    qkv[pl.ds(r, 64), :].astype(f32),
                    hot_s[0:4, :].astype(f32),
                    split3(-lse[pl.ds(step * group + j, 1), :]),
                    jnp.zeros((57, tokens), f32),
                ],
                axis=0,
            ).astype(bf16)
            gext[j] = jnp.concatenate(
                [grad, split3(-total), jnp.zeros((61, tokens), f32)], axis=0
            ).astype(bf16)
        for j in range(group):
            r = rows[j]
            if j:
                hook(step, j)
            for i in range(blocks):
                n = (i + 1) * BLK
                at = slice(i * BLK, n)
                raw = dot_nn(krow[j, 0:n, :], qext[j, :, at])
                if i:
                    raw = jnp.concatenate([raw[: i * BLK], raw[i * BLK :] + tri[...]], axis=0)
                else:
                    raw = raw + tri[...]
                weights = jnp.exp2(raw)
                slopes = dot_nn(vrow[j, 0:n, :], gext[j, :, at])
                dscore[0:n, at] = (weights * slopes).astype(bf16)
                probs[0:n, at] = weights.astype(bf16)
            dq, dk, dv = [], [], []
            for i in range(blocks):
                n = (i + 1) * BLK
                at = slice(i * BLK, n)
                dq.append(dot_nn(qkv[pl.ds(width + r, 64), 0:n], dscore[0:n, at]))
                dk.append(dot_nt(qkv[pl.ds(r, 64), i * BLK :], dscore[at, i * BLK :]))
                dv.append(dot_nt(grad_mix[pl.ds(r, 64), i * BLK :], probs[at, i * BLK :]))
            dq = jnp.concatenate(dq, axis=1) * 64**-0.5
            dk = jnp.concatenate(dk, axis=1) * LN2
            qkv[pl.ds(r, 64), :] = rotate(dq, cos_s[...], -sin_s[...]).astype(bf16)
            qkv[pl.ds(width + r, 64), :] = rotate(dk, cos_s[...], -sin_s[...]).astype(bf16)
            qkv[pl.ds(2 * width + r, 64), :] = jnp.concatenate(dv, axis=1).astype(bf16)
        return carry

    lax.fori_loop(0, HEADS // group, heads, 0)


def train_kernel(
    pairs,
    lens,
    gain,
    bias,
    qkv_bias,
    out_bias,
    up_bias,
    down_bias,
    block_input,
    out_grad,
    qkv_w_h,
    out_w_h,
    up_in,
    down_in,
    block_output,
    input_grad,
    mlp_out,
    att_out,
    vec_out,
    up_all,
    down_all,
    hid_h,
    qkv_h,
    mix_h,
    lse_h,
    act_h,
    slope_h,
    stream,
    grad_low,
    grad_mix,
    hid,
    qkv,
    mix,
    lse,
    act,
    slope,
    qkv_w,
    out_w,
    up_w,
    down_w,
    up_b,
    hot_s,
    mask_s,
    cos_s,
    sin_s,
    tri,
    krow,
    vrow,
    qext,
    gext,
    probs,
    dscore,
    scores,
    mlp_grad,
    att_grad,
    vec_grad,
    mlp_core,
    att_core,
    mlp_recv,
    att_recv,
    vec_recv,
    in_sem,
    save_sem,
    out_sem,
    send_sem,
    recv_sem,
):
    tokens, width = grad_low.shape
    layers = gain.shape[0]
    half = up_w.shape[2]
    units = 2 * half
    blocks = tokens // BLK
    last = layers - 1
    grad = input_grad
    split = pairs <= 4

    by_mlp, by_row, by_far = (Group(name, list(BITS[name])) for name in "XYa")
    own, other = by_mlp.me, by_mlp.index(1)

    class Loads:
        def __init__(self):
            self.flight, self.used = {}, 0

        def start(self, name, *pairs_):
            copies = []
            for src, dst in pairs_:
                copies.append(pltpu.make_async_copy(src, dst, in_sem.at[self.used]))
                copies[-1].start()
                self.used += 1
            self.flight[name] = copies

        def wait(self, *names):
            for name in names:
                for copy in self.flight.pop(name):
                    copy.wait()

    loads = Loads()

    def fetch(layer, *names):
        for name in names:
            pairs_ = {
                "act": [(act_h.at[layer], act)],
                "slope": [(slope_h.at[layer], slope)],
                UP_OWN: [(up_in.at[layer], up_w.at[own])],
                UP_OTHER: [(up_all.at[layer, other], up_w.at[other])],
                DOWN_OWN: [(down_in.at[layer], down_w.at[own])],
                DOWN_OTHER: [(down_all.at[layer, other], down_w.at[other])],
                "hid": [(hid_h.at[layer], hid.at[0:width, :])],
                "qkv": [(qkv_h.at[layer], qkv)],
                "mix": [(mix_h.at[layer], mix)],
                "lse": [(lse_h.at[layer], lse)],
                "out_w": [(out_w_h.at[layer], out_w)],
                "qkv_w": [(qkv_w_h.at[layer], qkv_w)],
            }[name]
            loads.start(name, *pairs_)

    saves = {}

    def save(name, src, dst):
        copy = pltpu.make_async_copy(src, dst, save_sem.at[len(saves)])
        copy.start()
        saves[name] = copy

    loads.start("input", (block_input, grad_low))
    fetch(0, "qkv_w")

    sems = (send_sem, recv_sem)
    core = Group("C", list(BITS["C"]))
    by_core = core
    here, there = core.me, core.index(1)
    met, used_sems, travel, swaps = {}, [0], {}, {}

    def meet(groups):
        for group in groups:
            for k in group.others():
                met[tuple(b for b, f in zip(group.bits, group.flips(k)) if f)] = (group, k)
        return groups

    def add(name, kind, *rest):
        travel[name] = kind(sems, used_sems[0], *rest)
        used_sems[0] += travel[name].count

    def swap(name, src, dst):
        swaps[name] = Link(src, dst, sems, used_sems[0], core.device(1))
        used_sems[0] += 1

    meet([core, by_mlp, by_row, by_far])
    hh, hw = half // 2, width // 2
    att_rows = 4 * width
    pieces = {
        "out": (0, width, 0, hw),
        "a": (width, 5 * hw, 0, hw),
        "b": (5 * hw, att_rows, 0, hw // 2),
        "c": (5 * hw, att_rows, hw // 2, hw),
    }
    whole = {"c": (0, att_rows, 0, hw)}
    starts = {}
    for layer in reversed(range(layers)):
        tag = "_" + str(layer)

        def stages(name):
            return meet(groups_of(ORDERS[name + tag], pairs))

        for kind, name in enumerate(("up", "down")):
            for x in range(2):
                swap(
                    (name, x, layer),
                    mlp_grad.at[layer, x, pl.ds(pl.multiple_of(kind * half + there * hh, 16), hh), :],
                    mlp_core.at[kind, x],
                )
            subs = 4 if split else 1
            for sub in range(subs):
                count = hh // subs
                add(
                    name + str(sub) + tag,
                    Unit,
                    mlp_grad.at[layer],
                    pl.multiple_of(kind * half + here * hh + sub * count, 16),
                    count,
                    mlp_recv.at[layer, kind, sub],
                    stages(name + str(sub)),
                    core,
                    mlp_out.at[layer],
                    out_sem.at[layer, kind * 4 + sub],
                )
                starts[name + str(sub) + tag] = name + "3" + tag
        for name, (a, b, lo, hi) in pieces.items():
            swap(
                (name, layer),
                att_grad.at[
                    layer, pl.ds(pl.multiple_of(there * att_rows + a, 16), b - a), lo:hi
                ],
                att_core.at[a:b, lo:hi],
            )
        for k, (name, (a, b, lo, hi)) in enumerate((pieces if split else whole).items()):
            add(
                name + tag,
                Unit,
                att_grad.at[layer, :, lo:hi],
                pl.multiple_of(here * att_rows + a, 16),
                b - a,
                att_recv.at[layer, a:b, lo:hi],
                stages(name),
                core,
                att_out.at[layer, :, lo:hi],
                out_sem.at[layer, 8 + k],
            )
            starts[name + tag] = {"out": "out", "a": "head2_1", "b": "head3_1", "c": "att"}[name] + tag
        add(
            "vec" + tag,
            Vector,
            vec_grad.at[layer],
            vec_recv.at[layer],
            [core] + stages("vec"),
        )
        starts["vec" + tag] = "norm%d" % (blocks - 1) + tag

    barrier = pltpu.get_barrier_semaphore()
    for group, k in met.values():
        pl.semaphore_signal(barrier, inc=1, device_id=group.device(k), device_id_type=MESH)

    moves = {}
    for layer in range(layers):
        for k, (src, dst) in enumerate(
            ((up_in, up_all), (up_in, up_all), (down_in, down_all), (down_in, down_all))
        ):
            part = src.shape[1] // 2
            quarter = part // 4
            relay = by_row if k < 2 else by_far
            pair = pl.multiple_of((k % 2) * part + 2 * core.me * quarter, 16)
            first = pl.multiple_of(pair + relay.me * quarter, 16)
            sent = dst.at[layer, own, pl.ds(first, quarter), :]
            got = dst.at[layer, other, pl.ds(first, quarter), :]
            both = dst.at[layer, other, pl.ds(pair, 2 * quarter), :]
            moves[layer, k] = []
            for a, b, group in (
                (src.at[layer, pl.ds(first, quarter), :], sent, by_mlp),
                (got, got, relay),
                (both, both, core),
            ):
                moves[layer, k].append(Link(a, b, sems, used_sems[0], group.device(1)))
                used_sems[0] += 1
    bias_link = Link(up_b.at[own], up_b.at[own], sems, used_sems[0], by_mlp.device(1))

    def begin(layer, k, step):
        moves[layer, k][step].start()

    def end(layer, k, step):
        moves[layer, k][step].wait()

    def on(layer, k, step):
        end(layer, k, step)
        begin(layer, k, step + 1)

    points = []
    for layer in reversed(range(layers)):
        tag = "_" + str(layer)
        points += [("down%d" % c + tag, 1.32 if c == 2 else 0.825) for c in range(4)]
        if layer < last:
            points += [("out" + tag, 0.55)]
        points += [
            ("mlp%d" % i + tag, 3.1 if i == 0 and layer == last else 1.1) for i in range(blocks)
        ]
        points += [("up0" + tag, 0.825), ("up1" + tag, 0.825)]
        if layer < last:
            points += [("mix" + tag, 0.99)]
        points += [("up2" + tag, 0.825), ("up3" + tag, 0.825)]
        if layer == last:
            points += [("fwd0" + tag, 0.3), ("fwd1" + tag, 3.6), ("mix" + tag, 4.9)]
            points += [("out" + tag, 0.5)]
        for i in range(HEADS // 2):
            extra = {2: 0.6, 3: 0.5}.get(i, 0.0)
            points += [("head%d_0" % i + tag, 2.035 + extra if i else 0.33)]
            points += [("head%d_1" % i + tag, 1.925 + extra)]
        points += [("att" + tag, 3.3)]
        points += [("norm%d" % i + tag, 1.375) for i in range(blocks)]
    points += [("last%d" % i, 1.0) for i in range(blocks)]
    actions = plan(points, starts, travel)

    def run(name):
        for unit, at in actions[name]:
            travel[unit].advance(at)

    def run_at(step, count, name):
        for i in range(count):
            if actions[name % i]:

                @pl.when(step == i)
                def _():
                    run(name % i)

    hot, position = doc_tables(lens, tokens)
    zeros8 = jnp.zeros_like(hot)
    hot_s[...] = jnp.concatenate([hot, zeros8], axis=0).astype(bf16)
    mask_s[...] = jnp.concatenate([mask_rows(hot), zeros8], axis=0).astype(bf16)
    cos_s[...], sin_s[...] = rotary_tables(position)
    tri[...] = causal_bias()
    hid[width : width + 16, :] = jnp.ones((16, tokens), bf16)
    up_b[own, 0:layers, :] = up_bias[...].astype(f32)
    loads.wait("input")
    stream[...] = grad_low[...].astype(f32)
    pl.semaphore_wait(barrier, len(met))
    begin(0, 0, 0)
    bias_link.start()
    begin(0, 1, 0)

    def norm(layer):
        gain_row, bias_row = row_of(gain, layer), row_of(bias, layer)

        def block(i, carry):
            rows = pl.ds(pl.multiple_of(i * BLK, BLK), BLK)
            centred, scale = norm_stats(stream[rows, :])
            hid[0:width, rows] = (centred * scale * gain_row + bias_row).astype(bf16).T
            return carry

        lax.fori_loop(0, blocks, block, 0)

    def project(layer):
        bias_row = row_of(qkv_bias, layer)
        for part in range(3):
            cols = slice(part * width, (part + 1) * width)
            column = jnp.broadcast_to(bias_row[:, cols], (128, width)).T
            column = jnp.concatenate([column] * (BLK // 128), axis=1)
            for i in range(blocks):
                at = slice(i * BLK, (i + 1) * BLK)
                value = dot_tn(qkv_w[:, cols], hid[0:width, at]) + column
                if part < 2:
                    value = rotate(value, cos_s[:, at], sin_s[:, at])
                if part == 0:
                    value = value * (64**-0.5 * LOG2E)
                qkv[cols, at] = value.astype(bf16)

    def attend(hook):
        attention_forward(
            qkv,
            mix,
            lse,
            hot_s,
            mask_s,
            tri,
            (krow.at[0], krow.at[1], vrow.at[0], vrow.at[1]),
            scores,
            (probs, dscore),
            4,
            hook,
        )

    def mlp_up(layer, x, rows):
        row = up_b[x, layer : layer + 1, :]
        for c in range(half // 512):
            cs = slice(c * 512, (c + 1) * 512)
            u = dot_tn(hid[0:width, rows], up_w[x, :, cs]) + row[:, cs]
            cdf = 0.5 + 0.5 * lax.erf(u * (2.0**-0.5))
            pdf = jnp.exp2(u * u * (-0.5 * LOG2E)) * ((2.0 * math.pi) ** -0.5)
            act[x, rows, cs] = (u * cdf).astype(bf16)
            slope[x, rows, cs] = (cdf + u * pdf).astype(bf16)

    def block_rows(i):
        return pl.ds(pl.multiple_of(i * BLK, BLK), BLK)

    def at_block(i, at, *steps):
        @pl.when(i == at)
        def _():
            for step in steps:
                on(*step)

    for layer in range(last):
        norm(layer)
        loads.wait("qkv_w")
        loads.start("grad", (out_grad, grad_low))
        fetch(layer, UP_OWN, DOWN_OWN, "out_w")
        project(layer)
        fetch(layer + 1, "qkv_w")

        def hook(step):
            @pl.when(step == 0)
            def _():
                begin(layer, 2, 0)

            @pl.when(step == 1)
            def _():
                on(layer, 0, 0)
                begin(layer, 3, 0)

        attend(hook)
        on(layer, 1, 0)
        save("hid", hid.at[0:width, :], hid_h.at[layer])
        save("qkv", qkv, qkv_h.at[layer])
        save("mix", mix, mix_h.at[layer])
        save("lse", lse, lse_h.at[layer])
        loads.wait(UP_OWN, DOWN_OWN, "out_w")
        shift = row_of(out_bias, layer) + row_of(down_bias, layer)
        bias_link.wait()

        def own_block(i, carry):
            rows = block_rows(i)
            mlp_up(layer, own, rows)
            total = dot_tn(mix[:, rows], out_w[...]) + dot_nn(act[own, rows, :], down_w[own])
            stream[rows, :] = stream[rows, :] + (total + shift)
            at_block(i, 1, (layer, 2, 0))

            @pl.when(i == 1)
            def _():
                begin(layer + 1, 0, 0)
                begin(layer + 1, 1, 0)

            at_block(i, 2, (layer, 0, 1))
            at_block(i, 3, (layer, 3, 0))
            return carry

        def other_up(i, carry):
            mlp_up(layer, other, block_rows(i))
            at_block(i, 1, (layer, 2, 1))
            at_block(i, 3, (layer + 1, 0, 0))
            return carry

        def other_down(i, carry):
            rows = block_rows(i)
            stream[rows, :] = stream[rows, :] + dot_nn(act[other, rows, :], down_w[other])
            at_block(i, 1, (layer + 1, 1, 0))
            return carry

        lax.fori_loop(0, blocks, own_block, 0)
        save("act0", act.at[own], act_h.at[layer, own])
        save("slope0", slope.at[own], slope_h.at[layer, own])
        fetch(layer + 1, "out_w")
        on(layer, 1, 1)
        end(layer, 0, 2)
        end(layer, 1, 2)
        fetch(layer, UP_OTHER)
        loads.wait(UP_OTHER)
        lax.fori_loop(0, blocks, other_up, 0)
        save("act1", act.at[other], act_h.at[layer, other])
        save("slope1", slope.at[other], slope_h.at[layer, other])
        fetch(layer + 1, UP_OWN)
        on(layer, 3, 1)
        begin(layer + 1, 2, 0)
        begin(layer + 1, 3, 0)
        end(layer, 2, 2)
        end(layer, 3, 2)
        fetch(layer, DOWN_OTHER)
        loads.wait(DOWN_OTHER)
        lax.fori_loop(0, blocks, other_down, 0)
        fetch(layer + 1, DOWN_OWN)

    saves["hid"].wait()
    norm(last)
    loads.wait(UP_OWN, "grad")
    grad[...] = grad_low[...].astype(f32)
    for name in ("act0", "slope0", "act1", "slope1"):
        saves[name].wait()

    def last_own(i, carry):
        mlp_up(last, own, block_rows(i))
        at_block(i, 2, (last, 0, 1))
        return carry

    def last_other(i, carry):
        mlp_up(last, other, block_rows(i))
        at_block(i, 1, (last, 2, 1))
        return carry

    lax.fori_loop(0, blocks, last_own, 0)
    on(last, 1, 1)
    on(last, 2, 0)
    loads.wait("qkv_w")
    saves["qkv"].wait()
    project(last)
    on(last, 3, 0)
    end(last, 0, 2)
    end(last, 1, 2)
    fetch(last, UP_OTHER)
    loads.wait(UP_OTHER)
    lax.fori_loop(0, blocks, last_other, 0)
    save("act_last", act, act_h.at[last])

    for layer in reversed(range(layers)):

        def ahead(*names):
            for name in names:
                if layer:
                    fetch(layer - 1, name)
                elif name in ("act", DOWN_OWN, DOWN_OTHER, "out_w", "mix"):
                    fetch(last, name)

        tag = "_" + str(layer)

        def join(value, own, name, target, rows, received):
            if own:
                swaps[name].wait()
                target[rows, :] = (value + received[...].astype(f32)).astype(bf16)
            else:
                target[rows, :] = value.astype(bf16)
                swaps[name].start()

        def down_grads(own, x):
            at = pl.multiple_of((here if own else there) * hh, 256)
            join(
                dot_tn(act[x, :, pl.ds(at, hh)], grad_low[...]),
                own,
                ("down", x, layer),
                mlp_grad.at[layer, x],
                pl.ds(pl.multiple_of(half + at, 256), hh),
                mlp_core.at[1, x],
            )

        def out_grads(own):
            side = here if own else there
            value = dot_nn(mix[pl.ds(pl.multiple_of(side * hw, 256), hw), :], grad_low[...])
            join(
                jnp.concatenate([value[:, :hw], value[:, hw:]], axis=0),
                own,
                ("out", layer),
                att_grad.at[layer],
                pl.ds(pl.multiple_of(side * att_rows, 256), width),
                att_core.at[0:width],
            )

        def up_grads(own, x):
            side = here if own else there
            at = pl.multiple_of(side * hh, 256)
            up = dot_nn(hid[...], slope[x, :, pl.ds(at, hh)])
            vec_grad[layer, 0, pl.ds(6 + 2 * x + side, 1), :] = up[width : width + 1]
            join(
                up[:width],
                own,
                ("up", x, layer),
                mlp_grad.at[layer, x],
                pl.ds(at, hh),
                mlp_core.at[0, x],
            )

        if layer < last:
            loads.wait("act")
        down_grads(False, 0)
        run("down0" + tag)
        down_grads(False, 1)
        run("down1" + tag)
        if layer == last:
            on(last, 3, 1)
        if layer < last:
            loads.wait("mix")
            out_grads(False)
        down_grads(True, 0)
        run("down2" + tag)
        down_grads(True, 1)
        run("down3" + tag)
        if layer < last:
            ahead("act")
            out_grads(True)
            run("out" + tag)
            loads.wait("slope", DOWN_OWN, DOWN_OTHER)
        else:
            saves["act_last"].wait()
            ahead("act")
            end(last, 2, 2)
            end(last, 3, 2)
            fetch(last, DOWN_OTHER)
            loads.wait(DOWN_OWN, DOWN_OTHER)

        def mlp_block(i, carry):
            rows = pl.ds(pl.multiple_of(i * BLK, BLK), BLK)
            for c in range(units // 512):
                x, at = divmod(c * 512, half)
                cs = slice(at, at + 512)
                da = dot_nt(grad_low[rows, :], down_w[x, cs, :])
                slope[x, rows, cs] = (slope[x, rows, cs].astype(f32) * da).astype(bf16)
            run_at(i, blocks, "mlp%d" + tag)
            return carry

        lax.fori_loop(0, blocks, mlp_block, 0)
        ahead(DOWN_OWN, DOWN_OTHER)
        if layer < last:
            loads.wait("hid")
        up_grads(False, 0)
        run("up0" + tag)
        up_grads(False, 1)
        run("up1" + tag)
        vec_grad[layer, 0, 5:6, :] = jnp.sum(grad_low[...].astype(f32), axis=0, keepdims=True)
        if layer < last:
            loads.wait("out_w")
            grad_mix[...] = dot_nt(out_w[...], grad_low[...]).astype(bf16)
            run("mix" + tag)
            ahead("out_w")
        if layer == 0:
            loads.start("input", (block_input, grad_low))
        up_grads(True, 0)
        run("up2" + tag)
        up_grads(True, 1)
        run("up3" + tag)
        if layer == last:
            saves["mix"].wait()
            saves["lse"].wait()
            attend(lambda step: run_at(step, 2, "fwd%d" + tag))
            save("mix_last", mix, mix_h.at[last])
            out_grads(False)
            loads.wait("out_w")
            grad_mix[...] = dot_nt(out_w[...], grad_low[...]).astype(bf16)
            run("mix" + tag)
            ahead("out_w")
            out_grads(True)
            run("out" + tag)
        else:
            loads.wait("qkv", "lse")

        heads_of = {"a": (0, hw), "b": (hw, 3 * hw // 2), "c": (3 * hw // 2, width)}

        def qkv_part(name, part):
            first, last = heads_of[name]
            return qkv[part * width + first : part * width + last, :]

        def qkv_grads(name, own):
            a, b, first, last = pieces[name]
            side = here if own else there
            left = hid[pl.ds(pl.multiple_of(side * hw, 256), hw), :]
            join(
                jnp.concatenate([dot_nt(left, qkv_part(name, part)) for part in range(3)], axis=0),
                own,
                (name, layer),
                att_grad.at[layer, :, first:last],
                pl.ds(pl.multiple_of(side * att_rows + a, 256), b - a),
                att_core.at[a:b, first:last],
            )

        def qkv_sums(name):
            first, last = heads_of[name]
            for part in range(3):
                total = dot_nt(hid[width : width + 16, :], qkv_part(name, part))
                vec_grad[layer, 0, 2 + part : 3 + part, first:last] = total[:1]

        def head_hook(step, j):
            for at, name in ((2, "a"), (3, "b")):

                @pl.when(step == at)
                def _():
                    qkv_grads(name, j > 0)

            run_at(step, HEADS // 2, "head%d_" + str(j) + tag)

        attention_backward(
            qkv,
            mix,
            grad_mix,
            lse,
            hot_s,
            mask_s,
            tri,
            cos_s,
            sin_s,
            (krow, vrow, qext, gext, probs, dscore),
            2,
            head_hook,
        )
        qkv_grads("c", False)
        for name in heads_of:
            qkv_sums(name)
        qkv_grads("c", True)
        run("att" + tag)
        if layer == last:
            saves["mix_last"].wait()
        ahead("hid", "mix", "lse")
        if layer < last:
            loads.wait(UP_OWN, UP_OTHER, "qkv_w")
        if layer == 0:
            loads.wait("input")
        gain_row = row_of(gain, layer)
        vec_grad[layer, 0, 0:2, :] = jnp.zeros((2, width), f32)
        vec_grad[layer, 0, 10:16, :] = jnp.zeros((6, width), f32)

        def norm_block(i, carry):
            rows = pl.ds(pl.multiple_of(i * BLK, BLK), BLK)
            back = lax.dot_general(
                qkv[:, rows], qkv_w[...], (((0,), (1,)), ((), ())), preferred_element_type=f32
            )
            dh = back + (dot_nt(slope[0, rows, :], up_w[0]) + dot_nt(slope[1, rows, :], up_w[1]))
            if layer:
                centred, scale = norm_stats(stream[rows, :])
            else:
                centred, scale = norm_stats(grad_low[rows, :].astype(f32))
            n = centred * scale
            product = dh * n
            vec_grad[layer, 0, 0:1, :] += jnp.sum(product, axis=0, keepdims=True)
            vec_grad[layer, 0, 1:2, :] += jnp.sum(dh, axis=0, keepdims=True)
            e = dh * gain_row
            mean_e = jnp.mean(e, axis=-1, keepdims=True)
            mean_en = jnp.mean(product * gain_row, axis=-1, keepdims=True)
            total = grad[rows, :] + scale * (e - mean_e - n * mean_en)
            grad[rows, :] = total
            if layer:
                grad_low[rows, :] = total.astype(bf16)
            run_at(i, blocks, "norm%d" + tag)
            return carry

        lax.fori_loop(0, blocks, norm_block, 0)
        ahead("slope", UP_OWN, UP_OTHER, "qkv", "qkv_w")
    loads.wait("act", DOWN_OWN, DOWN_OTHER, "out_w", "mix")
    shift = row_of(out_bias, last) + row_of(down_bias, last)

    def last_block(i, carry):
        rows = pl.ds(pl.multiple_of(i * BLK, BLK), BLK)
        total = dot_tn(mix[:, rows], out_w[...])
        for x in range(2):
            total = total + dot_nn(act[x, rows, :], down_w[x])
        grad_low[rows, :] = (stream[rows, :] + (total + shift)).astype(bf16)
        run_at(i, blocks - 1, "last%d")
        return carry

    lax.fori_loop(0, blocks, last_block, 0)
    loads.start("result", (grad_low, block_output))
    run("last%d" % (blocks - 1))
    loads.wait("result")
    mine = lax.axis_index("mlp")
    for layer in range(layers):
        done = len(travel["vec_" + str(layer)].steps)
        total = vec_grad[layer, done]
        vec_out[layer] = total
        vec_out[layer, 6:8, :] = jnp.where(mine == 0, total[6:8], total[8:10])


VMEM = pl.BlockSpec(memory_space=pltpu.VMEM)
SMEM = pl.BlockSpec(memory_space=pltpu.SMEM)
ANY = pl.BlockSpec(memory_space=pl.ANY)


def run_layers(
    lens,
    gain,
    bias,
    qkv_b,
    out_b,
    up_b,
    down_b,
    block_input,
    out_grad,
    qkv_w,
    out_w,
    up_w,
    down_w,
):
    tokens, width = block_input.shape
    layers = gain.shape[0]
    half = up_w.shape[2]
    units = 2 * half
    shape = jax.ShapeDtypeStruct
    v = pltpu.VMEM
    pairs = lax.axis_size("dp").bit_length() - 1
    subs = 4 if pairs <= 4 else 1
    blocks = tokens // BLK
    outs = pl.pallas_call(
        functools.partial(train_kernel, pairs),
        out_shape=(
            shape((tokens, width), bf16),
            shape((tokens, width), f32),
            shape((layers, units, width), bf16),
            shape((layers, 8 * width, width // 2), bf16),
            shape((layers, 16, width), f32),
            shape((layers, 2, width, half), bf16),
            shape((layers, 2, half, width), bf16),
            shape((layers, width, tokens), bf16),
            shape((layers, 3 * width, tokens), bf16),
            shape((layers, width, tokens), bf16),
            shape((layers, HEADS, tokens), f32),
            shape((layers, 2, tokens, half), bf16),
            shape((layers, 2, tokens, half), bf16),
        ),
        in_specs=[SMEM] + [VMEM] * 6 + [ANY] * 6,
        out_specs=(ANY, VMEM, ANY, ANY, VMEM) + (ANY,) * 8,
        scratch_shapes=[
            v((tokens, width), f32),
            v((tokens, width), bf16),
            v((width, tokens), bf16),
            v((width + 16, tokens), bf16),
            v((3 * width, tokens), bf16),
            v((width, tokens), bf16),
            v((HEADS, tokens), f32),
            v((2, tokens, half), bf16),
            v((2, tokens, half), bf16),
            v((width, 3 * width), bf16),
            v((width, width), bf16),
            v((2, width, half), bf16),
            v((2, half, width), bf16),
            v((2, 8, half), f32),
            v((16, tokens), bf16),
            v((16, tokens), bf16),
            v((HALF, tokens), f32),
            v((HALF, tokens), f32),
            v((BLK, BLK), f32),
            v((2, tokens, 128), bf16),
            v((2, tokens, 128), bf16),
            v((2, 128, tokens), bf16),
            v((2, 128, tokens), bf16),
            v((tokens, tokens), bf16),
            v((tokens, tokens), bf16),
            v((blocks * (blocks + 1) // 2 * BLK, BLK), f32),
            v((layers, 2, units, width), bf16),
            v((layers, 8 * width, width // 2), bf16),
            v((layers, 7, 16, width), f32),
            v((2, 2, half // 2, width), bf16),
            v((4 * width, width // 2), bf16),
            v((layers, 2, subs, half // subs, width), bf16),
            v((layers, 4 * width, width // 2), bf16),
            v((layers, 10 if pairs <= 4 else 16, 16, width), f32),
            pltpu.SemaphoreType.DMA((48,)),
            pltpu.SemaphoreType.DMA((16,)),
            pltpu.SemaphoreType.DMA((layers, 12)),
            pltpu.SemaphoreType.DMA((360,)),
            pltpu.SemaphoreType.DMA((360,)),
        ],
        compiler_params=pltpu.CompilerParams(
            vmem_limit_bytes=63 * 2**20, collective_id=0, has_side_effects=True
        ),
        name="layers",
    )(
        lens,
        gain,
        bias,
        qkv_b,
        out_b,
        up_b,
        down_b,
        block_input,
        out_grad,
        qkv_w,
        out_w,
        up_w,
        down_w,
    )
    return outs[:5]


def body(
    block_input,
    doc_lengths,
    norm_gain,
    norm_bias,
    qkv_weight,
    qkv_bias,
    out_weight,
    out_bias,
    up_weight,
    up_bias,
    down_weight,
    down_bias,
    out_grad,
):
    return finish(
        *run_layers(
            doc_lengths,
            norm_gain,
            norm_bias,
            qkv_bias,
            out_bias,
            up_bias,
            down_bias,
            block_input,
            out_grad,
            qkv_weight,
            out_weight,
            up_weight,
            down_weight,
        )
    )


def finish_kernel(
    vec,
    block_output,
    input_grad,
    mlp_low,
    att_low,
    block_out,
    input_out,
    gain_out,
    bias_out,
    qkv_out,
    qkv_b_out,
    out_w_out,
    out_b_out,
    up_out,
    up_b_out,
    down_out,
    down_b_out,
    mlp_s,
    att_s,
    qkv_s,
    out_w_s,
    up_s,
    down_s,
    block_s,
    input_s,
    in_sem,
    out_sem,
    pass_sem,
):
    layers, units, width = mlp_low.shape
    half, hw = units // 2, width // 2
    rows = 4 * width
    count = [0]

    def store(src, dst):
        copy = pltpu.make_async_copy(src, dst, out_sem.at[count[0]])
        count[0] += 1
        copy.start()
        return copy

    loads = []
    for layer in range(layers):
        for k, (src, dst) in enumerate(((mlp_low, mlp_s), (att_low, att_s))):
            for part in range(2):
                size = src.shape[1] // 2
                at = pl.ds(part * size, size)
                copy = pltpu.make_async_copy(
                    src.at[layer, at, :], dst.at[layer, at, :], in_sem.at[layer, k, part]
                )
                copy.start()
                loads.append(copy)
    passed = []
    for k, (src, dst) in enumerate(((block_output, block_s), (input_grad, input_s))):
        copy = pltpu.make_async_copy(src, dst, pass_sem.at[k])
        copy.start()
        passed.append(copy)
    stores = []
    for layer in range(layers):
        one = slice(layer, layer + 1)
        gain_out[one, :] = vec[layer, 0:1, :]
        bias_out[one, :] = vec[layer, 1:2, :]
        for part in range(3):
            qkv_b_out[one, part * width : (part + 1) * width] = vec[layer, 2 + part : 3 + part, :]
        out_b_out[one, :] = vec[layer, 5:6, :]
        down_b_out[one, :] = vec[layer, 5:6, :]
        for part in range(half // width):
            up_b_out[one, part * width : (part + 1) * width] = vec[layer, 6 + part : 7 + part, :]
    for layer in range(layers):
        up_load, down_load, first_load, second_load = loads[4 * layer : 4 * layer + 4]
        up_load.wait()
        for c in range(half // width):
            at = slice(c * width, (c + 1) * width)
            up_s[layer, :, at] = mlp_s[layer, at, :].astype(f32)
        stores.append(store(up_s.at[layer], up_out.at[layer]))
        down_load.wait()
        down_s[layer] = mlp_s[layer, half:units, :].astype(f32)
        stores.append(store(down_s.at[layer], down_out.at[layer]))
        for side, load in enumerate((first_load, second_load)):
            load.wait()
            to = slice(side * hw, (side + 1) * hw)
            base = side * rows
            for c in range(2):
                out_w_s[layer, to, c * hw : (c + 1) * hw] = att_s[
                    layer, base + c * hw : base + (c + 1) * hw, :
                ].astype(f32)
                for part in range(3):
                    first = base + width + (c * 3 + part) * hw
                    qkv_s[layer, to, part * width + c * hw : part * width + (c + 1) * hw] = att_s[
                        layer, first : first + hw, :
                    ].astype(f32)
            stores.append(store(out_w_s.at[layer, to, :], out_w_out.at[layer, to, :]))
            stores.append(store(qkv_s.at[layer, to, :], qkv_out.at[layer, to, :]))
    for copy, src, dst in zip(passed, (block_s, input_s), (block_out, input_out)):
        copy.wait()
        stores.append(store(src, dst))
    for copy in stores:
        copy.wait()


def finish(block_output, input_grad, mlp_low, att_low, vec):
    layers, units, width = mlp_low.shape
    half = units // 2
    shape = jax.ShapeDtypeStruct
    v = pltpu.VMEM
    row = shape((layers, width), f32)
    big = {
        "qkv": (layers, width, 3 * width),
        "out": (layers, width, width),
        "up": (layers, width, half),
        "down": (layers, half, width),
    }
    return pl.pallas_call(
        finish_kernel,
        out_shape=(
            shape(block_output.shape, bf16),
            shape(input_grad.shape, f32),
            row,
            row,
            shape(big["qkv"], f32),
            shape((layers, 3 * width), f32),
            shape(big["out"], f32),
            row,
            shape(big["up"], f32),
            shape((layers, half), f32),
            shape(big["down"], f32),
            row,
        ),
        in_specs=[VMEM] + [ANY] * 4,
        out_specs=(ANY, ANY, VMEM, VMEM, ANY, VMEM, ANY, VMEM, ANY, VMEM, ANY, VMEM),
        scratch_shapes=[v(mlp_low.shape, bf16), v(att_low.shape, bf16)]
        + [v(dims, f32) for dims in big.values()]
        + [v(block_output.shape, bf16), v(input_grad.shape, f32)]
        + [
            pltpu.SemaphoreType.DMA((layers, 2, 2)),
            pltpu.SemaphoreType.DMA((2 + 6 * layers,)),
            pltpu.SemaphoreType.DMA((2,)),
        ],
        compiler_params=pltpu.CompilerParams(vmem_limit_bytes=63 * 2**20),
        name="finish",
    )(vec, block_output, input_grad, mlp_low, att_low)


def solution(mesh):
    rows = P(("dp", "mlp"), None)
    return jax.shard_map(
        body,
        mesh=mesh,
        in_specs=(
            rows,
            rows,
            P(),
            P(),
            P(),
            P(),
            P(),
            P(),
            P(None, None, "mlp"),
            P(None, "mlp"),
            P(None, "mlp", None),
            P(),
            rows,
        ),
        out_specs=(
            rows,
            rows,
            P(),
            P(),
            P(),
            P(),
            P(),
            P(),
            P(None, None, "mlp"),
            P(None, "mlp"),
            P(None, "mlp", None),
            P(),
        ),
        check_vma=False,
    )
```
